32 devices in a mesh: dp: 16 (over z, x, core), tensor: 2 (over y).
Axes of the slice: x: 2, y: 2, z: 4, core: 2. Of those that a mesh axis runs over, the one named last changes fastest.
Arguments:
- inputs: bfloat16 [32768, 512], P('dp'), may hold values from -6 to 6
- memory: bfloat16 [32768, 512], P('dp'), may hold values from -6 to 6
- tgt_seg: int32 [32, 1024], P('dp'), may hold values from 0 to 31, as said below
- src_seg: int32 [32, 1024], P('dp'), may hold values from 0 to 31, as said below
- self_query: bfloat16 [512, 512], P(None, 'tensor'), may hold values from -0.25 to 0.25
- self_key: bfloat16 [512, 512], P(None, 'tensor'), may hold values from -0.25 to 0.25
- self_value: bfloat16 [512, 512], P(None, 'tensor'), may hold values from -0.25 to 0.25
- self_out: bfloat16 [512, 512], P('tensor'), may hold values from -1 to 1
- cross_query: bfloat16 [512, 512], P(None, 'tensor'), may hold values from -0.25 to 0.25
- cross_key: bfloat16 [512, 512], P(None, 'tensor'), may hold values from -0.25 to 0.25
- cross_value: bfloat16 [512, 512], P(None, 'tensor'), may hold values from -0.25 to 0.25
- cross_out: bfloat16 [512, 512], P('tensor'), may hold values from -1 to 1
- ffn_in: bfloat16 [512, 2048], P(None, 'tensor'), may hold values from -0.25 to 0.25
- ffn_out: bfloat16 [2048, 512], P('tensor'), may hold values from -0.125 to 0.125
- norm_gain: float32 [3, 512], replicated, may hold values from 0.25 to 1.75
- norm_shift: float32 [3, 512], replicated, may hold values from -3 to 3
- residual_scale: float32 [3, 512], replicated, may hold values from 0.8 to 2
- cotangent: bfloat16 [32768, 512], P('dp')
Outputs:
- output: bfloat16 [32768, 512], P('dp')
- input_grad: float32 [32768, 512], P('dp', 'tensor')
- memory_grad: float32 [32768, 512], P('dp', 'tensor')
- self_query_grad: float32 [512, 512], P('dp', 'tensor')
- self_key_grad: float32 [512, 512], P('dp', 'tensor')
- self_value_grad: float32 [512, 512], P('dp', 'tensor')
- self_out_grad: float32 [512, 512], P('tensor', 'dp')
- cross_query_grad: float32 [512, 512], P('dp', 'tensor')
- cross_key_grad: float32 [512, 512], P('dp', 'tensor')
- cross_value_grad: float32 [512, 512], P('dp', 'tensor')
- cross_out_grad: float32 [512, 512], P('tensor', 'dp')
- ffn_in_grad: float32 [512, 2048], P('dp', 'tensor')
- ffn_out_grad: float32 [2048, 512], P('tensor', 'dp')
- norm_gain_grad: float32 [3, 512], P(None, 'dp')
- norm_shift_grad: float32 [3, 512], P(None, 'dp')
- residual_scale_grad: float32 [3, 512], P(None, 'dp')
The draws below stay inside these ranges and needn't reach their ends.
Inputs may be any that keep to these rules, and one draw needn't show every extreme that they name: `tgt_seg`: along each row the ids never fall, and every id from 0 to 31 holds one or more positions of every row; target id s of row r is the same sentence pair as memory id s of row r. `src_seg`: along each row the ids never fall, and every id from 0 to 31 holds one or more positions of every row.
All inputs are finite; a program needn't handle non-finite values.
Results may differ from the reference program's by a relative error of at most 0.025.
Values may be sent and summed in bfloat16 or wider, within the bound.
No kernel may reach another device: no remote copies, remote signals or barrier semaphores. Data moves between devices by JAX's collectives and lax.ppermute only.
A program may use at most 192 MiB of HBM per device.

```python
import math
import jax
import jax.numpy as jnp
from jax import lax

D = 512
HEADS = 8
HEAD_DIM = 64
FF = 2048
LEN = 1024
MEM_LEN = 1024
SEGS = 32
ROWS = 32
TOKENS = 32768
MEM_TOKENS = 32768
N_TENSOR = 2


def draw_cuts(key, count, length):

    def single_row(subkey):
        cuts = jax.random.permutation(subkey, length - 1)[:count - 1] + 1
        places = jnp.arange(length, dtype=jnp.int32)
        return jnp.sum((places[:, None] >= cuts[None, :]).astype(jnp.int32), axis=1).astype(jnp.int32)
    return jax.vmap(single_row)(jax.random.split(key, ROWS))


def draw_tgt_seg(key, part):
    return draw_cuts(jax.random.fold_in(key, 11), SEGS, LEN)


def draw_src_seg(key, part):
    return draw_cuts(jax.random.fold_in(key, 23), SEGS, MEM_LEN)


def draw_cotangent(key, part):
    places = jnp.arange(TOKENS, dtype=jnp.float32) / float(max(TOKENS - 1, 1))
    ramp = jnp.exp(places * math.log(3.0))[:, None]
    return (jax.random.normal(jax.random.fold_in(key, 3), (TOKENS, D), jnp.float32) * ramp).astype(jnp.bfloat16)


def block_levels(rng, extent, cuts, smallest, top_value):
    def one(dim, blocks):
        draws = jax.random.uniform(jax.random.fold_in(jax.random.fold_in(rng, 6), dim), (blocks,), jnp.float32, smallest / len(cuts), top_value / len(cuts))
        return jnp.repeat(jnp.exp(draws), extent[dim] // blocks).reshape((-1,) + (1,) * (len(extent) - dim - 1))

    factor_of = one(*cuts[0])
    for cut in cuts[1:]:
        factor_of = factor_of * one(*cut)
    return factor_of


def bell_draw(key, extent, spread, most, shards=(), kind=jnp.bfloat16):
    values = spread * jax.random.normal(key, extent, jnp.float32)
    if shards:
        values = values * block_levels(key, extent, shards, -0.22, 0.18)
    return jnp.clip(values, -most, most).astype(kind)


def setup_inputs(seed: int = 0) -> dict:
    key_of = jax.random.split(jax.random.key(seed), 19)
    inputs = bell_draw(key_of[0], (TOKENS, D), 1.0, 6.0, ((0, 16),))
    memory = bell_draw(key_of[1], (MEM_TOKENS, D), 1.0, 6.0, ((0, 16),))
    tgt_seg = draw_tgt_seg(jax.random.fold_in(key_of[18], 71), 0)
    src_seg = draw_src_seg(jax.random.fold_in(key_of[18], 71), 0)
    self_query = bell_draw(key_of[4], (D, D), D ** -0.5, 0.25, ((1, 2),))
    self_key = bell_draw(key_of[5], (D, D), D ** -0.5, 0.25, ((1, 2),))
    self_value = bell_draw(key_of[6], (D, D), D ** -0.5, 0.25, ((1, 2),))
    self_out = bell_draw(key_of[7], (D, D), (D // 16) ** -0.5, 1.0, ((0, 2),))
    cross_query = bell_draw(key_of[8], (D, D), D ** -0.5, 0.25, ((1, 2),))
    cross_key = bell_draw(key_of[9], (D, D), D ** -0.5, 0.25, ((1, 2),))
    cross_value = bell_draw(key_of[10], (D, D), D ** -0.5, 0.25, ((1, 2),))
    cross_out = bell_draw(key_of[11], (D, D), (D // 16) ** -0.5, 1.0, ((0, 2),))
    ffn_in = bell_draw(key_of[12], (D, FF), D ** -0.5, 0.25, ((1, 2),))
    ffn_out = bell_draw(key_of[13], (FF, D), FF ** -0.5, 0.125, ((0, 2),))
    norm_gain = jnp.clip(1.0 + 0.15 * jax.random.normal(key_of[14], (3, D), jnp.float32), 0.25, 1.75)
    norm_shift = bell_draw(key_of[15], (3, D), 0.3, 3.0, (), jnp.float32)
    residual_scale = jnp.clip(jax.random.uniform(key_of[16], (3, D), jnp.float32, 0.8, 2.0), 0.8, 2.0)
    cotangent = draw_cotangent(jax.random.fold_in(key_of[18], 71), 0)
    return dict(inputs=inputs, memory=memory, tgt_seg=tgt_seg, src_seg=src_seg, self_query=self_query, self_key=self_key, self_value=self_value, self_out=self_out, cross_query=cross_query, cross_key=cross_key, cross_value=cross_value, cross_out=cross_out, ffn_in=ffn_in, ffn_out=ffn_out, norm_gain=norm_gain, norm_shift=norm_shift, residual_scale=residual_scale, cotangent=cotangent)


@jax.custom_vjp
def low(v):
    return lax.optimization_barrier(v.astype(jnp.bfloat16)).astype(jnp.float32)

@jax.custom_vjp
def low_back(v):
    return v

def low_keep(v):
    return (low(v), None)

def low_pass(kept, grad):
    return (grad,)

def back_keep(v):
    return (v, None)

def back_low(kept, grad):
    return (low(grad),)
low.defvjp(low_keep, low_pass)
low_back.defvjp(back_keep, back_low)

def matmul(left, right):
    return jnp.dot(left, right, precision=lax.Precision.HIGHEST, preferred_element_type=jnp.float32)

def rounded(value):
    return low_back(low(value))

def layer_norm(stream, gain, shift):
    center = lax.optimization_barrier(jnp.mean(stream, axis=-1, keepdims=True))
    centered = stream - center
    variance = lax.optimization_barrier(jnp.mean(centered * centered, axis=-1, keepdims=True))
    return centered * lax.rsqrt(variance + 1e-05) * gain + shift

def gelu_tanh(value):
    return 0.5 * value * (1.0 + jnp.tanh(0.7978845608028654 * (value + 0.044715 * value * value * value)))

def attend_row(query, keys, values, allowed):
    scores = jnp.einsum('qhd,khd->hqk', query, keys, precision=lax.Precision.HIGHEST) * float(HEAD_DIM) ** (-0.5)
    scores = low_back(scores)
    scores = jnp.where(allowed[None], scores, -1e+30)
    peak = lax.optimization_barrier(jnp.max(scores, axis=-1, keepdims=True))
    weights = jnp.exp(scores - peak)
    probs = weights / lax.optimization_barrier(jnp.sum(weights, axis=-1, keepdims=True))
    return jnp.einsum('hqk,khd->qhd', low(probs), values, precision=lax.Precision.HIGHEST)

def attention(query, keys, values, query_seg, key_seg, causal):
    rows, length = query_seg.shape
    key_length = key_seg.shape[1]
    later = jnp.arange(key_length)[None, :] <= jnp.arange(length)[:, None]

    def one_row(pack):
        row_query, row_keys, row_values, row_qseg, row_kseg = pack
        allowed = row_qseg[:, None] == row_kseg[None, :]
        if causal:
            allowed = allowed & later
        return attend_row(row_query, row_keys, row_values, allowed)
    mixed = lax.map(jax.checkpoint(one_row), (query.reshape(rows, length, HEADS, HEAD_DIM), keys.reshape(rows, key_length, HEADS, HEAD_DIM), values.reshape(rows, key_length, HEADS, HEAD_DIM), query_seg, key_seg))
    return mixed.reshape(rows * length, HEADS * HEAD_DIM)

def split_sum(hidden, weight):
    width = hidden.shape[1] // N_TENSOR
    total = jnp.zeros((hidden.shape[0], weight.shape[1]), jnp.float32)
    for group in range(N_TENSOR):
        total = total + low(matmul(hidden[:, group * width:(group + 1) * width], weight[group * width:(group + 1) * width]))
    return low_back(total)

def reference(inputs, memory, tgt_seg, src_seg, self_query, self_key, self_value, self_out, cross_query, cross_key, cross_value, cross_out, ffn_in, ffn_out, norm_gain, norm_shift, residual_scale, cotangent):
    floats = tuple((value.astype(jnp.float32) for value in (inputs, memory, self_query, self_key, self_value, self_out, cross_query, cross_key, cross_value, cross_out, ffn_in, ffn_out, norm_gain, norm_shift, residual_scale)))

    def forward(stream, source, s_query, s_key, s_value, s_out, c_query, c_key, c_value, c_out, f_in, f_out, gains, shifts, scales):
        query = rounded(matmul(stream, s_query))
        keys = rounded(matmul(stream, s_key))
        values = rounded(matmul(stream, s_value))
        mixed = rounded(attention(query, keys, values, tgt_seg, tgt_seg, True))
        pre1 = scales[0] * stream + split_sum(mixed, s_out)
        norm1 = layer_norm(pre1, gains[0], shifts[0])
        query = rounded(matmul(low(norm1), c_query))
        keys = rounded(matmul(source, c_key))
        values = rounded(matmul(source, c_value))
        mixed = rounded(attention(query, keys, values, tgt_seg, src_seg, False))
        pre2 = scales[1] * norm1 + split_sum(mixed, c_out)
        norm2 = layer_norm(pre2, gains[1], shifts[1])
        upper = low_back(matmul(low(norm2), f_in))
        act = low(gelu_tanh(upper))
        pre3 = scales[2] * norm2 + split_sum(act, f_out)
        return layer_norm(pre3, gains[2], shifts[2])
    output, pullback = jax.vjp(forward, *floats)
    grads = pullback(cotangent.astype(jnp.float32))
    return (output.astype(jnp.bfloat16), grads[0], grads[1], grads[2], grads[3], grads[4], grads[5], grads[6], grads[7], grads[8], grads[9], grads[10], grads[11], grads[12], grads[13], grads[14])
```

```python
import functools

import jax
import jax.numpy as jnp
from jax import lax
from jax.experimental import pallas as pl
from jax.experimental.pallas import tpu as pltpu
from jax.sharding import PartitionSpec as P

HEAD_DIM = 64
QB = 128
KC = 256
GW = 256
EPS = 1e-05
NEG = -1e30
F32 = jnp.float32
BF16 = jnp.bfloat16
VMEM_LIMIT = 60 * 1024 * 1024


def nn(left, right):
    return lax.dot_general(left, right, (((1,), (0,)), ((), ())), preferred_element_type=F32)


def nt(left, right):
    return lax.dot_general(left, right, (((1,), (1,)), ((), ())), preferred_element_type=F32)


def tn(left, right):
    return lax.dot_general(left, right, (((0,), (0,)), ((), ())), preferred_element_type=F32)


def iota(shape, dim):
    return lax.broadcasted_iota(jnp.int32, shape, dim)


def normalise(pre):
    center = jnp.mean(pre, axis=-1, keepdims=True)
    centered = pre - center
    rstd = lax.rsqrt(jnp.mean(centered * centered, axis=-1, keepdims=True) + EPS)
    return centered * rstd, rstd


def norm_back(grad, gain, xhat, rstd):
    scaled = grad * gain
    first = jnp.mean(scaled, axis=-1, keepdims=True)
    second = jnp.mean(scaled * xhat, axis=-1, keepdims=True)
    return rstd * (scaled - first - xhat * second)


def rows_at(block, size):
    return pl.ds(pl.multiple_of(block * size, size), size)


def stack_heads(block):
    head = iota((1, GW), 1) // HEAD_DIM
    return jnp.concatenate(
        [block * (head == h).astype(F32).astype(BF16) for h in range(GW // HEAD_DIM)], axis=0
    )


def unstack_heads(stacked, rows):
    low_half = iota((1, 128), 1) < HEAD_DIM
    tiles = []
    for tile in range(GW // 128):
        cols = slice(tile * 128, tile * 128 + 128)
        first, second = 2 * tile, 2 * tile + 1
        tiles.append(
            jnp.where(
                low_half,
                stacked[first * rows : (first + 1) * rows, cols],
                stacked[second * rows : (second + 1) * rows, cols],
            )
        )
    return jnp.concatenate(tiles, axis=1)


def attend_block(i, q_ref, k_ref, v_ref, lo, hi, first, count, lse_ref, s_scr, m_scr, l_scr, o_scr):
    heads = GW // HEAD_DIM
    groups = q_ref.shape[1] // GW
    rows = rows_at(i, QB)
    stacks = [stack_heads(q_ref[rows, g * GW : (g + 1) * GW]) for g in range(groups)]

    def key_rows(j):
        return pl.multiple_of(first + j * KC, 16)

    def scores(g, j):
        start = key_rows(j)
        place = start + iota((QB, KC), 1)
        allowed = (place >= lo) & (place < hi)
        s = nt(stacks[g], k_ref[pl.ds(start, KC), g * GW : (g + 1) * GW])
        s = jnp.where(allowed[None], s.reshape(heads, QB, KC), NEG).reshape(heads * QB, KC)
        s_scr[g, j] = s
        return jnp.maximum(s[:, :128], s[:, 128:])

    for g in range(groups):
        m_scr[g] = scores(g, 0)

    @pl.loop(1, count)
    def _(j):
        for g in range(groups):
            m_scr[g] = jnp.maximum(m_scr[g], scores(g, j))

    peaks = [jnp.max(m_scr[g], axis=-1, keepdims=True) for g in range(groups)]

    def weigh(g, j):
        p = jnp.exp(s_scr[g, j] - peaks[g])
        o = nn(p.astype(BF16), v_ref[pl.ds(key_rows(j), KC), g * GW : (g + 1) * GW])
        return p[:, :128] + p[:, 128:], o

    for g in range(groups):
        l_scr[g], o_scr[g] = weigh(g, 0)

    @pl.loop(1, count)
    def _(j):
        for g in range(groups):
            more_l, more_o = weigh(g, j)
            l_scr[g] = l_scr[g] + more_l
            o_scr[g] = o_scr[g] + more_o

    lane = iota((1, 128), 1)
    logs = jnp.zeros((QB, 128), F32)
    parts = []
    for g in range(groups):
        total = jnp.sum(l_scr[g], axis=-1, keepdims=True)
        log = peaks[g] + jnp.log(total)
        for h in range(heads):
            logs = jnp.where(lane == g * heads + h, log[h * QB : (h + 1) * QB], logs)
        parts.append(unstack_heads(o_scr[g] * (1.0 / total), QB).astype(BF16))
    lse_ref[:, rows] = jnp.transpose(logs)[: groups * heads]
    return jnp.concatenate(parts, axis=1)


def attend_back_block(
    i, q_ref, k_ref, v_ref, do_ref, lse_ref, delta_ref, lo, hi, first, count, dq_ref, dk_scr, dv_scr, r_scr
):
    heads = GW // HEAD_DIM
    groups = q_ref.shape[1] // GW
    rows = rows_at(i, QB)

    for g in range(groups):
        cols = slice(g * GW, (g + 1) * GW)
        qs = stack_heads(q_ref[rows, cols])
        ds = stack_heads(do_ref[rows, cols])

        def chunk(j):
            start = pl.multiple_of(first + j * KC, 16)
            keys = pl.ds(start, KC)
            kg = k_ref[keys, cols]
            place = start + iota((KC, QB), 0)
            allowed = (place >= lo) & (place < hi)
            st = nt(kg, qs)
            dp = nt(v_ref[keys, cols], ds)
            probs, grads = [], []
            for h in range(heads):
                part = slice(h * QB, (h + 1) * QB)
                row = slice(g * heads + h, g * heads + h + 1)
                p = jnp.where(allowed, jnp.exp(st[:, part] - lse_ref[row, rows]), 0.0)
                probs.append(p.astype(BF16))
                grads.append((p * (dp[:, part] - delta_ref[row, rows])).astype(BF16))
            prob = jnp.concatenate(probs, axis=1)
            grad = jnp.concatenate(grads, axis=1)
            dv_scr[keys, cols] += nn(prob, ds)
            dk_scr[keys, cols] += nn(grad, qs)
            return tn(grad, kg)

        r_scr[g] = chunk(0)

        @pl.loop(1, count)
        def _(j):
            r_scr[g] = r_scr[g] + chunk(j)

        dq_ref[rows, cols] = (unstack_heads(r_scr[g], QB) * HEAD_DIM**-0.5).astype(BF16)


def set_delta(i, do, mixed, delta_scr):
    heads = do.shape[1] // HEAD_DIM
    product = do.astype(F32) * mixed.astype(F32)
    high = product.astype(BF16)
    rest = (product - high.astype(F32)).astype(BF16)
    pick = (iota((heads, do.shape[1]), 1) // HEAD_DIM == iota((heads, do.shape[1]), 0)).astype(F32).astype(BF16)
    delta_scr[:, rows_at(i, QB)] = nt(pick, high) + nt(pick, rest)


def put_transposed(i, block, scr, chunk):
    turned = jnp.transpose(block)
    for n in range(turned.shape[0] // chunk):
        scr[n % 2, (n // 2) * chunk : (n // 2 + 1) * chunk, rows_at(i, QB)] = turned[n * chunk : (n + 1) * chunk]


def add_sum(ref, row, value):
    ref[row : row + 1, :] += jnp.sum(value, axis=0, keepdims=True)


def self_forward(
    sc, x, qo, qx, ko, kx, vo, vx, oo, ox, bcol, gain, shift, omega,
    q, k, v, mixed, lse, xhat, rstd, s_scr, m_scr, l_scr, o_scr,
):
    half = qo.shape[1]
    scale = HEAD_DIM**-0.5

    @pl.loop(0, x.shape[0] // 256)
    def _(i):
        rows = rows_at(i, 256)
        block = x[rows, :]
        for out, own, other, factor in ((q, qo, qx, scale), (k, ko, kx, 1.0), (v, vo, vx, 1.0)):
            out[rows, :half] = (nn(block, own[...]) * factor).astype(BF16)
            out[rows, half:] = (nn(block, other[...]) * factor).astype(BF16)

    blocks = x.shape[0] // QB

    @pl.loop(0, blocks)
    def _(i):
        rows = rows_at(i, QB)
        block = attend_block(
            i, q, k, v, bcol[rows, 0:1], bcol[rows, 1:2], sc[2 + i], sc[2 + blocks + i], lse, s_scr, m_scr, l_scr, o_scr
        )
        mixed[rows, :] = block
        branch = nn(block[:, :half], oo[...]) + nn(block[:, half:], ox[...])
        pre = omega[0:1] * x[rows, :].astype(F32) + branch
        hat, inv = normalise(pre)
        xhat[rows, :] = hat
        rstd[rows, :] = jnp.broadcast_to(inv, (QB, rstd.shape[1]))


def cross_forward(
    sc, xhat1, mem, qo, qx, ko, kx, vo, vx, oo, ox, bcol, gain, shift, omega,
    q, k, v, mixed, lse, xhat, rstd, s_scr, m_scr, l_scr, o_scr,
):
    half = qo.shape[1]
    scale = HEAD_DIM**-0.5

    @pl.loop(0, mem.shape[0] // 256)
    def _(i):
        rows = rows_at(i, 256)
        low1 = (xhat1[rows, :] * gain[0:1] + shift[0:1]).astype(BF16)
        block = mem[rows, :]
        for out, left, own, other, factor in (
            (q, low1, qo, qx, scale), (k, block, ko, kx, 1.0), (v, block, vo, vx, 1.0)
        ):
            out[rows, :half] = (nn(left, own[...]) * factor).astype(BF16)
            out[rows, half:] = (nn(left, other[...]) * factor).astype(BF16)

    blocks = mem.shape[0] // QB

    @pl.loop(0, blocks)
    def _(i):
        rows = rows_at(i, QB)
        block = attend_block(
            i, q, k, v, bcol[rows, 2:3], bcol[rows, 3:4], sc[2 + 2 * blocks + i], sc[2 + 3 * blocks + i],
            lse, s_scr, m_scr, l_scr, o_scr,
        )
        mixed[rows, :] = block
        branch = nn(block[:, :half], oo[...]) + nn(block[:, half:], ox[...])
        pre = omega[1:2] * (xhat1[rows, :] * gain[0:1] + shift[0:1]) + branch
        hat, inv = normalise(pre)
        xhat[rows, :] = hat
        rstd[rows, :] = jnp.broadcast_to(inv, (QB, rstd.shape[1]))


def ffn_forward(
    sc, xhat2, io, ix, oo, ox, cot, gain, shift, omega,
    out, act, slope, d_pre3, sums,
):
    sums[...] = jnp.zeros_like(sums)
    size = 256
    width = 512
    half = io.shape[1]

    @pl.loop(0, xhat2.shape[0] // size)
    def _(i):
        rows = rows_at(i, size)
        norm2 = xhat2[rows, :] * gain[1:2] + shift[1:2]
        low2 = norm2.astype(BF16)
        pre = omega[2:3] * norm2
        for first in range(0, 2 * half, width):
            part = first % half
            win = (io if first < half else ix)[:, part : part + width]
            wout = (oo if first < half else ox)[part : part + width, :]
            u = nn(low2, win)
            square = u * u
            t = jnp.tanh(0.7978845608028654 * u * (1.0 + 0.044715 * square))
            a = (0.5 * u * (1.0 + t)).astype(BF16)
            act[rows, first : first + width] = a
            slope[rows, first : first + width] = (
                0.5 * (1.0 + t)
                + 0.5 * u * (1.0 - t * t) * (0.7978845608028654 * (1.0 + 0.134145 * square))
            ).astype(BF16)
            pre = pre + nn(a, wout)
        hat, inv = normalise(pre)
        out[rows, :] = (hat * gain[2:3] + shift[2:3]).astype(BF16)
        grad = cot[rows, :].astype(F32)
        d_pre = norm_back(grad, gain[2:3], hat, inv)
        d_pre3[rows, :] = d_pre
        add_sum(sums, 0, grad * hat)
        add_sum(sums, 1, grad)
        add_sum(sums, 2, d_pre * norm2)


def ffn_backward(
    sc, d_pre3, act, slope, xhat2, rstd2, io, ix, oo, ox, gain, shift, omega,
    d_pre2, keep_own, keep_oth, send_own, send_oth, sums, up_scr, norm_t, grad_t, *, chunk,
):
    sums[...] = jnp.zeros_like(sums)
    half = io.shape[1]

    @pl.loop(0, xhat2.shape[0] // QB)
    def _(i):
        rows = rows_at(i, QB)
        grad = d_pre3[rows, :]
        low = grad.astype(BF16)
        hat = xhat2[rows, :]
        low2 = (hat * gain[1:2] + shift[1:2]).astype(BF16)
        put_transposed(i, low2, norm_t, chunk)
        put_transposed(i, low, grad_t, chunk)
        total = omega[2:3] * grad
        for side, (win, wout) in enumerate(((io, oo), (ix, ox))):
            up = (slope[rows, side * half : (side + 1) * half].astype(F32) * nt(low, wout[...])).astype(BF16)
            up_scr[rows, side * half : (side + 1) * half] = up
            total = total + nt(up, win[...])
        d_pre2[rows, :] = norm_back(total, gain[1:2], hat, rstd2[rows, 0:1])
        add_sum(sums, 0, total * hat)
        add_sum(sums, 1, total)

    core = sc[1]
    width = 256
    for slot, (own, oth) in enumerate(((keep_own, keep_oth), (send_own, send_oth))):
        place = core if slot == 0 else 1 - core
        for side, out in enumerate((own, oth)):

            @pl.loop(0, half // width)
            def _(n):
                cols = pl.ds(pl.multiple_of(side * half + n * width, width), width)
                out[:, pl.ds(pl.multiple_of(n * width, width), width)] = nn(norm_t[place], up_scr[:, cols]).astype(BF16)
                out[:, pl.ds(pl.multiple_of(half + n * width, width), width)] = nn(grad_t[place], act[:, cols]).astype(
                    BF16
                )


def weight_grads(core, pairs, keep_own, keep_oth, send_own, send_oth):
    for slot, (own, oth) in enumerate(((keep_own, keep_oth), (send_own, send_oth))):
        place = core if slot == 0 else 1 - core
        for n, (left, right) in enumerate(pairs):
            half = right.shape[1] // 2
            own[:, n * half : (n + 1) * half] = nn(left[place], right[:, :half]).astype(BF16)
            oth[:, n * half : (n + 1) * half] = nn(left[place], right[:, half:]).astype(BF16)


def cross_backward(
    sc, d_pre2, q, k, v, mixed, lse, xhat1, rstd1, mem, qo, qx, ko, kx, vo, vx, oo, ox, brow, gain, shift, omega,
    d_pre1, mem_keep, mem_send, keep_own, keep_oth, send_own, send_oth, sums,
    do_scr, delta, dq_scr, dk_scr, dv_scr, dkb, dvb, r_scr, norm_t, mem_t, grad_t, *, chunk,
):
    sums[...] = jnp.zeros_like(sums)
    half = qo.shape[1]
    blocks = mem.shape[0] // QB
    dk_scr[...] = jnp.zeros_like(dk_scr)
    dv_scr[...] = jnp.zeros_like(dv_scr)

    @pl.loop(0, blocks)
    def _(i):
        rows = rows_at(i, QB)
        grad = d_pre2[rows, :]
        low = grad.astype(BF16)
        norm1 = xhat1[rows, :] * gain[0:1] + shift[0:1]
        put_transposed(i, low, grad_t, chunk)
        put_transposed(i, norm1.astype(BF16), norm_t, chunk)
        put_transposed(i, mem[rows, :], mem_t, chunk)
        do = jnp.concatenate([nt(low, oo[...]), nt(low, ox[...])], axis=1).astype(BF16)
        do_scr[rows, :] = do
        set_delta(i, do, mixed[rows, :], delta)
        add_sum(sums, 0, grad * norm1)

    @pl.loop(0, blocks)
    def _(i):
        rows = rows_at(i, QB)
        attend_back_block(
            i, q, k, v, do_scr, lse, delta, brow[2:3, rows], brow[3:4, rows],
            sc[2 + 2 * blocks + i], sc[2 + 3 * blocks + i], dq_scr, dk_scr, dv_scr, r_scr,
        )

    tensor = sc[0]
    mine = pl.ds(pl.multiple_of(tensor * half, half), half)
    theirs = pl.ds(pl.multiple_of((1 - tensor) * half, half), half)

    @pl.loop(0, blocks)
    def _(i):
        rows = rows_at(i, QB)
        dq = dq_scr[rows, :]
        total = omega[1:2] * d_pre2[rows, :] + nt(dq[:, :half], qo[...]) + nt(dq[:, half:], qx[...])
        hat = xhat1[rows, :]
        d_pre1[rows, :] = norm_back(total, gain[0:1], hat, rstd1[rows, 0:1])
        add_sum(sums, 1, total * hat)
        add_sum(sums, 2, total)
        dk = dk_scr[rows, :].astype(BF16)
        dv = dv_scr[rows, :].astype(BF16)
        dkb[rows, :] = dk
        dvb[rows, :] = dv

        def part(which):
            return (
                nt(dk[:, :half], ko[which, :]) + nt(dk[:, half:], kx[which, :])
                + nt(dv[:, :half], vo[which, :]) + nt(dv[:, half:], vx[which, :])
            )

        mem_keep[rows, :] = part(mine)
        mem_send[rows, :] = part(theirs).astype(BF16)

    weight_grads(
        sc[1], ((norm_t, dq_scr), (mem_t, dkb), (mem_t, dvb), (grad_t, mixed)), keep_own, keep_oth, send_own, send_oth
    )


def self_backward(
    sc, d_pre1, q, k, v, mixed, lse, x, qo, qx, ko, kx, vo, vx, oo, ox, brow, omega,
    in_keep, in_send, keep_own, keep_oth, send_own, send_oth, sums,
    do_scr, delta, dq_scr, dk_scr, dv_scr, dkb, dvb, r_scr, in_t, grad_t, *, chunk,
):
    sums[...] = jnp.zeros_like(sums)
    half = qo.shape[1]
    blocks = x.shape[0] // QB
    dk_scr[...] = jnp.zeros_like(dk_scr)
    dv_scr[...] = jnp.zeros_like(dv_scr)

    @pl.loop(0, blocks)
    def _(i):
        rows = rows_at(i, QB)
        grad = d_pre1[rows, :]
        low = grad.astype(BF16)
        block = x[rows, :]
        put_transposed(i, low, grad_t, chunk)
        put_transposed(i, block, in_t, chunk)
        do = jnp.concatenate([nt(low, oo[...]), nt(low, ox[...])], axis=1).astype(BF16)
        do_scr[rows, :] = do
        set_delta(i, do, mixed[rows, :], delta)
        add_sum(sums, 0, grad * block.astype(F32))

    @pl.loop(0, blocks)
    def _(i):
        rows = rows_at(i, QB)
        attend_back_block(
            i, q, k, v, do_scr, lse, delta, brow[0:1, rows], brow[1:2, rows],
            sc[2 + i], sc[2 + blocks + i], dq_scr, dk_scr, dv_scr, r_scr,
        )

    tensor = sc[0]

    @pl.loop(0, blocks)
    def _(i):
        rows = rows_at(i, QB)
        dq = dq_scr[rows, :]
        dk = dk_scr[rows, :].astype(BF16)
        dv = dv_scr[rows, :].astype(BF16)
        dkb[rows, :] = dk
        dvb[rows, :] = dv

        def part(side):
            which = pl.ds(pl.multiple_of(side * half, half), half)
            return (
                nt(dq[:, :half], qo[which, :]) + nt(dq[:, half:], qx[which, :])
                + nt(dk[:, :half], ko[which, :]) + nt(dk[:, half:], kx[which, :])
                + nt(dv[:, :half], vo[which, :]) + nt(dv[:, half:], vx[which, :])
                + omega[0:1, which] * d_pre1[rows, which]
            )

        in_keep[rows, :] = part(tensor)
        in_send[rows, :] = part(1 - tensor).astype(BF16)

    weight_grads(
        sc[1], ((in_t, dq_scr), (in_t, dkb), (in_t, dvb), (grad_t, mixed)), keep_own, keep_oth, send_own, send_oth
    )


def whole_spec(shape):
    return pl.BlockSpec(shape, lambda i, sc: (0,) * len(shape))


def call(body, sc, args, outs, scratch, row_args=(), name=None):
    in_specs = []
    for n, arg in enumerate(args):
        if n in row_args:
            in_specs.append(pl.BlockSpec((row_args[n], arg.shape[1]), lambda i, sc: (sc[0], 0)))
        else:
            in_specs.append(whole_spec(arg.shape))
    return pl.pallas_call(
        body,
        out_shape=[jax.ShapeDtypeStruct(shape, kind) for shape, kind in outs],
        grid_spec=pltpu.PrefetchScalarGridSpec(
            num_scalar_prefetch=1,
            grid=(1,),
            in_specs=in_specs,
            out_specs=[whole_spec(shape) for shape, _ in outs],
            scratch_shapes=[pltpu.VMEM(shape, kind) for shape, kind in scratch],
        ),
        compiler_params=pltpu.CompilerParams(vmem_limit_bytes=VMEM_LIMIT),
        name=name,
    )(sc, *args)


def local(
    inputs, memory, tgt_seg, src_seg, self_query, self_key, self_value, self_out,
    cross_query, cross_key, cross_value, cross_out, ffn_in, ffn_out,
    norm_gain, norm_shift, residual_scale, cotangent, *, n_dp, n_tensor,
):
    d = lax.axis_index("dp")
    t = lax.axis_index("tensor")
    core = d % 2
    length = tgt_seg.shape[1]
    model = inputs.shape[1]
    half = model // n_tensor
    hidden = ffn_in.shape[1]
    blocks = length // QB
    chunk = model // n_dp
    dealt = chunk % 16 == 0
    swap_y = [(0, 1), (1, 0)]

    def swap(n_bit):
        return [(i, i ^ n_bit) for i in range(n_dp)]

    tgt = lax.dynamic_index_in_dim(tgt_seg, t, 0, keepdims=False)
    src = lax.dynamic_index_in_dim(src_seg, t, 0, keepdims=False)
    self_lo = jnp.sum((tgt[None, :] < tgt[:, None]).astype(jnp.int32), axis=1)
    self_hi = jnp.arange(1, length + 1, dtype=jnp.int32)
    cross_lo = jnp.sum((src[None, :] < tgt[:, None]).astype(jnp.int32), axis=1)
    cross_hi = jnp.sum((src[None, :] <= tgt[:, None]).astype(jnp.int32), axis=1)

    def ranges(lo, hi):
        start = lo[::QB] // 16 * 16
        count = (hi[QB - 1 :: QB] - start + KC - 1) // KC
        return jnp.minimum(start, length - count * KC), count

    bounds = jnp.stack([self_lo, self_hi, cross_lo, cross_hi])
    brow = jnp.concatenate([bounds, bounds])
    bcol = bounds.T
    sc = jnp.concatenate(
        [jnp.stack([t, core if dealt else jnp.zeros_like(core)]).astype(jnp.int32), *ranges(self_lo, self_hi),
         *ranges(cross_lo, cross_hi)]
    )

    def fetch(weights, after=None):
        parts = [lax.dynamic_slice_in_dim(w, core * (w.shape[0] // 2), w.shape[0] // 2, 0) for w in weights]
        if after is not None:
            parts, _ = lax.optimization_barrier((parts, after))
        mine = [lax.ppermute(p, "tensor", swap_y) for p in parts]
        other = [lax.ppermute(p, "dp", swap(1)) for p in mine]
        return mine, [
            jnp.where(core == 0, jnp.concatenate([a, b]), jnp.concatenate([b, a])) for a, b in zip(mine, other)
        ]

    s_first, s_oth = fetch((self_query, self_key, self_value, self_out))
    c_first, c_oth = fetch((cross_query, cross_key, cross_value, cross_out), s_first)
    _, (in_oth, out_oth) = fetch((ffn_in, ffn_out), c_first)
    s_weights = []
    for own, oth in zip((self_query, self_key, self_value, self_out), s_oth):
        s_weights += [own, oth]
    c_weights = []
    for own, oth in zip((cross_query, cross_key, cross_value, cross_out), c_oth):
        c_weights += [own, oth]
    f_weights = [ffn_in, in_oth, ffn_out, out_oth]
    norms = [norm_gain, norm_shift, residual_scale]

    wide = (length, model)
    kept = [(wide, BF16)] * 4 + [((model // HEAD_DIM, length), F32), (wide, F32), ((length, 128), F32)]
    heads = GW // HEAD_DIM
    groups = model // GW
    attend_scratch = [
        ((groups, length // KC, heads * QB, KC), F32),
        ((groups, heads * QB, 128), F32),
        ((groups, heads * QB, 128), F32),
        ((groups, heads * QB, GW), F32),
    ]
    q1, k1, v1, mixed1, lse1, xhat1, rstd1 = call(
        self_forward, sc, [inputs, *s_weights, bcol, *norms], kept, attend_scratch, {0: length}, "self_forward"
    )
    q2, k2, v2, mixed2, lse2, xhat2, rstd2 = call(
        cross_forward, sc, [xhat1, memory, *c_weights, bcol, *norms], kept, attend_scratch, {1: length}, "cross_forward"
    )
    sums_shape = ((8, model), F32)
    low_wide = ((length, n_tensor * hidden), BF16)
    out_row, act, slope, d_pre3, sums3 = call(
        ffn_forward, sc, [xhat2, *f_weights, cotangent, *norms],
        [(wide, BF16), low_wide, low_wide, (wide, F32), sums_shape], [], {5: length}, "ffn_forward",
    )
    def grads(width):
        return [((model // 2, width), BF16)] * 4

    turned = ((2, model // 2, length), BF16)
    chunk_rows = chunk if dealt else model // 2
    d_pre2, *f_grads, sums2 = call(
        functools.partial(ffn_backward, chunk=chunk_rows), sc,
        [d_pre3, act, slope, xhat2, rstd2, *f_weights, *norms],
        [(wide, F32), *grads(2 * hidden), sums_shape], [low_wide, turned, turned], {}, "ffn_backward",
    )
    back_scratch = [
        (wide, BF16), ((model // HEAD_DIM, length), F32), (wide, BF16), (wide, F32), (wide, F32), (wide, BF16),
        (wide, BF16), ((groups, heads * QB, GW), F32),
    ]
    halves = [((length, half), F32), ((length, half), BF16)]
    d_pre1, mem_keep, mem_send, *c_grads, sums1 = call(
        functools.partial(cross_backward, chunk=chunk_rows), sc,
        [d_pre2, q2, k2, v2, mixed2, lse2, xhat1, rstd1, memory, *c_weights, brow, *norms],
        [(wide, F32), *halves, *grads(4 * half), sums_shape], [*back_scratch, turned, turned, turned],
        {8: length}, "cross_backward",
    )
    in_keep, in_send, *s_grads, sums0 = call(
        functools.partial(self_backward, chunk=chunk_rows), sc,
        [d_pre1, q1, k1, v1, mixed1, lse1, inputs, *s_weights, brow, residual_scale],
        [*halves, *grads(4 * half), sums_shape], [*back_scratch, turned, turned], {6: length}, "self_backward",
    )

    def both_rows(own, other):
        other = other.astype(own.dtype)
        return jnp.where(t == 0, jnp.concatenate([own, other]), jnp.concatenate([other, own]))

    output = both_rows(out_row, lax.ppermute(out_row, "tensor", swap_y))
    memory_grad = both_rows(mem_keep, lax.ppermute(mem_send, "tensor", swap_y))
    input_grad = both_rows(in_keep, lax.ppermute(in_send, "tensor", swap_y))

    def add(a, b):
        return (a.astype(F32) + b.astype(F32)).astype(BF16)

    def reduce_grads(parts):
        keep_own, keep_oth, send_own, send_oth = parts
        if not dealt:
            own = lax.psum_scatter(
                jnp.concatenate([keep_own, send_own]).astype(F32), "dp", scatter_dimension=0, tiled=True
            )
            oth = lax.psum_scatter(
                jnp.concatenate([keep_oth, send_oth]).astype(F32), "dp", scatter_dimension=0, tiled=True
            )
            return own + lax.ppermute(oth, "tensor", swap_y)
        oth = add(keep_oth, lax.ppermute(send_oth, "dp", swap(1)))
        own = add(keep_own, lax.ppermute(send_own, "dp", swap(1)))
        total = add(own, lax.ppermute(oth, "tensor", swap_y))
        bit = 2
        while bit < n_dp:
            mine = (d // bit) % 2
            dealt_rows = total.reshape(-1, 2, chunk, total.shape[1])
            keep = lax.dynamic_index_in_dim(dealt_rows, mine, 1, keepdims=False)
            send = lax.dynamic_index_in_dim(dealt_rows, 1 - mine, 1, keepdims=False)
            total = keep.astype(F32) + lax.ppermute(send, "dp", swap(bit)).astype(F32)
            bit *= 2
            if bit < n_dp:
                total = total.astype(BF16)
            total = total.reshape(-1, total.shape[-1])
        return total.astype(F32)

    f_sum = reduce_grads(f_grads)
    c_sum = reduce_grads(c_grads)
    s_sum = reduce_grads(s_grads)
    ffn_in_grad, ffn_out_grad = f_sum[:, :hidden], f_sum[:, hidden:].T
    c_out = [c_sum[:, n * half : (n + 1) * half] for n in range(4)]
    s_out = [s_sum[:, n * half : (n + 1) * half] for n in range(4)]

    sums = jnp.concatenate([sums0[0:1], sums1[:3], sums2[:2], sums3[:3]])
    if n_dp & (n_dp - 1):
        sums = lax.psum(sums, ("dp", "tensor"))
    else:
        bit = 1
        while bit < n_dp:
            sums = sums + lax.ppermute(sums, "dp", swap(bit))
            bit *= 2
        sums = sums + lax.ppermute(sums, "tensor", swap_y)
    sums = lax.dynamic_slice_in_dim(sums, d * chunk, chunk, 1)
    gain_grad = jnp.stack([sums[2], sums[4], sums[6]])
    shift_grad = jnp.stack([sums[3], sums[5], sums[7]])
    scale_grad = jnp.stack([sums[0], sums[1], sums[8]])
    return (
        output, input_grad, memory_grad, s_out[0], s_out[1], s_out[2], s_out[3].T, c_out[0], c_out[1], c_out[2],
        c_out[3].T, ffn_in_grad, ffn_out_grad, gain_grad, shift_grad, scale_grad,
    )


def solution(mesh):
    rows, cols = P("dp", None), P(None, "tensor")
    both, turned = P("dp", "tensor"), P("tensor", "dp")
    return jax.shard_map(
        functools.partial(local, n_dp=mesh.shape["dp"], n_tensor=mesh.shape["tensor"]),
        mesh=mesh,
        in_specs=(
            rows, rows, rows, rows, cols, cols, cols, turned_rows(), cols, cols, cols, turned_rows(), cols,
            turned_rows(), P(), P(), P(), rows,
        ),
        out_specs=(
            rows, both, both, both, both, both, turned, both, both, both, turned, both, turned,
            P(None, "dp"), P(None, "dp"), P(None, "dp"),
        ),
        check_vma=False,
    )


def turned_rows():
    return P("tensor", None)
```

```python
import functools

import jax
import jax.numpy as jnp
from jax import lax
from jax.experimental import pallas as pl
from jax.experimental.pallas import tpu as pltpu
from jax.sharding import PartitionSpec as P

HEAD_DIM = 64
QB = 128
KC = 256
GW = 256
EPS = 1e-05
NEG = -1e30
F32 = jnp.float32
BF16 = jnp.bfloat16
MB = 512
VMEM_LIMIT = 56 * 1024 * 1024
SEGMENTS = 32
FLOPS_PER_US = 9e8


def nn(left, right):
    return lax.dot_general(left, right, (((1,), (0,)), ((), ())), preferred_element_type=F32)


def nt(left, right):
    return lax.dot_general(left, right, (((1,), (1,)), ((), ())), preferred_element_type=F32)


def tn(left, right):
    return lax.dot_general(left, right, (((0,), (0,)), ((), ())), preferred_element_type=F32)


def iota(shape, dim):
    return lax.broadcasted_iota(jnp.int32, shape, dim)


def normalise(pre):
    center = jnp.mean(pre, axis=-1, keepdims=True)
    centered = pre - center
    rstd = lax.rsqrt(jnp.mean(centered * centered, axis=-1, keepdims=True) + EPS)
    return centered * rstd, rstd


def norm_back(grad, gain, xhat, rstd):
    scaled = grad * gain
    first = jnp.mean(scaled, axis=-1, keepdims=True)
    second = jnp.mean(scaled * xhat, axis=-1, keepdims=True)
    return rstd * (scaled - first - xhat * second)


def rows_at(block, size):
    return pl.ds(pl.multiple_of(block * size, size), size)


def stack_heads(block):
    head = iota((1, GW), 1) // HEAD_DIM
    return jnp.concatenate(
        [block * (head == h).astype(F32).astype(BF16) for h in range(GW // HEAD_DIM)], axis=0
    )


def unstack_heads(stacked, rows):
    low_half = iota((1, 128), 1) < HEAD_DIM
    tiles = []
    for tile in range(GW // 128):
        cols = slice(tile * 128, tile * 128 + 128)
        first, second = 2 * tile, 2 * tile + 1
        tiles.append(
            jnp.where(
                low_half,
                stacked[first * rows : (first + 1) * rows, cols],
                stacked[second * rows : (second + 1) * rows, cols],
            )
        )
    return jnp.concatenate(tiles, axis=1)


def attend_units(units, s_scr, m_scr, l_scr, o_scr):
    heads = GW // HEAD_DIM
    stacks = [stack_heads(q[rows_at(i, QB), :]) for i, q, *_ in units]

    def scores(n, j):
        _, _, k, _, lo, hi, first, _ = units[n]
        start = pl.multiple_of(first + j * KC, 128)
        place = start + iota((KC, QB), 0)
        allowed = (place >= lo) & (place < hi)
        s = nt(k[pl.ds(start, KC), :], stacks[n])
        peaks = []
        for h in range(heads):
            part = slice(h * QB, (h + 1) * QB)
            masked = jnp.where(allowed, s[:, part], NEG)
            s_scr[n, j, :, part] = masked
            peaks.append(jnp.max(masked, axis=0, keepdims=True))
        return jnp.concatenate(peaks, axis=1)

    for n in range(len(units)):
        m_scr[n : n + 1, :] = scores(n, 0)
    for n, unit in enumerate(units):

        @pl.loop(1, unit[7])
        def _(j):
            m_scr[n : n + 1, :] = jnp.maximum(m_scr[n : n + 1, :], scores(n, j))

    peaks = [m_scr[n : n + 1, :] for n in range(len(units))]

    def weigh(n, j):
        p = jnp.exp(s_scr[n, j] - peaks[n])
        keys = pl.ds(pl.multiple_of(units[n][6] + j * KC, 128), KC)
        return jnp.sum(p, axis=0, keepdims=True), nn(units[n][3][:, keys], p.astype(BF16))

    for n in range(len(units)):
        l_scr[n : n + 1, :], o_scr[n] = weigh(n, 0)
    for n, unit in enumerate(units):

        @pl.loop(1, unit[7])
        def _(j):
            more_l, more_o = weigh(n, j)
            l_scr[n : n + 1, :] = l_scr[n : n + 1, :] + more_l
            o_scr[n] = o_scr[n] + more_o

    results = []
    for n in range(len(units)):
        total = l_scr[n : n + 1, :]
        log = peaks[n] + jnp.log(total)
        scale = 1.0 / total
        parts = [
            o_scr[n, h * HEAD_DIM : (h + 1) * HEAD_DIM, h * QB : (h + 1) * QB] * scale[:, h * QB : (h + 1) * QB]
            for h in range(heads)
        ]
        mixed = jnp.transpose(jnp.concatenate(parts, axis=0).astype(BF16))
        results.append((mixed, [log[:, h * QB : (h + 1) * QB] for h in range(heads)]))
    return results


def attend_back_units(units, r_scr):
    heads = GW // HEAD_DIM

    def chunk(n, j):
        i, q, k, v, do, lse, delta, lo, hi, first, _, _, dk, dv = units[n]
        rows = rows_at(i, QB)
        keys = pl.ds(pl.multiple_of(first + j * KC, 16), KC)
        qs = stack_heads(q[rows, :])
        ds = stack_heads(do[rows, :])
        kg = k[keys, :]
        place = first + j * KC + iota((KC, QB), 0)
        allowed = (place >= lo) & (place < hi)
        st = nt(kg, qs)
        dp = nt(v[keys, :], ds)
        probs, grads = [], []
        for h in range(heads):
            part = slice(h * QB, (h + 1) * QB)
            p = jnp.where(allowed, jnp.exp(st[:, part] - lse[h : h + 1, rows]), 0.0)
            probs.append(p.astype(BF16))
            grads.append((p * (dp[:, part] - delta[h : h + 1, rows])).astype(BF16))
        prob = jnp.concatenate(probs, axis=1)
        grad = jnp.concatenate(grads, axis=1)
        dv[keys, :] += nn(prob, ds)
        dk[keys, :] += nn(grad, qs)
        return tn(grad, kg)

    for n in range(len(units)):
        r_scr[n] = chunk(n, 0)
    for n, unit in enumerate(units):

        @pl.loop(1, unit[10])
        def _(j):
            r_scr[n] = r_scr[n] + chunk(n, j)

    for n, unit in enumerate(units):
        unit[11][rows_at(unit[0], QB), :] = (unstack_heads(r_scr[n], QB) * HEAD_DIM**-0.5).astype(BF16)


def set_delta(rows, do, mixed, delta_scr):
    heads = do.shape[1] // HEAD_DIM
    product = do.astype(F32) * mixed.astype(F32)
    high = product.astype(BF16)
    rest = (product - high.astype(F32)).astype(BF16)
    pick = (iota((heads, do.shape[1]), 1) // HEAD_DIM == iota((heads, do.shape[1]), 0)).astype(F32).astype(BF16)
    delta_scr[:, rows] = nt(pick, high) + nt(pick, rest)


def put_transposed(rows, block, scr, chunk):
    turned = jnp.transpose(block)
    size = turned.shape[0]
    for n in range(size // chunk):
        first = (n % 2) * (size // 2) + n // 2 * chunk if chunk < size // 2 else n * chunk
        scr[first : first + chunk, rows] = turned[n * chunk : (n + 1) * chunk]


def add_sum(ref, row, value):
    ref[row : row + 1, :] += jnp.sum(value, axis=0, keepdims=True)


def project(rows, left, weight, out, factor=1.0):
    out[rows, :] = (nn(left, weight[...]) * factor).astype(BF16)


def unpack_square(mine, sib, weights):
    core = core_index()
    *cols, out = weights
    part, half = cols[0].shape[0] // 2, out.shape[0]
    small = half // 2
    for place, source in ((core, mine), (1 - core, sib)):
        for n, w in enumerate(cols):
            w[rows_at(place, part), :] = source[n * part : (n + 1) * part, :]
        base = len(cols) * part
        for n in range(out.shape[1] // half):
            out[rows_at(place, small), n * half : (n + 1) * half] = source[
                base + n * small : base + (n + 1) * small, :
            ]


def unpack_ffn(mine, sib, win, wout):
    core = core_index()
    part, rows, width = win.shape[0] // 2, wout.shape[0] // 2, wout.shape[1]
    tiles = win.shape[1] // width
    for place, source in ((core, mine), (1 - core, sib)):
        for n in range(tiles):
            win[rows_at(place, part), n * width : (n + 1) * width] = source[n * part : (n + 1) * part, :]
        wout[rows_at(place, rows), :] = source[tiles * part :, :]


def core_index():
    return lax.axis_index("dp") % 2


def set_ranges(tgt, src, brow, blocks):
    rows, length = tgt.shape
    mine = lax.axis_index("tensor")

    def row(ref):
        value = ref[0:1, :]
        for n in range(1, rows):
            value = jnp.where(mine == n, ref[n : n + 1, :], value)
        return value

    target, source = row(tgt), row(src)
    ids = iota((SEGMENTS, length), 0)

    def before(ids_of, limit):
        count = jnp.sum((ids_of < limit).astype(F32), axis=1, keepdims=True)
        return jnp.sum(jnp.where(ids == target, count, 0.0), axis=0, keepdims=True).astype(jnp.int32)

    values = [
        before(target, ids), iota((1, length), 1) + 1, before(source, ids), before(source, ids + 1)
    ]
    lane = iota((1, 128), 1)
    for n, value in enumerate(values):
        brow[n : n + 1, :] = value
        brow[n + 4 : n + 5, :] = value
    blocks[...] = jnp.zeros_like(blocks)
    for n in range(2):
        first = jnp.zeros((1, 128), jnp.int32)
        last = jnp.zeros((1, 128), jnp.int32)
        for i in range(length // QB):
            low, high = values[2 * n][:, i * QB : i * QB + 1], values[2 * n + 1][:, (i + 1) * QB - 1 : (i + 1) * QB]
            first = jnp.where(lane == i, low, first)
            last = jnp.where(lane == i, high, last)
        first = lax.shift_left(lax.shift_right_logical(first, 7), 7)
        count = lax.shift_right_logical(last - first + (KC - 1), KC.bit_length() - 1)
        blocks[2 * n : 2 * n + 1, :] = jnp.minimum(first, length - count * KC)
        blocks[2 * n + 1 : 2 * n + 2, :] = count


def forward_unit(sc, brow, i, q, k, v, which):
    rows = rows_at(i, QB)
    return (
        i, q, k, v, brow[2 * which : 2 * which + 1, rows], brow[2 * which + 1 : 2 * which + 2, rows],
        sc[2 * which, i], sc[2 * which + 1, i],
    )


def put_logs(lse, i, logs):
    for h, log in enumerate(logs):
        lse[h : h + 1, rows_at(i, QB)] = log


def project_self(x, weights, outs, v_t):
    @pl.loop(0, x.chunks)
    def _(i):
        x.need(i)
        rows = rows_at(i, MB)
        block = x[rows, :]
        for weight, out, factor in zip(weights, outs, (HEAD_DIM**-0.5, 1.0, 1.0)):
            project(rows, block, weight, out, factor)
            out.put(i)
        v_t[:, rows] = jnp.transpose(outs[2][rows, :])


def self_forward_own(sc, qo, ko, vo, x, brow, q, k, v, mixed, lse, v_t, *scratch):
    need(qo, ko, vo)
    project_self(x, (qo, ko, vo), (q, k, v), v_t)
    need(brow)

    @pl.loop(0, x.shape[0] // QB // 2)
    def _(pair):
        pair_of = [2 * pair, 2 * pair + 1]
        units = [forward_unit(sc, brow, i, q, k, v_t, 0) for i in pair_of]
        for i, (block, logs) in zip(pair_of, attend_units(units, *scratch)):
            mixed[rows_at(i, QB), :] = block
            put_logs(lse, i, logs)


def norm_rows(i, pre, xhat, rstd):
    @pl.loop(0, MB // QB)
    def _(n):
        rows = rows_at(i * (MB // QB) + n, QB)
        hat, inv = normalise(pre[rows_at(n, QB), :])
        xhat[rows, :] = hat
        rstd[rows, :] = jnp.broadcast_to(inv, (QB, rstd.shape[1]))

    xhat.put(i)
    rstd.put(i)


def self_forward_rest(
    sc, mine, sib, x, brow, mixed_own, oo, omega,
    q, k, v, mixed, lse, xhat, rstd, qx, kx, vx, ox, pre, v_t, *scratch,
):
    need(mine, sib)
    unpack_square(mine, sib, (qx, kx, vx, ox))
    project_self(x, (qx, kx, vx), (q, k, v), v_t)
    need(brow)

    @pl.loop(0, x.shape[0] // QB // 2)
    def _(pair):
        pair_of = [2 * pair, 2 * pair + 1]
        units = [forward_unit(sc, brow, i, q, k, v_t, 0) for i in pair_of]
        for i, (block, logs) in zip(pair_of, attend_units(units, *scratch)):
            mixed[rows_at(i, QB), :] = block
            put_logs(lse, i, logs)

    need(mixed_own, oo, omega)

    @pl.loop(0, x.chunks)
    def _(i):
        rows = rows_at(i, MB)
        branch = nn(mixed_own[rows, :], oo[...]) + nn(mixed[rows, :], ox[...])
        pre[...] = omega[0:1] * x[rows, :].astype(F32) + branch
        norm_rows(i, pre, xhat, rstd)


def cross_forward(
    sc, mine, sib, qo, ko, vo, gain, shift, xhat1, mem, brow, oo, omega,
    q, k, v, mixed, lse, q_x, k_x, v_x, mixed_x, lse_x, xhat, rstd, qx, kx, vx, ox, pre, v_t, v_xt, *scratch,
):
    need(mine, sib, qo, ko, vo, gain, shift)
    unpack_square(mine, sib, (qx, kx, vx, ox))

    @pl.loop(0, mem.chunks)
    def _(i):
        rows = rows_at(i, MB)
        xhat1.need(i)
        mem.need(i)
        low1 = (xhat1[rows, :] * gain[0:1] + shift[0:1]).astype(BF16)
        block = mem[rows, :]
        for weights, outs, turned in (((qo, ko, vo), (q, k, v), v_t), ((qx, kx, vx), (q_x, k_x, v_x), v_xt)):
            project(rows, low1, weights[0], outs[0], HEAD_DIM**-0.5)
            project(rows, block, weights[1], outs[1])
            project(rows, block, weights[2], outs[2])
            turned[:, rows] = jnp.transpose(outs[2][rows, :])
            for result in outs:
                result.put(i)

    need(brow)

    @pl.loop(0, mem.shape[0] // QB)
    def _(i):
        units = [forward_unit(sc, brow, i, *group, 1) for group in ((q, k, v_t), (q_x, k_x, v_xt))]
        for (block, logs), out, lse_out in zip(attend_units(units, *scratch), (mixed, mixed_x), (lse, lse_x)):
            out[rows_at(i, QB), :] = block
            put_logs(lse_out, i, logs)

    need(oo, omega)

    @pl.loop(0, mem.chunks)
    def _(i):
        rows = rows_at(i, MB)
        branch = nn(mixed[rows, :], oo[...]) + nn(mixed_x[rows, :], ox[...])
        pre[...] = omega[1:2] * (xhat1[rows, :] * gain[0:1] + shift[0:1]) + branch
        norm_rows(i, pre, xhat, rstd)


def ffn_forward(
    sc, io, oo, gain, shift, omega, xhat2, mine, sib, cot,
    out, out_all, act, slope, d_pre3, sums, ix, ox, pre,
):
    need(io, oo, gain, shift, omega, mine, sib)
    unpack_ffn(mine, sib, ix, ox)
    sums[...] = jnp.zeros_like(sums)
    width = 512
    half = io.shape[1]

    @pl.loop(0, xhat2.chunks)
    def _(i):
        rows = rows_at(i, MB)
        xhat2.need(i)
        cot.need(i)
        norm2 = xhat2[rows, :] * gain[1:2] + shift[1:2]
        low2 = norm2.astype(BF16)
        pre[...] = omega[2:3] * norm2
        for side, (win, wout) in enumerate(((io, oo), (ix, ox))):
            for first in range(0, half, width):
                u = nn(low2, win[:, first : first + width])
                square = u * u
                t = jnp.tanh(u * (0.7978845608028654 + (0.7978845608028654 * 0.044715) * square))
                h = 0.5 + 0.5 * t
                a = u * h
                place = slice(side * half + first, side * half + first + width)
                act[rows, place] = a.astype(BF16)
                steep = 2 * 0.7978845608028654 + (6 * 0.7978845608028654 * 0.044715) * square
                slope[rows, place] = (h + a * (1.0 - h) * steep).astype(BF16)
            pre[...] += nn(act[rows, side * half : (side + 1) * half], wout[...])
        act.put(i)
        slope.put(i)

        @pl.loop(0, MB // QB)
        def _(n):
            small = rows_at(i * (MB // QB) + n, QB)
            hat, inv = normalise(pre[rows_at(n, QB), :])
            result = (hat * gain[2:3] + shift[2:3]).astype(BF16)
            out[small, :] = result
            out_all[small, :] = result
            grad = cot[small, :].astype(F32)
            d_pre = norm_back(grad, gain[2:3], hat, inv)
            d_pre3[small, :] = d_pre
            add_sum(sums, 0, grad * hat)
            add_sum(sums, 1, grad)
            add_sum(sums, 2, d_pre * (xhat2[small, :] * gain[1:2] + shift[1:2]))

        for result in (out, out_all, d_pre3):
            result.put(i)


def put_grads(scr, keep, send):
    core = core_index() if keep.dealt else 0
    half = scr.shape[0] // 2
    keep.copy_from(scr.at[rows_at(core, half)])
    send.copy_from(scr.at[rows_at(1 - core, half)])


def ffn_backward(
    sc, oo, io, gain, shift, omega, d_pre3, slope, xhat2, mine, sib, rstd2, act,
    d_pre2, keep, send, sums, up_scr, norm_t, grad_t, ix, ox, acc, grads, *, chunk,
):
    need(io, oo, gain, shift, omega, mine, sib)
    unpack_ffn(mine, sib, ix, ox)
    sums[...] = jnp.zeros_like(sums)
    half = io.shape[1]
    width = 512

    @pl.loop(0, xhat2.chunks)
    def _(i):
        rows = rows_at(i, MB)
        for argument in (d_pre3, slope, xhat2):
            argument.need(i)
        grad = d_pre3[rows, :]
        low = grad.astype(BF16)
        put_transposed(rows, low, grad_t, chunk)
        acc[...] = omega[2:3] * grad
        for side, (win, wout) in enumerate(((io, oo), (ix, ox))):
            for first in range(0, half, width):
                place = slice(side * half + first, side * half + first + width)
                up_scr[rows, place] = (
                    slope[rows, place].astype(F32) * nt(low, wout[first : first + width, :])
                ).astype(BF16)
            acc[...] += nt(up_scr[rows, side * half : (side + 1) * half], win[...])

        if True:
            rstd2.need(i)

        @pl.loop(0, MB // QB)
        def _(n):
            small = rows_at(i * (MB // QB) + n, QB)
            total = acc[rows_at(n, QB), :]
            hat = xhat2[small, :]
            put_transposed(small, (hat * gain[1:2] + shift[1:2]).astype(BF16), norm_t, chunk)
            d_pre2[small, :] = norm_back(total, gain[1:2], hat, rstd2[small, 0:1])
            add_sum(sums, 0, total * hat)
            add_sum(sums, 1, total)

        d_pre2.put(i)

    need(act)
    for side in range(2):
        for left, right, base in ((norm_t, up_scr, 0), (grad_t, act, half)):
            for first in range(0, half, width):
                place = 2 * side * half + base + first
                grads[:, place : place + width] = nn(
                    left[...], right[:, side * half + first : side * half + first + width]
                ).astype(BF16)
    put_grads(grads, keep, send)


def weight_grads(pairs, grads):
    width = grads.shape[1] // 2
    for n, (left, *rights) in enumerate(pairs):
        for side, right in enumerate(rights):
            half = right.shape[1]
            first = side * width + n * half
            grads[:, first : first + half] = nn(left[...], right[...]).astype(BF16)


def backward_unit(sc, brow, i, which, q, k, v, do, lse, delta, dq, dk, dv):
    rows = rows_at(i, QB)
    return (
        i, q, k, v, do, lse, delta, brow[2 * which : 2 * which + 1, rows], brow[2 * which + 1 : 2 * which + 2, rows],
        sc[2 * which, i], sc[2 * which + 1, i], dq, dk, dv,
    )


def attention_grads(low, rows, outs):
    for out, weight, was, total in outs:
        value = nt(low, weight[...]).astype(BF16)
        out[rows, :] = value
        set_delta(rows, value, was[rows, :], total)


def cross_backward(
    sc, mine, sib, oo, gain, shift, omega, d_pre2, xhat1, mem, mixed, mixed_x, q, k, v, q_x, k_x, v_x, lse, lse_x,
    brow, qo, ko, vo, rstd1,
    d_pre1, mem_all, mem_send, keep, send, sums,
    qx, kx, vx, ox, do, do_x, delta, delta_x, dq, dq_x, dk, dk_x, dv, dv_x, dkb, dkb_x, dvb, dvb_x, r_scr,
    grad_t, norm_t, mem_t, acc, grads, *, chunk,
):
    need(mine, sib, oo, gain, shift, omega)
    unpack_square(mine, sib, (qx, kx, vx, ox))
    sums[...] = jnp.zeros_like(sums)
    half = qo.shape[1]
    blocks = mem.shape[0] // QB
    for ref in (dk, dk_x, dv, dv_x):
        ref[...] = jnp.zeros_like(ref)

    @pl.loop(0, mem.chunks)
    def _(i):
        rows = rows_at(i, MB)
        for argument in (d_pre2, xhat1, mem, mixed, mixed_x):
            argument.need(i)
        grad = d_pre2[rows, :]
        low = grad.astype(BF16)
        norm1 = xhat1[rows, :] * gain[0:1] + shift[0:1]
        put_transposed(rows, low, grad_t, chunk)
        put_transposed(rows, norm1.astype(BF16), norm_t, chunk)
        put_transposed(rows, mem[rows, :], mem_t, chunk)
        attention_grads(low, rows, ((do, oo, mixed, delta), (do_x, ox, mixed_x, delta_x)))
        add_sum(sums, 0, grad * norm1)

    need(q, k, v, q_x, k_x, v_x, lse, lse_x, brow)

    @pl.loop(0, blocks)
    def _(i):
        attend_back_units(
            [
                backward_unit(sc, brow, i, 1, q, k, v, do, lse, delta, dq, dk, dv),
                backward_unit(sc, brow, i, 1, q_x, k_x, v_x, do_x, lse_x, delta_x, dq_x, dk_x, dv_x),
            ],
            r_scr,
        )

    need(qo, ko, vo, rstd1)
    tensor = lax.axis_index("tensor")

    @pl.loop(0, mem.chunks)
    def _(i):
        rows = rows_at(i, MB)
        acc[...] = omega[1:2] * d_pre2[rows, :] + nt(dq[rows, :], qo[...]) + nt(dq_x[rows, :], qx[...])
        for low, wide in ((dkb, dk), (dkb_x, dk_x), (dvb, dv), (dvb_x, dv_x)):
            low[rows, :] = wide[rows, :].astype(BF16)

        def part(side):
            which = rows_at(side, half)
            return (
                nt(dkb[rows, :], ko[which, :]) + nt(dkb_x[rows, :], kx[which, :])
                + nt(dvb[rows, :], vo[which, :]) + nt(dvb_x[rows, :], vx[which, :])
            )

        mem_all[rows, :] = part(tensor)
        mem_send[rows, :] = part(1 - tensor).astype(BF16)

        @pl.loop(0, MB // QB)
        def _(n):
            small = rows_at(i * (MB // QB) + n, QB)
            total = acc[rows_at(n, QB), :]
            hat = xhat1[small, :]
            d_pre1[small, :] = norm_back(total, gain[0:1], hat, rstd1[small, 0:1])
            add_sum(sums, 1, total * hat)
            add_sum(sums, 2, total)

        for result in (d_pre1, mem_all, mem_send):
            result.put(i)

    weight_grads(
        ((norm_t, dq, dq_x), (mem_t, dkb, dkb_x), (mem_t, dvb, dvb_x), (grad_t, mixed, mixed_x)), grads
    )
    put_grads(grads, keep, send)


def self_backward(
    sc, mine, sib, oo, d_pre1, x, mixed, mixed_x, q, k, v, q_x, k_x, v_x, lse, lse_x, brow, sums1, sums2, sums3,
    dq, dq_x, dkb, dkb_x, dvb, dvb_x, keep, send,
    qx, kx, vx, ox, do, do_x, delta, delta_x, dk, dk_x, dv, dv_x, r_scr, grad_t, in_t, sums, sums_t, grads, *, chunk,
):
    need(mine, sib, oo)
    unpack_square(mine, sib, (qx, kx, vx, ox))
    blocks = x.shape[0] // QB
    sums[...] = jnp.zeros_like(sums)
    for ref in (dk, dk_x, dv, dv_x):
        ref[...] = jnp.zeros_like(ref)

    @pl.loop(0, x.chunks)
    def _(i):
        rows = rows_at(i, MB)
        for argument in (d_pre1, x, mixed, mixed_x):
            argument.need(i)
        grad = d_pre1[rows, :]
        low = grad.astype(BF16)
        block = x[rows, :]
        put_transposed(rows, low, grad_t, chunk)
        put_transposed(rows, block, in_t, chunk)
        attention_grads(low, rows, ((do, oo, mixed, delta), (do_x, ox, mixed_x, delta_x)))
        add_sum(sums, 0, grad * block.astype(F32))

    need(q, k, v, q_x, k_x, v_x, lse, lse_x, brow, sums1, sums2, sums3)

    @pl.loop(0, blocks)
    def _(i):
        attend_back_units(
            [
                backward_unit(sc, brow, i, 0, q, k, v, do, lse, delta, dq, dk, dv),
                backward_unit(sc, brow, i, 0, q_x, k_x, v_x, do_x, lse_x, delta_x, dq_x, dk_x, dv_x),
            ],
            r_scr,
        )

    for low, wide in ((dkb, dk), (dkb_x, dk_x), (dvb, dv), (dvb_x, dv_x)):
        low[...] = wide[...].astype(BF16)
    sums[1:4, :] = sums1[0:3, :]
    sums[4:6, :] = sums2[0:2, :]
    sums[6:9, :] = sums3[0:3, :]
    put_transposed(pl.ds(0, QB), sums[...].astype(BF16), sums_t, chunk)
    weight_grads(((in_t, dq, dq_x), (in_t, dkb, dkb_x), (in_t, dvb, dvb_x), (grad_t, mixed, mixed_x)), grads)
    width = grads.shape[1] // 2
    for side in range(2):
        grads[:, (side + 1) * width - QB : (side + 1) * width] = sums_t[...]
    put_grads(grads, keep, send)


def input_backward(
    sc, mine, sib, qo, ko, vo, omega, d_pre1, dq, dq_x, dk, dk_x, dv, dv_x, in_all, in_send, qx, kx, vx, ox
):
    need(mine, sib, qo, ko, vo, omega)
    unpack_square(mine, sib, (qx, kx, vx, ox))
    half = qo.shape[1]
    tensor = lax.axis_index("tensor")

    @pl.loop(0, d_pre1.chunks)
    def _(i):
        rows = rows_at(i, MB)
        for argument in (d_pre1, dq, dq_x, dk, dk_x, dv, dv_x):
            argument.need(i)

        def part(side):
            which = rows_at(side, half)
            total = omega[0:1, which] * d_pre1[rows, which]
            for grad, weight in ((dq, qo), (dq_x, qx), (dk, ko), (dk_x, kx), (dv, vo), (dv_x, vx)):
                total = total + nt(grad[rows, :], weight[which, :])
            return total

        in_all[rows, :] = part(tensor)
        in_send[rows, :] = part(1 - tensor).astype(BF16)
        in_all.put(i)
        in_send.put(i)


def fill_kernel(sc, other, out):
    @pl.loop(0, other.chunks)
    def _(i):
        other.need(i)
        rows = rows_at(i, other.shape[0] // other.chunks)
        out[rows, :] = other[rows, :].astype(out.dtype)
        out.put(i)


class Buffer:
    def __init__(self, ref, far, sems, chunks):
        self.ref, self.far, self.sems, self.chunks = ref, far, sems, chunks
        self.shape, self.dtype = far.shape, far.dtype

    def __getitem__(self, index):
        return self.ref[index]

    def __setitem__(self, index, value):
        self.ref[index] = value

    def chunk(self, i):
        size = self.shape[0] // self.chunks
        if self.chunks == 1:
            return self.ref, self.far
        rows = rows_at(i, size)
        return self.ref.at[rows], self.far.at[rows]

    def load(self):
        for i in range(self.chunks):
            near, far = self.chunk(i)
            pltpu.make_async_copy(far, near, self.sems.at[i]).start()

    def need(self, i):
        near, far = self.chunk(i)
        pltpu.make_async_copy(far, near, self.sems.at[i]).wait()

    def put(self, i=0):
        near, far = self.chunk(i)
        pltpu.make_async_copy(near, far, self.sems.at[0]).start()

    def copy_from(self, near):
        pltpu.make_async_copy(near, self.far, self.sems.at[0]).start()

    def done(self):
        pltpu.make_async_copy(self.far, self.far, self.sems.at[0]).wait()


def need(*buffers):
    for buffer in buffers:
        for i in range(buffer.chunks):
            buffer.need(i)


def call(
    body, sc, args, outs, scratch, us, picks=None, puts=None, alias=None, cuts=None, out_cuts=None, bare=(), dealt=True
):
    picks, puts, cuts, out_cuts = picks or {}, puts or {}, cuts or {}, out_cuts or {}

    def block(ref, pick):
        if pick is None:
            return ref
        rows, other = pick
        place = lax.axis_index("tensor")
        return ref.at[rows_at(1 - place if other else place, rows)]

    def size(shape, pick):
        return shape if pick is None else (pick[0], *shape[1:])

    loads = [n for n in range(len(args)) if n != alias]

    def kernel(sc, *refs):
        refs = list(refs)
        ins = [refs.pop(0) for _ in args]
        far_outs = [refs.pop(0) for _ in outs]
        near_ins = [refs.pop(0) for _ in loads]
        near_outs = [None if n in bare else refs.pop(0) for n in range(len(outs))]
        in_sems = [refs.pop(0) for _ in loads]
        out_sems = [refs.pop(0) for _ in outs]
        arguments = [
            Buffer(near, block(ins[n], picks.get(n)), sems, cuts.get(n, 1))
            for n, near, sems in zip(loads, near_ins, in_sems)
        ]
        results = [
            Buffer(near, block(far, puts.get(n)), sems, out_cuts.get(n, 1))
            for n, (far, near, sems) in enumerate(zip(far_outs, near_outs, out_sems))
        ]
        for result in results:
            result.dealt = dealt
        for argument in arguments:
            argument.load()
        body(sc, *arguments, *results, *refs)
        for n, result in enumerate(results):
            if n not in out_cuts and n not in bare:
                result.put()
        for result in results:
            result.done()

    return pl.pallas_call(
        kernel,
        out_shape=[jax.ShapeDtypeStruct(shape, kind) for shape, kind in outs],
        grid_spec=pltpu.PrefetchScalarGridSpec(
            num_scalar_prefetch=1,
            grid=(1,),
            in_specs=[pl.BlockSpec(memory_space=pl.ANY)] * len(args),
            out_specs=[pl.BlockSpec(memory_space=pl.ANY)] * len(outs),
            scratch_shapes=[
                *[pltpu.VMEM(size(args[n].shape, picks.get(n)), args[n].dtype) for n in loads],
                *[pltpu.VMEM(size(shape, puts.get(n)), kind) for n, (shape, kind) in enumerate(outs) if n not in bare],
                *[pltpu.SemaphoreType.DMA((cuts.get(n, 1),)) for n in loads],
                *[pltpu.SemaphoreType.DMA((1,)) for _ in outs],
                *[pltpu.VMEM(shape, kind) for shape, kind in scratch],
            ],
        ),
        input_output_aliases={} if alias is None else {alias + 1: 0},
        cost_estimate=pl.CostEstimate(flops=int(us * FLOPS_PER_US), bytes_accessed=1024, transcendentals=0),
        compiler_params=pltpu.CompilerParams(vmem_limit_bytes=VMEM_LIMIT),
        name=(body.func if isinstance(body, functools.partial) else body).__name__,
    )(sc, *args)


def pack(weights, outs, moves, segments=None):
    extra = [] if segments is None else list(segments)
    length = extra[0].shape[1] if extra else 0
    ranges = [((8, length), jnp.int32), ((8, 128), jnp.int32)] if extra else []

    def pack_weights(*refs):
        refs = list(refs)
        sources = [refs.pop(0) for _ in weights]
        ids = [refs.pop(0) for _ in extra]
        targets = [refs.pop(0) for _ in outs]
        sem = refs.pop()
        core = core_index()
        copies = []
        for n, (which, rows, first, out, start) in enumerate(moves):
            width = outs[out][0][1]
            copies.append(
                pltpu.make_async_copy(
                    sources[which].at[rows_at(core, rows), first : first + width],
                    targets[out].at[start : start + rows, :],
                    sem.at[n],
                )
            )
        for copy in copies:
            copy.start()
        if ids:
            set_ranges(*ids, *refs)
        for copy in copies:
            copy.wait()

    near = pl.BlockSpec(memory_space=pltpu.VMEM)
    return pl.pallas_call(
        pack_weights,
        out_shape=[jax.ShapeDtypeStruct(shape, kind) for shape, kind in outs + ranges],
        in_specs=[pl.BlockSpec(memory_space=pl.ANY)] * len(weights) + [near] * len(extra),
        out_specs=[near] * len(outs + ranges),
        scratch_shapes=[pltpu.SemaphoreType.DMA((len(moves),))],
        cost_estimate=pl.CostEstimate(flops=int(FLOPS_PER_US), bytes_accessed=1024, transcendentals=0),
        compiler_params=pltpu.CompilerParams(vmem_limit_bytes=16 * 1024 * 1024),
        name="pack_weights",
    )(*weights, *extra)


def local(
    inputs, memory, tgt_seg, src_seg, self_query, self_key, self_value, self_out,
    cross_query, cross_key, cross_value, cross_out, ffn_in, ffn_out,
    norm_gain, norm_shift, residual_scale, cotangent, *, n_dp, n_tensor,
):
    d = lax.axis_index("dp")
    t = lax.axis_index("tensor")
    length = tgt_seg.shape[1]
    model = inputs.shape[1]
    half = model // n_tensor
    hidden = ffn_in.shape[1]
    blocks = length // QB
    chunk = model // n_dp
    dealt = chunk % 16 == 0 and n_dp & (n_dp - 1) == 0
    swap_y = [(0, 1), (1, 0)]

    def swap(n_bit):
        return [(i, i ^ n_bit) for i in range(n_dp)]

    def after(value, *others):
        return lax.optimization_barrier((value, others))[0]

    own_s = [self_query, self_key, self_value, self_out]
    own_c = [cross_query, cross_key, cross_value, cross_out]
    own_f = [ffn_in, ffn_out]
    square = ((4 * half, half), BF16)

    def square_moves(base, out):
        part = model // 2
        moves = [(base + n, part, 0, out, n * part) for n in range(3)]
        return moves + [(base + 3, half // 2, n * half, out, 3 * part + n * half // 2) for n in range(n_tensor)]

    (pack_s,) = pack(own_s, [square], square_moves(0, 0))
    tiles = hidden // model
    pack_c, pack_f, brow, sc = pack(
        own_c + own_f, [square, ((tiles * half + hidden // 2, model), BF16)],
        square_moves(0, 0)
        + [(4, model // 2, n * model, 1, n * model // 2) for n in range(tiles)]
        + [(5, hidden // 2, 0, 1, tiles * model // 2)],
        (tgt_seg, src_seg),
    )
    mine_s = lax.ppermute(pack_s, "tensor", swap_y)

    def fill(whole, other):
        (result,) = call(
            fill_kernel, sc, [whole, other], [(whole.shape, whole.dtype)], [], 1, None, {0: (length, True)}, 0,
            cuts={1: 4}, out_cuts={0: 4},
        )
        return result

    def total(*parts):
        if not dealt:
            return jnp.concatenate(parts)
        result = parts[0].astype(F32)
        for part in parts[1:]:
            result = result + part.astype(F32)
        return result

    def core_send(send):
        return lax.ppermute(send, "dp", swap(1)) if dealt else send

    def near_send(keep):
        if not dealt:
            return keep
        width = keep.shape[1] // 2
        mine = (d // 2) % 2
        near = keep.reshape(-1, 2, chunk, 2 * width)
        here = lax.dynamic_index_in_dim(near, mine, 1, keepdims=False)
        there = lax.dynamic_index_in_dim(near, 1 - mine, 1, keepdims=False)
        across = [(i * 2 + j, (i ^ 2) * 2 + 1 - j) for i in range(n_dp) for j in range(2)]
        return (
            here[..., :width],
            lax.ppermute(there[..., width:], ("dp", "tensor"), across),
            lax.ppermute(here[..., width:], "tensor", swap_y),
            lax.ppermute(there[..., :width], "dp", swap(2)),
        )

    def near_sum(near):
        return total(*near).astype(BF16) if dealt else near

    def far_send(part):
        if not dealt:
            return part
        far = n_dp // 4
        row = d // 4
        parts = [lax.dynamic_index_in_dim(part, row, 0, keepdims=False)]
        for step in range(1, far):
            perm = [(i, i % 4 + (i // 4 + step) % far * 4) for i in range(n_dp)]
            out = lax.dynamic_index_in_dim(part, (row + step) % far, 0, keepdims=False)
            parts.append(lax.ppermute(out, "dp", perm))
        return parts

    def far_sum(parts):
        if dealt:
            return total(*parts)
        return reduce_any(parts)

    def reduce_any(grad):
        grad = lax.psum_scatter(grad.astype(F32), "dp", scatter_dimension=0, tiled=True)
        width = grad.shape[1] // 2
        return grad[:, :width] + lax.ppermute(grad[:, width:], "tensor", swap_y)

    wide, side = (length, model), (length, half)
    heads = GW // HEAD_DIM
    group = [(side, BF16)] * 4 + [((half // HEAD_DIM, length), F32)]
    square_weights = [((model, half), BF16)] * 3 + [((half, model), BF16)]
    stats = [(wide, F32), ((length, 128), F32)]
    attend_scratch = [
        ((2, length // KC, KC, heads * QB), F32),
        ((2, heads * QB), F32),
        ((2, heads * QB), F32),
        ((2, GW, heads * QB), F32),
    ]
    turned_side, block_wide = ((half, length), BF16), ((MB, model), F32)
    cut = length // MB
    norms = [norm_gain, norm_shift, residual_scale]
    s_own = call(
        self_forward_own, sc, [*own_s[:3], inputs, brow], group, [turned_side, *attend_scratch], 7, {3: (length, False)},
        cuts={3: cut}, out_cuts={0: cut, 1: cut, 2: cut},
    )
    s_own, mine_s = lax.optimization_barrier((s_own, mine_s))
    sib_s = lax.ppermute(mine_s, "dp", swap(1))
    mine_c = lax.ppermute(after(pack_c, mine_s), "tensor", swap_y)
    s_rest_stats = call(
        self_forward_rest, sc, [mine_s, sib_s, inputs, brow, s_own[3], self_out, residual_scale], group + stats,
        [*square_weights, block_wide, turned_side, *attend_scratch], 8, {2: (length, False)},
        cuts={2: cut}, out_cuts={n: cut for n in (0, 1, 2, 5, 6)},
    )
    s_rest_stats, mine_c = lax.optimization_barrier((s_rest_stats, mine_c))
    *s_rest, xhat1, rstd1 = s_rest_stats
    sib_c = lax.ppermute(mine_c, "dp", swap(1))
    mine_f = lax.ppermute(after(pack_f, mine_c), "tensor", swap_y)
    c_stats = call(
        cross_forward, sc,
        [mine_c, sib_c, *own_c[:3], norm_gain, norm_shift, xhat1, memory, brow, cross_out, residual_scale],
        group + group + stats,
        [*square_weights, block_wide, turned_side, turned_side, *attend_scratch], 14, {8: (length, False)}, cuts={7: cut, 8: cut},
        out_cuts={n: cut for n in (0, 1, 2, 5, 6, 7, 10, 11)},
    )
    c_stats, mine_f = lax.optimization_barrier((c_stats, mine_f))
    *c_state, xhat2, rstd2 = c_stats
    sib_f = lax.ppermute(mine_f, "dp", swap(1))
    sums_shape = ((8, model), F32)
    low_wide = ((length, n_tensor * hidden), BF16)
    f_weights = [((model, hidden), BF16), ((hidden, model), BF16)]
    out_row, output, act, slope, d_pre3, sums3 = call(
        ffn_forward, sc, [*own_f, *norms, xhat2, mine_f, sib_f, cotangent],
        [(wide, BF16), ((n_tensor * length, model), BF16), low_wide, low_wide, (wide, F32), sums_shape],
        [*f_weights, block_wide], 12,
        {8: (length, False)}, {1: (length, False)}, cuts={5: cut, 8: cut}, out_cuts={n: cut for n in range(5)},
    )
    out_other = lax.ppermute(out_row, "tensor", swap_y)

    def grads(width):
        return [((model // 2, 2 * width), BF16)] * 2

    turned = ((model, length), BF16)
    chunk_rows = chunk if dealt else model // 2
    back, out_other = lax.optimization_barrier((
        call(
            functools.partial(ffn_backward, chunk=chunk_rows), sc,
            [ffn_out, ffn_in, *norms, d_pre3, slope, xhat2, mine_f, sib_f, rstd2, act],
            [(wide, F32), *grads(2 * hidden), sums_shape],
            [low_wide, turned, turned, *f_weights, block_wide, ((model, 4 * hidden), BF16)], 18,
            cuts={n: cut for n in (5, 6, 7, 10)}, out_cuts={0: cut}, bare=(1, 2), dealt=dealt,
        ),
        out_other,
    ))
    d_pre2, f_keep, f_send, sums2 = back
    f_other = core_send(f_send)
    output = fill(output, out_other)
    f_total = total(f_keep, f_other).astype(BF16)
    f_near = near_send(f_total)
    logs = ((half // HEAD_DIM, length), F32)
    halves = [((n_tensor * length, half), F32), (side, BF16)]
    back, f_near = lax.optimization_barrier((
        call(
            functools.partial(cross_backward, chunk=chunk_rows), sc,
            [mine_c, sib_c, cross_out, *norms, after(d_pre2, f_total, output), xhat1, memory, c_state[3], c_state[8],
             *c_state[:3], *c_state[5:8], c_state[4], c_state[9], brow, *own_c[:3], rstd1],
            [(wide, F32), *halves, *grads(4 * half), sums_shape],
            [*square_weights, *[(side, BF16)] * 2, logs, logs, *[(side, BF16)] * 2, *[(side, F32)] * 4,
             *[(side, BF16)] * 4, ((2, heads * QB, GW), F32), turned, turned, turned, block_wide,
             ((model, 8 * half), BF16)],
            22, {8: (length, False)}, {1: (length, False)}, cuts={n: cut for n in range(6, 11)},
            out_cuts={n: cut for n in range(3)}, bare=(3, 4), dealt=dealt,
        ),
        f_near,
    ))
    d_pre1, memory_grad, mem_send, c_keep, c_send, sums1 = back
    mem_other = lax.ppermute(mem_send, "tensor", swap_y)
    c_other = core_send(c_send)
    f_part = near_sum(f_near)
    c_total = total(c_keep, c_other).astype(BF16)
    c_near, f_far = near_send(c_total), far_send(f_part)
    back, c_near, f_far, mem_other = lax.optimization_barrier((
        call(
            functools.partial(self_backward, chunk=chunk_rows), sc,
            [mine_s, sib_s, self_out, after(d_pre1, c_total, f_part), inputs, s_own[3], s_rest[3], *s_own[:3],
             *s_rest[:3], s_own[4], s_rest[4], brow, sums1, sums2, sums3],
            [*[(side, BF16)] * 6, *grads(4 * half + QB)],
            [*square_weights, *[(side, BF16)] * 2, logs, logs, *[(side, F32)] * 4,
             ((2, heads * QB, GW), F32), turned, turned, ((QB, model), F32), ((model, QB), BF16),
             ((model, 2 * (4 * half + QB)), BF16)],
            16, {4: (length, False)}, cuts={n: cut for n in range(3, 7)}, bare=(6, 7), dealt=dealt,
        ),
        c_near, f_far, mem_other,
    ))
    *d_self, s_keep, s_send = back
    s_other = core_send(s_send)
    c_part = near_sum(c_near)
    c_far = far_send(c_part)
    back, c_far, s_other = lax.optimization_barrier((
        call(
            input_backward, sc, [mine_s, sib_s, *own_s[:3], residual_scale, after(d_pre1, c_part), *d_self], halves,
            square_weights, 5, None, {0: (length, False)}, cuts={n: cut for n in range(6, 13)},
            out_cuts={0: cut, 1: cut},
        ),
        c_far, s_other,
    ))
    input_grad, in_send = back
    s_near = near_send(total(s_keep, s_other).astype(BF16))
    in_other = lax.ppermute(in_send, "tensor", swap_y)
    memory_grad = fill(memory_grad, mem_other)
    f_sum, c_sum = far_sum(f_far), far_sum(c_far)
    s_sum = far_sum(far_send(near_sum(s_near)))
    input_grad = fill(input_grad, in_other)
    ffn_in_grad, ffn_out_grad = f_sum[:, :hidden], f_sum[:, hidden:].T
    c_out = [c_sum[:, n * half : (n + 1) * half] for n in range(4)]
    s_out = [s_sum[:, n * half : (n + 1) * half] for n in range(4)]
    sums = s_sum[:, 4 * half : 4 * half + 9].T
    gain_grad = jnp.stack([sums[2], sums[4], sums[6]])
    shift_grad = jnp.stack([sums[3], sums[5], sums[7]])
    scale_grad = jnp.stack([sums[0], sums[1], sums[8]])
    return (
        output, input_grad, memory_grad, s_out[0], s_out[1], s_out[2], s_out[3].T, c_out[0], c_out[1], c_out[2],
        c_out[3].T, ffn_in_grad, ffn_out_grad, gain_grad, shift_grad, scale_grad,
    )


def solution(mesh):
    rows, cols = P("dp", None), P(None, "tensor")
    both, turned = P("dp", "tensor"), P("tensor", "dp")
    return jax.shard_map(
        functools.partial(local, n_dp=mesh.shape["dp"], n_tensor=mesh.shape["tensor"]),
        mesh=mesh,
        in_specs=(
            rows, rows, rows, rows, cols, cols, cols, turned_rows(), cols, cols, cols, turned_rows(), cols,
            turned_rows(), P(), P(), P(), rows,
        ),
        out_specs=(
            rows, both, both, both, both, both, turned, both, both, both, turned, both, turned,
            P(None, "dp"), P(None, "dp"), P(None, "dp"),
        ),
        check_vma=False,
    )


def turned_rows():
    return P("tensor", None)
```

```python
import functools
import math

import jax
import jax.numpy as jnp
from jax import lax
from jax.experimental import pallas as pl
from jax.experimental.pallas import tpu as pltpu
from jax.sharding import PartitionSpec as P

HEAD_DIM = 64
QB = 128
KC = 256
GW = 256
EPS = 1e-05
NEG = -1e30
F32 = jnp.float32
BF16 = jnp.bfloat16
MB = 512
SPARE = 12 * 1024 * 1024
FULL = 56 * 1024 * 1024
SEGMENTS = 32
FLOPS_PER_US = 5e9


def nn(left, right):
    return lax.dot_general(left, right, (((1,), (0,)), ((), ())), preferred_element_type=F32)


def nt(left, right):
    return lax.dot_general(left, right, (((1,), (1,)), ((), ())), preferred_element_type=F32)


def tn(left, right):
    return lax.dot_general(left, right, (((0,), (0,)), ((), ())), preferred_element_type=F32)


def iota(shape, dim):
    return lax.broadcasted_iota(jnp.int32, shape, dim)


def normalise(pre):
    center = jnp.mean(pre, axis=-1, keepdims=True)
    centered = pre - center
    rstd = lax.rsqrt(jnp.mean(centered * centered, axis=-1, keepdims=True) + EPS)
    return centered * rstd, rstd


def norm_back(grad, gain, xhat, rstd):
    scaled = grad * gain
    first = jnp.mean(scaled, axis=-1, keepdims=True)
    second = jnp.mean(scaled * xhat, axis=-1, keepdims=True)
    return rstd * (scaled - first - xhat * second)


def rows_at(block, size):
    return pl.ds(pl.multiple_of(block * size, size), size)


def stack_heads(block):
    head = iota((1, GW), 1) // HEAD_DIM
    return jnp.concatenate(
        [block * (head == h).astype(F32).astype(BF16) for h in range(GW // HEAD_DIM)], axis=0
    )


def unstack_heads(stacked, rows):
    low_half = iota((1, 128), 1) < HEAD_DIM
    tiles = []
    for tile in range(GW // 128):
        cols = slice(tile * 128, tile * 128 + 128)
        first, second = 2 * tile, 2 * tile + 1
        tiles.append(
            jnp.where(
                low_half,
                stacked[first * rows : (first + 1) * rows, cols],
                stacked[second * rows : (second + 1) * rows, cols],
            )
        )
    return jnp.concatenate(tiles, axis=1)


def attend_units(units, s_scr, m_scr, l_scr, o_scr):
    heads = GW // HEAD_DIM
    stacks = [stack_heads(q[rows_at(i, QB), :]) for i, q, *_ in units]

    def scores(n, j):
        _, _, k, _, lo, hi, first, _ = units[n]
        start = pl.multiple_of(first + j * KC, 16)
        place = start + iota((KC, QB), 0)
        allowed = (place >= lo) & (place < hi)
        s = nt(k[pl.ds(start, KC), :], stacks[n])
        peaks = []
        for h in range(heads):
            part = slice(h * QB, (h + 1) * QB)
            masked = jnp.where(allowed, s[:, part], NEG)
            s_scr[n, j, :, part] = masked
            peaks.append(jnp.max(masked, axis=0, keepdims=True))
        return jnp.concatenate(peaks, axis=1)

    for n in range(len(units)):
        m_scr[n : n + 1, :] = scores(n, 0)
    for n, unit in enumerate(units):

        @pl.loop(1, unit[7])
        def _(j):
            m_scr[n : n + 1, :] = jnp.maximum(m_scr[n : n + 1, :], scores(n, j))

    peaks = [m_scr[n : n + 1, :] for n in range(len(units))]

    def weigh(n, j):
        p = jnp.exp(s_scr[n, j] - peaks[n])
        keys = pl.ds(pl.multiple_of(units[n][6] + j * KC, 16), KC)
        return jnp.sum(p, axis=0, keepdims=True), tn(units[n][3][keys, :], p.astype(BF16))

    for n in range(len(units)):
        l_scr[n : n + 1, :], o_scr[n] = weigh(n, 0)
    for n, unit in enumerate(units):

        @pl.loop(1, unit[7])
        def _(j):
            more_l, more_o = weigh(n, j)
            l_scr[n : n + 1, :] = l_scr[n : n + 1, :] + more_l
            o_scr[n] = o_scr[n] + more_o

    results = []
    for n in range(len(units)):
        total = l_scr[n : n + 1, :]
        log = peaks[n] + jnp.log(total)
        scale = 1.0 / total
        parts = [
            o_scr[n, h * HEAD_DIM : (h + 1) * HEAD_DIM, h * QB : (h + 1) * QB] * scale[:, h * QB : (h + 1) * QB]
            for h in range(heads)
        ]
        mixed = jnp.transpose(jnp.concatenate(parts, axis=0).astype(BF16))
        results.append((mixed, [log[:, h * QB : (h + 1) * QB] for h in range(heads)]))
    return results


def attend_back_units(units, r_scr):
    heads = GW // HEAD_DIM

    def chunk(n, j):
        i, q, k, v, do, lse, delta, lo, hi, first, _, _, dk, dv = units[n]
        rows = rows_at(i, QB)
        keys = pl.ds(pl.multiple_of(first + j * KC, 16), KC)
        qs = stack_heads(q[rows, :])
        ds = stack_heads(do[rows, :])
        kg = k[keys, :]
        place = first + j * KC + iota((KC, QB), 0)
        allowed = (place >= lo) & (place < hi)
        st = nt(kg, qs)
        dp = nt(v[keys, :], ds)
        probs, grads = [], []
        for h in range(heads):
            part = slice(h * QB, (h + 1) * QB)
            p = jnp.where(allowed, jnp.exp(st[:, part] - lse[h : h + 1, rows]), 0.0)
            probs.append(p.astype(BF16))
            grads.append((p * (dp[:, part] - delta[h : h + 1, rows])).astype(BF16))
        prob = jnp.concatenate(probs, axis=1)
        grad = jnp.concatenate(grads, axis=1)
        dv[keys, :] += nn(prob, ds)
        dk[keys, :] += nn(grad, qs)
        return tn(grad, kg)

    for n in range(len(units)):
        r_scr[n] = chunk(n, 0)
    for n, unit in enumerate(units):

        @pl.loop(1, unit[10])
        def _(j):
            r_scr[n] = r_scr[n] + chunk(n, j)

    for n, unit in enumerate(units):
        unit[11][rows_at(unit[0], QB), :] = (unstack_heads(r_scr[n], QB) * HEAD_DIM**-0.5).astype(BF16)


def set_delta(rows, do, mixed, delta_scr):
    heads = do.shape[1] // HEAD_DIM
    product = do.astype(F32) * mixed.astype(F32)
    high = product.astype(BF16)
    rest = (product - high.astype(F32)).astype(BF16)
    pick = (iota((heads, do.shape[1]), 1) // HEAD_DIM == iota((heads, do.shape[1]), 0)).astype(F32).astype(BF16)
    delta_scr[:, rows] = nt(pick, high) + nt(pick, rest)


def put_transposed(rows, block, scr, chunk):
    turned = jnp.transpose(block)
    size = turned.shape[0]
    count = size // chunk
    for n in range(count):
        first = (n % 2 * 2 + n // 2 % 2) * (size // 4) + n // 4 * chunk if chunk else 0
        scr[first : first + chunk, rows] = turned[n * chunk : (n + 1) * chunk]


def add_sum(ref, row, value):
    ref[row : row + 1, :] += jnp.sum(value, axis=0, keepdims=True)


def project(rows, left, weight, out, factor=1.0):
    out[rows, :] = (nn(left, weight[...]) * factor).astype(BF16)


def unpack_square(mine, sib, weights):
    core = core_index()
    *cols, out = weights
    part, half = cols[0].shape[0] // 2, out.shape[0]
    small = half // 2
    for place, source in ((core, mine), (1 - core, sib)):
        for n, w in enumerate(cols):
            w[rows_at(place, part), :] = source[n * part : (n + 1) * part, :]
        base = len(cols) * part
        for n in range(out.shape[1] // half):
            out[rows_at(place, small), n * half : (n + 1) * half] = source[
                base + n * small : base + (n + 1) * small, :
            ]


def unpack_ffn(mine, sib, win, wout):
    core = core_index()
    part, rows, width = win.shape[0] // 2, wout.shape[0] // 2, wout.shape[1]
    tiles = win.shape[1] // width
    for place, source in ((core, mine), (1 - core, sib)):
        for n in range(tiles):
            win[rows_at(place, part), n * width : (n + 1) * width] = source[n * part : (n + 1) * part, :]
        wout[rows_at(place, rows), :] = source[tiles * part :, :]


def core_index():
    return lax.axis_index("dp") % 2


def set_ranges(tgt, src, brow, blocks):
    rows, length = tgt.shape
    mine = lax.axis_index("tensor")

    def row(ref):
        value = ref[0:1, :]
        for n in range(1, rows):
            value = jnp.where(mine == n, ref[n : n + 1, :], value)
        return value

    target, source = row(tgt), row(src)
    ids = iota((SEGMENTS, length), 0)

    def before(ids_of, limit):
        count = jnp.sum((ids_of < limit).astype(F32), axis=1, keepdims=True)
        return jnp.sum(jnp.where(ids == target, count, 0.0), axis=0, keepdims=True).astype(jnp.int32)

    values = [
        before(target, ids), iota((1, length), 1) + 1, before(source, ids), before(source, ids + 1)
    ]
    lane = iota((1, 128), 1)
    for n, value in enumerate(values):
        brow[n : n + 1, :] = value
        brow[n + 4 : n + 5, :] = value
    blocks[...] = jnp.zeros_like(blocks)
    for n in range(2):
        first = jnp.zeros((1, 128), jnp.int32)
        last = jnp.zeros((1, 128), jnp.int32)
        for i in range(length // QB):
            low, high = values[2 * n][:, i * QB : i * QB + 1], values[2 * n + 1][:, (i + 1) * QB - 1 : (i + 1) * QB]
            first = jnp.where(lane == i, low, first)
            last = jnp.where(lane == i, high, last)
        first = lax.shift_left(lax.shift_right_logical(first, 4), 4)
        count = lax.shift_right_logical(last - first + (KC - 1), KC.bit_length() - 1)
        blocks[2 * n : 2 * n + 1, :] = jnp.minimum(first, length - count * KC)
        blocks[2 * n + 1 : 2 * n + 2, :] = count


def forward_unit(sc, brow, i, q, k, v, which):
    rows = rows_at(i, QB)
    return (
        i, q, k, v, brow[2 * which : 2 * which + 1, rows], brow[2 * which + 1 : 2 * which + 2, rows],
        sc[2 * which, i], sc[2 * which + 1, i],
    )


def put_logs(lse, i, logs):
    for h, log in enumerate(logs):
        lse[h : h + 1, rows_at(i, QB)] = log


def project_self(x, weights, outs):
    @pl.loop(0, x.chunks)
    def _(i):
        x.need(i)
        rows = rows_at(i, MB)
        block = x[rows, :]
        for weight, out, factor in zip(weights, outs, (HEAD_DIM**-0.5, 1.0, 1.0)):
            project(rows, block, weight, out, factor)
            out.put(i)


def self_forward_own(sc, qo, ko, vo, x, brow, q, k, v, mixed, lse, *scratch):
    need(qo, ko, vo)
    project_self(x, (qo, ko, vo), (q, k, v))
    need(brow)

    @pl.loop(0, x.shape[0] // QB // 2)
    def _(pair):
        pair_of = [2 * pair, 2 * pair + 1]
        units = [forward_unit(sc, brow, i, q, k, v, 0) for i in pair_of]
        for i, (block, logs) in zip(pair_of, attend_units(units, *scratch)):
            mixed[rows_at(i, QB), :] = block
            put_logs(lse, i, logs)


def norm_rows(i, pre, xhat, rstd):
    @pl.loop(0, MB // QB)
    def _(n):
        rows = rows_at(i * (MB // QB) + n, QB)
        hat, inv = normalise(pre[rows_at(n, QB), :])
        xhat[rows, :] = hat
        rstd[rows, :] = jnp.broadcast_to(inv, (QB, rstd.shape[1]))

    xhat.put(i)
    rstd.put(i)


def self_forward_rest(
    sc, mine, sib, x, brow, mixed_own, oo, omega,
    q, k, v, mixed, lse, xhat, rstd, qx, kx, vx, ox, pre, *scratch,
):
    need(mine, sib)
    unpack_square(mine, sib, (qx, kx, vx, ox))
    project_self(x, (qx, kx, vx), (q, k, v))
    need(brow)

    @pl.loop(0, x.shape[0] // QB // 2)
    def _(pair):
        pair_of = [2 * pair, 2 * pair + 1]
        units = [forward_unit(sc, brow, i, q, k, v, 0) for i in pair_of]
        for i, (block, logs) in zip(pair_of, attend_units(units, *scratch)):
            mixed[rows_at(i, QB), :] = block
            put_logs(lse, i, logs)

    need(mixed_own, oo, omega)

    @pl.loop(0, x.chunks)
    def _(i):
        rows = rows_at(i, MB)
        branch = nn(mixed_own[rows, :], oo[...]) + nn(mixed[rows, :], ox[...])
        pre[...] = omega[0:1] * x[rows, :].astype(F32) + branch
        norm_rows(i, pre, xhat, rstd)


def cross_forward(
    sc, mine, sib, qo, ko, vo, gain, shift, xhat1, mem, brow, oo, omega,
    q, k, v, mixed, lse, q_x, k_x, v_x, mixed_x, lse_x, xhat, rstd, qx, kx, vx, ox, pre, *scratch,
):
    need(mine, sib, qo, ko, vo, gain, shift)
    unpack_square(mine, sib, (qx, kx, vx, ox))

    @pl.loop(0, mem.chunks)
    def _(i):
        rows = rows_at(i, MB)
        xhat1.need(i)
        mem.need(i)
        low1 = (xhat1[rows, :] * gain[0:1] + shift[0:1]).astype(BF16)
        block = mem[rows, :]
        for weights, outs in (((qo, ko, vo), (q, k, v)), ((qx, kx, vx), (q_x, k_x, v_x))):
            project(rows, low1, weights[0], outs[0], HEAD_DIM**-0.5)
            project(rows, block, weights[1], outs[1])
            project(rows, block, weights[2], outs[2])
            for result in outs:
                result.put(i)

    need(brow)

    @pl.loop(0, mem.shape[0] // QB)
    def _(i):
        units = [forward_unit(sc, brow, i, *group, 1) for group in ((q, k, v), (q_x, k_x, v_x))]
        for (block, logs), out, lse_out in zip(attend_units(units, *scratch), (mixed, mixed_x), (lse, lse_x)):
            out[rows_at(i, QB), :] = block
            put_logs(lse_out, i, logs)

    need(oo, omega)

    @pl.loop(0, mem.chunks)
    def _(i):
        rows = rows_at(i, MB)
        branch = nn(mixed[rows, :], oo[...]) + nn(mixed_x[rows, :], ox[...])
        pre[...] = omega[1:2] * (xhat1[rows, :] * gain[0:1] + shift[0:1]) + branch
        norm_rows(i, pre, xhat, rstd)


def ffn_forward(
    sc, io, oo, gain, shift, omega, xhat2, mine, sib, cot,
    out, out_all, slope, d_pre3, keep, send, sums, act, ix, ox, pre, grad_t, grads, *, chunk,
):
    need(io, oo, gain, shift, omega, mine, sib)
    unpack_ffn(mine, sib, ix, ox)
    sums[...] = jnp.zeros_like(sums)
    width = 512
    half = io.shape[1]

    @pl.loop(0, xhat2.chunks)
    def _(i):
        rows = rows_at(i, MB)
        xhat2.need(i)
        cot.need(i)
        norm2 = xhat2[rows, :] * gain[1:2] + shift[1:2]
        low2 = norm2.astype(BF16)
        pre[...] = omega[2:3] * norm2
        for side, (win, wout) in enumerate(((io, oo), (ix, ox))):
            for first in range(0, half, width):
                u = nn(low2, win[:, first : first + width])
                square = u * u
                t = jnp.tanh(u * (0.7978845608028654 + (0.7978845608028654 * 0.044715) * square))
                h = 0.5 + 0.5 * t
                a = u * h
                place = slice(side * half + first, side * half + first + width)
                act[rows, place] = a.astype(BF16)
                steep = 2 * 0.7978845608028654 + (6 * 0.7978845608028654 * 0.044715) * square
                slope[rows, place] = (h + a * (1.0 - h) * steep).astype(BF16)
            pre[...] += nn(act[rows, side * half : (side + 1) * half], wout[...])
        slope.put(i)

        @pl.loop(0, MB // QB)
        def _(n):
            small = rows_at(i * (MB // QB) + n, QB)
            hat, inv = normalise(pre[rows_at(n, QB), :])
            result = (hat * gain[2:3] + shift[2:3]).astype(BF16)
            out[small, :] = result
            out_all[small, :] = result
            grad = cot[small, :].astype(F32)
            d_pre = norm_back(grad, gain[2:3], hat, inv)
            d_pre3[small, :] = d_pre
            put_transposed(small, d_pre.astype(BF16), grad_t, chunk)
            add_sum(sums, 0, grad * hat)
            add_sum(sums, 1, grad)
            add_sum(sums, 2, d_pre * (xhat2[small, :] * gain[1:2] + shift[1:2]))

        for result in (out, out_all, d_pre3):
            result.put(i)

    for first in range(0, 2 * half, width):
        grads[:, first : first + width] = nn(grad_t[...], act[:, first : first + width]).astype(BF16)
    put_grads(grads, keep, send)


def put_grads(scr, keep, send):
    dp = lax.axis_index("dp")
    core, x = (dp % 2, dp // 2 % 2) if keep.dealt else (0, 0)
    size, width = scr.shape[0] // 4, keep.shape[1]
    parts = keep.shape[0] // size
    for out, row in ((keep, core), (send, 1 - core)):
        for n in range(parts):
            side = n * 2 // parts
            first = n % 2 * width if parts == 4 else 0
            place = row * 2 + (x if side == 0 else 1 - x)
            out.copy_part(scr.at[rows_at(place, size), first : first + width], n * size)


def ffn_backward(
    sc, oo, io, gain, shift, omega, d_pre3, slope, xhat2, mine, sib, rstd2,
    d_pre2, keep, send, sums, up_scr, norm_t, ix, ox, acc, grads, *, chunk,
):
    need(io, oo, gain, shift, omega, mine, sib)
    unpack_ffn(mine, sib, ix, ox)
    sums[...] = jnp.zeros_like(sums)
    half = io.shape[1]
    width = 512

    @pl.loop(0, xhat2.chunks)
    def _(i):
        rows = rows_at(i, MB)
        for argument in (d_pre3, slope, xhat2):
            argument.need(i)
        grad = d_pre3[rows, :]
        low = grad.astype(BF16)
        acc[...] = omega[2:3] * grad
        for side, (win, wout) in enumerate(((io, oo), (ix, ox))):
            for first in range(0, half, width):
                place = slice(side * half + first, side * half + first + width)
                up_scr[rows, place] = (
                    slope[rows, place].astype(F32) * nt(low, wout[first : first + width, :])
                ).astype(BF16)
            acc[...] += nt(up_scr[rows, side * half : (side + 1) * half], win[...])

        rstd2.need(i)

        @pl.loop(0, MB // QB)
        def _(n):
            small = rows_at(i * (MB // QB) + n, QB)
            total = acc[rows_at(n, QB), :]
            hat = xhat2[small, :]
            put_transposed(small, (hat * gain[1:2] + shift[1:2]).astype(BF16), norm_t, chunk)
            d_pre2[small, :] = norm_back(total, gain[1:2], hat, rstd2[small, 0:1])
            add_sum(sums, 0, total * hat)
            add_sum(sums, 1, total)

        d_pre2.put(i)

    for first in range(0, 2 * half, width):
        grads[:, first : first + width] = nn(norm_t[...], up_scr[:, first : first + width]).astype(BF16)
    put_grads(grads, keep, send)


def weight_grads(pairs, grads):
    width = grads.shape[1] // 2
    for n, (left, *rights) in enumerate(pairs):
        for side, right in enumerate(rights):
            half = right.shape[1]
            first = side * width + n * half
            grads[:, first : first + half] = nn(left[...], right[...]).astype(BF16)


def backward_unit(sc, brow, i, which, q, k, v, do, lse, delta, dq, dk, dv):
    rows = rows_at(i, QB)
    return (
        i, q, k, v, do, lse, delta, brow[2 * which : 2 * which + 1, rows], brow[2 * which + 1 : 2 * which + 2, rows],
        sc[2 * which, i], sc[2 * which + 1, i], dq, dk, dv,
    )


def attention_grads(low, rows, outs):
    for out, weight, was, total in outs:
        value = nt(low, weight[...]).astype(BF16)
        out[rows, :] = value
        set_delta(rows, value, was[rows, :], total)


def cross_backward(
    sc, mine, sib, oo, gain, shift, omega, d_pre2, xhat1, mem, mixed, mixed_x, q, k, v, q_x, k_x, v_x, lse, lse_x,
    brow, qo, ko, vo, rstd1,
    d_pre1, mem_all, mem_send, keep, send, sums,
    qx, kx, vx, ox, do, do_x, delta, delta_x, dq, dq_x, dk, dk_x, dv, dv_x, dkb, dkb_x, dvb, dvb_x, r_scr,
    grad_t, norm_t, mem_t, acc, grads, *, chunk,
):
    need(mine, sib, oo, gain, shift, omega)
    unpack_square(mine, sib, (qx, kx, vx, ox))
    sums[...] = jnp.zeros_like(sums)
    half = qo.shape[1]
    blocks = mem.shape[0] // QB
    for ref in (dk, dk_x, dv, dv_x):
        ref[...] = jnp.zeros_like(ref)

    @pl.loop(0, mem.chunks)
    def _(i):
        rows = rows_at(i, MB)
        for argument in (d_pre2, xhat1, mem, mixed, mixed_x):
            argument.need(i)
        grad = d_pre2[rows, :]
        low = grad.astype(BF16)
        norm1 = xhat1[rows, :] * gain[0:1] + shift[0:1]
        put_transposed(rows, low, grad_t, chunk)
        put_transposed(rows, norm1.astype(BF16), norm_t, chunk)
        put_transposed(rows, mem[rows, :], mem_t, chunk)
        attention_grads(low, rows, ((do, oo, mixed, delta), (do_x, ox, mixed_x, delta_x)))
        add_sum(sums, 0, grad * norm1)

    need(q, k, v, q_x, k_x, v_x, lse, lse_x, brow)

    @pl.loop(0, blocks)
    def _(i):
        attend_back_units(
            [
                backward_unit(sc, brow, i, 1, q, k, v, do, lse, delta, dq, dk, dv),
                backward_unit(sc, brow, i, 1, q_x, k_x, v_x, do_x, lse_x, delta_x, dq_x, dk_x, dv_x),
            ],
            r_scr,
        )

    need(qo, ko, vo, rstd1)
    tensor = lax.axis_index("tensor")

    @pl.loop(0, mem.chunks)
    def _(i):
        rows = rows_at(i, MB)
        acc[...] = omega[1:2] * d_pre2[rows, :] + nt(dq[rows, :], qo[...]) + nt(dq_x[rows, :], qx[...])
        for low, wide in ((dkb, dk), (dkb_x, dk_x), (dvb, dv), (dvb_x, dv_x)):
            low[rows, :] = wide[rows, :].astype(BF16)

        def part(side):
            which = rows_at(side, half)
            return (
                nt(dkb[rows, :], ko[which, :]) + nt(dkb_x[rows, :], kx[which, :])
                + nt(dvb[rows, :], vo[which, :]) + nt(dvb_x[rows, :], vx[which, :])
            )

        mem_all[rows, :] = part(tensor)
        mem_send[rows, :] = part(1 - tensor).astype(BF16)

        @pl.loop(0, MB // QB)
        def _(n):
            small = rows_at(i * (MB // QB) + n, QB)
            total = acc[rows_at(n, QB), :]
            hat = xhat1[small, :]
            d_pre1[small, :] = norm_back(total, gain[0:1], hat, rstd1[small, 0:1])
            add_sum(sums, 1, total * hat)
            add_sum(sums, 2, total)

        for result in (d_pre1, mem_all, mem_send):
            result.put(i)

    weight_grads(
        ((norm_t, dq, dq_x), (mem_t, dkb, dkb_x), (mem_t, dvb, dvb_x), (grad_t, mixed, mixed_x)), grads
    )
    put_grads(grads, keep, send)


def self_backward(
    sc, mine, sib, oo, d_pre1, x, mixed, mixed_x, q, k, v, q_x, k_x, v_x, lse, lse_x, brow, sums1, sums2, sums3, out_other,
    dq, dq_x, dkb, dkb_x, dvb, dvb_x, keep, send, out_all,
    qx, kx, vx, ox, do, do_x, delta, delta_x, dk, dk_x, dv, dv_x, r_scr, grad_t, in_t, sums, all_sums, sums_t, grads, *, chunk,
):
    need(mine, sib, oo)
    unpack_square(mine, sib, (qx, kx, vx, ox))
    blocks = x.shape[0] // QB
    for ref in (sums, all_sums, dk, dk_x, dv, dv_x):
        ref[...] = jnp.zeros_like(ref)

    @pl.loop(0, x.chunks)
    def _(i):
        rows = rows_at(i, MB)
        for argument in (d_pre1, x, mixed, mixed_x):
            argument.need(i)
        grad = d_pre1[rows, :]
        low = grad.astype(BF16)
        block = x[rows, :]
        put_transposed(rows, low, grad_t, chunk)
        put_transposed(rows, block, in_t, chunk)
        attention_grads(low, rows, ((do, oo, mixed, delta), (do_x, ox, mixed_x, delta_x)))
        add_sum(sums, 0, grad * block.astype(F32))

    need(q, k, v, q_x, k_x, v_x, lse, lse_x, brow, sums1, sums2, sums3, out_other)
    out_all.copy_from(out_other.ref)

    @pl.loop(0, blocks)
    def _(i):
        attend_back_units(
            [
                backward_unit(sc, brow, i, 0, q, k, v, do, lse, delta, dq, dk, dv),
                backward_unit(sc, brow, i, 0, q_x, k_x, v_x, do_x, lse_x, delta_x, dq_x, dk_x, dv_x),
            ],
            r_scr,
        )

    for low, wide in ((dkb, dk), (dkb_x, dk_x), (dvb, dv), (dvb_x, dv_x)):
        low[...] = wide[...].astype(BF16)
    for row, source in enumerate(
        (sums1[1:2, :], sums2[0:1, :], sums3[0:1, :], sums1[2:3, :], sums2[1:2, :], sums3[1:2, :], sums[0:1, :],
         sums1[0:1, :], sums3[2:3, :])
    ):
        all_sums[row : row + 1, :] = source
    put_transposed(pl.ds(0, QB), all_sums[...].astype(BF16), sums_t, chunk)
    weight_grads(((in_t, dq, dq_x), (in_t, dkb, dkb_x), (in_t, dvb, dvb_x), (grad_t, mixed, mixed_x)), grads)
    width = grads.shape[1] // 2
    for side in range(2):
        grads[:, (side + 1) * width - QB : (side + 1) * width] = sums_t[...]
    put_grads(grads, keep, send)


def input_backward(
    sc, mine, sib, qo, ko, vo, omega, d_pre1, dq, dq_x, dk, dk_x, dv, dv_x, mem_other, in_all, in_send, mem_all,
    qx, kx, vx, ox,
):
    need(mine, sib, qo, ko, vo, omega)
    unpack_square(mine, sib, (qx, kx, vx, ox))
    half = qo.shape[1]
    tensor = lax.axis_index("tensor")

    @pl.loop(0, d_pre1.chunks)
    def _(i):
        rows = rows_at(i, MB)
        for argument in (d_pre1, dq, dq_x, dk, dk_x, dv, dv_x):
            argument.need(i)

        def part(side):
            which = rows_at(side, half)
            total = omega[0:1, which] * d_pre1[rows, which]
            for grad, weight in ((dq, qo), (dq_x, qx), (dk, ko), (dk_x, kx), (dv, vo), (dv_x, vx)):
                total = total + nt(grad[rows, :], weight[which, :])
            return total

        in_all[rows, :] = part(tensor)
        in_send[rows, :] = part(1 - tensor).astype(BF16)
        in_all.put(i)
        in_send.put(i)

    need(mem_other)
    mem_all[...] = mem_other[...].astype(F32)


def fill_kernel(sc, other, out):
    @pl.loop(0, other.chunks)
    def _(i):
        other.need(i)
        rows = rows_at(i, other.shape[0] // other.chunks)
        out[rows, :] = other[rows, :].astype(out.dtype)
        out.put(i)


def finish(
    sc, other, own_f, own_c, late, s0, s1, s2, s3,
    whole, sq, sk, sv, so, cq, ck, cv, co, win, wout, gain, shift, omega,
):
    @pl.loop(0, other.chunks)
    def _(i):
        other.need(i)
        rows = rows_at(i, other.shape[0] // other.chunks)
        whole[rows, :] = other[rows, :].astype(F32)
        whole.put(i)

    need(own_f, own_c, late, s0, s1, s2, s3)
    half, hidden = sq.shape[1], win.shape[1]

    def late_sum(own, first, base, width):
        return own[:, first : first + width].astype(F32) + late[:, base + first : base + first + width].astype(F32)

    wout[...] = late_sum(own_f, 0, 0, hidden)
    win[...] = late_sum(own_f, hidden, 0, hidden)
    for n, out in enumerate((cq, ck, cv, co)):
        out[...] = late_sum(own_c, n * half, 2 * hidden, half)

    def soon_sum(first, width):
        cols = slice(first, first + width)
        return (s0[:, cols].astype(F32) + s1[:, cols].astype(F32)) + (s2[:, cols].astype(F32) + s3[:, cols].astype(F32))

    for n, out in enumerate((sq, sk, sv, so)):
        out[...] = soon_sum(n * half, half)
    sums = jnp.transpose(soon_sum(4 * half, QB))
    for n, out in enumerate((gain, shift, omega)):
        out[...] = sums[3 * n : 3 * n + 3]


class Buffer:
    def __init__(self, ref, far, sems, chunks):
        self.ref, self.far, self.sems, self.chunks = ref, far, sems, chunks
        self.shape, self.dtype = far.shape, far.dtype

    def __getitem__(self, index):
        return self.ref[index]

    def __setitem__(self, index, value):
        self.ref[index] = value

    def chunk(self, i):
        size = self.shape[0] // self.chunks
        if self.chunks == 1:
            return self.ref, self.far
        rows = rows_at(i, size)
        return self.ref.at[rows], self.far.at[rows]

    def load(self):
        for i in range(self.chunks):
            near, far = self.chunk(i)
            pltpu.make_async_copy(far, near, self.sems.at[i]).start()

    def need(self, i):
        near, far = self.chunk(i)
        pltpu.make_async_copy(far, near, self.sems.at[i]).wait()

    def put(self, i=0):
        near, far = self.chunk(i)
        pltpu.make_async_copy(near, far, self.sems.at[0]).start()

    def copy_part(self, near, first):
        far = self.far.at[first : first + near.shape[0]]
        pltpu.make_async_copy(near, far, self.sems.at[0]).start()

    def copy_from(self, near):
        pltpu.make_async_copy(near, self.far, self.sems.at[0]).start()

    def done(self):
        pltpu.make_async_copy(self.far, self.far, self.sems.at[0]).wait()


def need(*buffers):
    for buffer in buffers:
        for i in range(buffer.chunks):
            buffer.need(i)


def call(
    body, sc, args, outs, scratch, us, picks=None, puts=None, alias=None, cuts=None, out_cuts=None, bare=(), dealt=True,
    full=False,
):
    picks, puts, cuts, out_cuts = picks or {}, puts or {}, cuts or {}, out_cuts or {}

    def block(ref, pick):
        if pick is None:
            return ref
        rows, other = pick
        place = lax.axis_index("tensor")
        return ref.at[rows_at(1 - place if other else place, rows)]

    def size(shape, pick):
        return shape if pick is None else (pick[0], *shape[1:])

    alias = alias or {}
    loads = [n for n in range(len(args)) if n not in alias]
    buffers = [
        *[(size(args[n].shape, picks.get(n)), args[n].dtype) for n in loads],
        *[(size(shape, puts.get(n)), kind) for n, (shape, kind) in enumerate(outs) if n not in bare],
        *scratch,
    ]
    room = sum(math.prod(shape[:-1]) * max(shape[-1], 128) * jnp.dtype(kind).itemsize for shape, kind in buffers)

    def kernel(sc, *refs):
        refs = list(refs)
        ins = [refs.pop(0) for _ in args]
        far_outs = [refs.pop(0) for _ in outs]
        near_ins = [refs.pop(0) for _ in loads]
        near_outs = [None if n in bare else refs.pop(0) for n in range(len(outs))]
        in_sems = [refs.pop(0) for _ in loads]
        out_sems = [refs.pop(0) for _ in outs]
        arguments = [
            Buffer(near, block(ins[n], picks.get(n)), sems, cuts.get(n, 1))
            for n, near, sems in zip(loads, near_ins, in_sems)
        ]
        results = [
            Buffer(near, block(far, puts.get(n)), sems, out_cuts.get(n, 1))
            for n, (far, near, sems) in enumerate(zip(far_outs, near_outs, out_sems))
        ]
        for result in results:
            result.dealt = dealt
        for argument in arguments:
            argument.load()
        body(sc, *arguments, *results, *refs)
        for n, result in enumerate(results):
            if n not in out_cuts and n not in bare:
                result.put()
        for result in results:
            result.done()

    return pl.pallas_call(
        kernel,
        out_shape=[jax.ShapeDtypeStruct(shape, kind) for shape, kind in outs],
        grid_spec=pltpu.PrefetchScalarGridSpec(
            num_scalar_prefetch=1,
            grid=(1,),
            in_specs=[pl.BlockSpec(memory_space=pl.ANY)] * len(args),
            out_specs=[pl.BlockSpec(memory_space=pl.ANY)] * len(outs),
            scratch_shapes=[
                *[pltpu.VMEM(shape, kind) for shape, kind in buffers[: len(buffers) - len(scratch)]],
                *[pltpu.SemaphoreType.DMA((cuts.get(n, 1),)) for n in loads],
                *[pltpu.SemaphoreType.DMA((1,)) for _ in outs],
                *[pltpu.VMEM(shape, kind) for shape, kind in scratch],
            ],
        ),
        input_output_aliases={n + 1: out for n, out in alias.items()},
        cost_estimate=pl.CostEstimate(flops=int(us * FLOPS_PER_US), bytes_accessed=1024, transcendentals=0),
        compiler_params=pltpu.CompilerParams(vmem_limit_bytes=FULL if full else room + SPARE),
        name=(body.func if isinstance(body, functools.partial) else body).__name__,
    )(sc, *args)


def pack(weights, outs, moves, segments=None):
    extra = [] if segments is None else list(segments)
    length = extra[0].shape[1] if extra else 0
    ranges = [((8, length), jnp.int32), ((8, 128), jnp.int32)] if extra else []

    def pack_weights(*refs):
        refs = list(refs)
        sources = [refs.pop(0) for _ in weights]
        ids = [refs.pop(0) for _ in extra]
        targets = [refs.pop(0) for _ in outs]
        sem = refs.pop()
        core = core_index()
        copies = []
        for n, (which, rows, first, out, start) in enumerate(moves):
            width = outs[out][0][1]
            copies.append(
                pltpu.make_async_copy(
                    sources[which].at[rows_at(core, rows), first : first + width],
                    targets[out].at[start : start + rows, :],
                    sem.at[n],
                )
            )
        for copy in copies:
            copy.start()
        if ids:
            set_ranges(*ids, *refs)
        for copy in copies:
            copy.wait()

    near = pl.BlockSpec(memory_space=pltpu.VMEM)
    return pl.pallas_call(
        pack_weights,
        out_shape=[jax.ShapeDtypeStruct(shape, kind) for shape, kind in outs + ranges],
        in_specs=[pl.BlockSpec(memory_space=pltpu.HBM)] * len(weights) + [near] * len(extra),
        out_specs=[near] * len(outs + ranges),
        scratch_shapes=[pltpu.SemaphoreType.DMA((len(moves),))],
        cost_estimate=pl.CostEstimate(flops=int(FLOPS_PER_US), bytes_accessed=1024, transcendentals=0),
        compiler_params=pltpu.CompilerParams(vmem_limit_bytes=60 * 1024 * 1024),
        name="pack_weights",
    )(*weights, *extra)


def local(
    inputs, memory, tgt_seg, src_seg, self_query, self_key, self_value, self_out,
    cross_query, cross_key, cross_value, cross_out, ffn_in, ffn_out,
    norm_gain, norm_shift, residual_scale, cotangent, *, n_dp, n_tensor,
):
    d = lax.axis_index("dp")
    t = lax.axis_index("tensor")
    length = tgt_seg.shape[1]
    model = inputs.shape[1]
    half = model // n_tensor
    hidden = ffn_in.shape[1]
    blocks = length // QB
    chunk = model // n_dp
    dealt = chunk % 16 == 0 and n_dp & (n_dp - 1) == 0
    swap_y = [(0, 1), (1, 0)]

    def swap(n_bit):
        return [(i, i ^ n_bit) for i in range(n_dp)]

    def after(value, *others):
        return lax.optimization_barrier((value, others))[0]

    own_s = [self_query, self_key, self_value, self_out]
    own_c = [cross_query, cross_key, cross_value, cross_out]
    own_f = [ffn_in, ffn_out]
    square = ((4 * half, half), BF16)

    def square_moves(base, out):
        part = model // 2
        moves = [(base + n, part, 0, out, n * part) for n in range(3)]
        return moves + [(base + 3, half // 2, n * half, out, 3 * part + n * half // 2) for n in range(n_tensor)]

    (pack_s,) = pack(own_s, [square], square_moves(0, 0))
    tiles = hidden // model
    pack_c, pack_f, brow, sc = pack(
        own_c + own_f, [square, ((tiles * half + hidden // 2, model), BF16)],
        square_moves(0, 0)
        + [(4, model // 2, n * model, 1, n * model // 2) for n in range(tiles)]
        + [(5, hidden // 2, 0, 1, tiles * model // 2)],
        (tgt_seg, src_seg),
    )
    mine_s = lax.ppermute(pack_s, "tensor", swap_y)

    def fill(whole, other):
        (result,) = call(
            fill_kernel, sc, [whole, other], [(whole.shape, whole.dtype)], [], 1, None, {0: (length, True)}, {0: 0},
            cuts={1: 4}, out_cuts={0: 4},
        )
        return result

    def total(*parts):
        result = parts[0].astype(F32)
        for part in parts[1:]:
            result = result + part.astype(F32)
        return result

    size = model // 4

    def part_total(n, *arrays):
        return total(*[array[n * size : (n + 1) * size] for array in arrays]).astype(BF16)

    def z_send(part):
        far = n_dp // 4
        row = d // 4
        part = part.reshape(far, chunk, -1)
        parts = [lax.dynamic_index_in_dim(part, row, 0, keepdims=False)]
        for step in range(1, far):
            perm = [(i, i % 4 + (i // 4 + step) % far * 4) for i in range(n_dp)]
            out = lax.dynamic_index_in_dim(part, (row + step) % far, 0, keepdims=False)
            parts.append(lax.ppermute(out, "dp", perm))
        return parts

    def reduce_any(keep, send):
        grad = lax.psum_scatter(jnp.concatenate([keep, send]).astype(F32), "dp", scatter_dimension=0, tiled=True)
        width = grad.shape[1] // 2
        return grad[:, :width] + lax.ppermute(grad[:, width:], "tensor", swap_y)

    wide, side = (length, model), (length, half)
    heads = GW // HEAD_DIM
    group = [(side, BF16)] * 4 + [((half // HEAD_DIM, length), F32)]
    square_weights = [((model, half), BF16)] * 3 + [((half, model), BF16)]
    stats = [(wide, F32), ((length, 128), F32)]
    attend_scratch = [
        ((2, length // KC, KC, heads * QB), F32),
        ((2, heads * QB), F32),
        ((2, heads * QB), F32),
        ((2, GW, heads * QB), F32),
    ]
    block_wide = ((MB, model), F32)
    cut = length // MB
    norms = [norm_gain, norm_shift, residual_scale]
    s_own = call(
        self_forward_own, sc, [*own_s[:3], inputs, brow], group, attend_scratch, 7, {3: (length, False)},
        cuts={3: cut}, out_cuts={0: cut, 1: cut, 2: cut},
    )
    s_own, mine_s = lax.optimization_barrier((s_own, mine_s))
    sib_s = lax.ppermute(mine_s, "dp", swap(1))
    mine_c = lax.ppermute(after(pack_c, mine_s), "tensor", swap_y)
    s_rest_stats = call(
        self_forward_rest, sc, [mine_s, sib_s, inputs, brow, s_own[3], self_out, residual_scale], group + stats,
        [*square_weights, block_wide, *attend_scratch], 8, {2: (length, False)},
        cuts={2: cut}, out_cuts={n: cut for n in (0, 1, 2, 5, 6)},
    )
    s_rest_stats, mine_c = lax.optimization_barrier((s_rest_stats, mine_c))
    *s_rest, xhat1, rstd1 = s_rest_stats
    sib_c = lax.ppermute(mine_c, "dp", swap(1))
    mine_f = lax.ppermute(after(pack_f, mine_c), "tensor", swap_y)
    c_stats = call(
        cross_forward, sc,
        [mine_c, sib_c, *own_c[:3], norm_gain, norm_shift, xhat1, memory, brow, cross_out, residual_scale],
        group + group + stats,
        [*square_weights, block_wide, *attend_scratch], 14, {8: (length, False)}, cuts={7: cut, 8: cut},
        out_cuts={n: cut for n in (0, 1, 2, 5, 6, 7, 10, 11)},
    )
    c_stats, mine_f = lax.optimization_barrier((c_stats, mine_f))
    *c_state, xhat2, rstd2 = c_stats
    sib_f = lax.ppermute(mine_f, "dp", swap(1))
    sums_shape = ((8, model), F32)
    low_wide = ((length, n_tensor * hidden), BF16)
    f_weights = [((model, hidden), BF16), ((hidden, model), BF16)]
    def grads(width, parts=2):
        return [((parts * size, 4 * width // parts), BF16)] * 2

    def core_swap(send):
        return lax.ppermute(send, "dp", swap(1)) if dealt else send

    turned = ((model, length), BF16)
    chunk_rows = chunk if dealt else model // 4
    out_row, output, slope, d_pre3, f1_keep, f1_send, sums3 = call(
        functools.partial(ffn_forward, chunk=chunk_rows), sc, [*own_f, *norms, xhat2, mine_f, sib_f, cotangent],
        [(wide, BF16), ((n_tensor * length, model), BF16), low_wide, (wide, F32), *grads(hidden), sums_shape],
        [low_wide, *f_weights, block_wide, turned, ((model, 2 * hidden), BF16)], 16,
        {8: (length, False)}, {1: (length, False)}, cuts={5: cut, 8: cut}, out_cuts={n: cut for n in range(4)},
        bare=(4, 5), dealt=dealt,
    )
    out_other = lax.ppermute(out_row, "tensor", swap_y)
    f1_other = core_swap(f1_send)
    back, f1_other = lax.optimization_barrier((
        call(
            functools.partial(ffn_backward, chunk=chunk_rows), sc,
            [ffn_out, ffn_in, *norms, d_pre3, slope, xhat2, mine_f, sib_f, rstd2],
            [(wide, F32), *grads(hidden), sums_shape],
            [low_wide, turned, *f_weights, block_wide, ((model, 2 * hidden), BF16)], 12,
            cuts={n: cut for n in (5, 6, 7, 10)}, out_cuts={0: cut}, bare=(1, 2), dealt=dealt,
        ),
        f1_other,
    ))
    d_pre2, f2_keep, f2_send, sums2 = back
    f2_other = core_swap(f2_send)
    if dealt:
        f_there = jnp.concatenate([part_total(1, f1_keep, f1_other), part_total(1, f2_keep, f2_other)], axis=1)
        d_pre2 = after(d_pre2, f_there)
        f_x = lax.ppermute(f_there, "dp", swap(2))
    else:
        f_x = sums2
    logs = ((half // HEAD_DIM, length), F32)
    halves = [((n_tensor * length, half), F32), (side, BF16)]
    back, f_x, out_other = lax.optimization_barrier((
        call(
            functools.partial(cross_backward, chunk=chunk_rows), sc,
            [mine_c, sib_c, cross_out, *norms, d_pre2, xhat1, memory, c_state[3], c_state[8],
             *c_state[:3], *c_state[5:8], c_state[4], c_state[9], brow, *own_c[:3], rstd1],
            [(wide, F32), *halves, *grads(4 * half), sums_shape],
            [*square_weights, *[(side, BF16)] * 2, logs, logs, *[(side, BF16)] * 2, *[(side, F32)] * 4,
             *[(side, BF16)] * 4, ((2, heads * QB, GW), F32), turned, turned, turned, block_wide,
             ((model, 8 * half), BF16)],
            23, {8: (length, False)}, {1: (length, False)}, cuts={n: cut for n in range(6, 11)},
            out_cuts={n: cut for n in range(3)}, bare=(3, 4), dealt=dealt,
        ),
        f_x, out_other,
    ))
    d_pre1, memory_grad, mem_send, c_keep, c_send, sums1 = back
    mem_other = lax.ppermute(mem_send, "tensor", swap_y)
    c_other = core_swap(c_send)
    c_x, f_z = sums1, sums1
    if dealt:
        f_part = jnp.concatenate(
            [
                part_total(
                    0, keep[:, first : first + hidden], other[:, first : first + hidden],
                    f_x[:, base + first : base + first + hidden],
                )
                for first in (0, hidden)
                for keep, other, base in ((f1_keep, f1_other, 0), (f2_keep, f2_other, 2 * hidden))
            ],
            axis=1,
        )
        f_z = z_send(f_part)
        c_there = part_total(1, c_keep, c_other)
        c_x = lax.ppermute(c_there, "dp", swap(2))
        d_pre1 = after(d_pre1, c_there, f_part)
    back, c_x, mem_other = lax.optimization_barrier((
        call(
            functools.partial(self_backward, chunk=chunk_rows), sc,
            [mine_s, sib_s, self_out, d_pre1, inputs, s_own[3], s_rest[3], *s_own[:3],
             *s_rest[:3], s_own[4], s_rest[4], brow, sums1, sums2, sums3, out_other, output],
            [*[(side, BF16)] * 6, *grads(4 * half + QB, 4 if dealt else 2), (output.shape, BF16)],
            [*square_weights, *[(side, BF16)] * 2, logs, logs, *[(side, F32)] * 4,
             ((2, heads * QB, GW), F32), turned, turned, ((8, model), F32), ((QB, model), F32), ((model, QB), BF16),
             ((model, 2 * (4 * half + QB)), BF16)],
            16, {4: (length, False)}, {8: (length, True)}, {20: 8}, cuts={n: cut for n in range(3, 7)},
            bare=(6, 7, 8), dealt=dealt,
        ),
        c_x, mem_other,
    ))
    *d_self, s_keep, s_send, output = back
    s_other = core_swap(s_send)
    if dealt:
        across = [(i * 2 + j, (i ^ 2) * 2 + 1 - j) for i in range(n_dp) for j in range(2)]
        s_near = [part_total(n, s_keep, s_other) for n in range(1, 4)]
        f_last = total(*f_z).astype(BF16)
        d_self[0] = after(d_self[0], *s_near, f_last)
        s_near = [
            lax.ppermute(s_near[0], "tensor", swap_y), lax.ppermute(s_near[1], "dp", swap(2)),
            lax.ppermute(s_near[2], ("dp", "tensor"), across),
        ]
        c_part = part_total(0, c_keep, c_other, c_x)
    input_grad, in_send, memory_grad = call(
        input_backward, sc,
        [mine_s, sib_s, *own_s[:3], residual_scale, d_pre1, *d_self, mem_other, memory_grad],
        [*halves, (memory_grad.shape, F32)], square_weights, 5, None, {0: (length, False), 2: (length, True)},
        {14: 2}, cuts={n: cut for n in range(6, 13)}, out_cuts={0: cut, 1: cut},
    )
    thin, broad = ((chunk, half), F32), ((chunk, hidden), F32)
    three = ((3, chunk), F32)
    if dealt:
        in_send, s_near, c_part = lax.optimization_barrier((in_send, s_near, c_part))
        in_other = lax.ppermute(in_send, "tensor", swap_y)
        c_z = z_send(c_part)
        s_far = z_send(part_total(0, s_keep, s_other, *s_near))
        c_last = total(*c_z).astype(BF16)
        late = lax.ppermute(
            jnp.concatenate([f_last[:, 2 * hidden :], c_last[:, 4 * half :]], axis=1), "tensor", swap_y
        )
        while len(s_far) < 4:
            s_far.append(jnp.zeros_like(s_far[0]))
        s_far = [*s_far[:3], s_far[3] if len(s_far) == 4 else total(*s_far[3:]).astype(BF16)]
        (
            input_grad, sq, sk, sv, so, cq, ck, cv, co, ffn_in_grad, ffn_out_grad, gain_grad, shift_grad, scale_grad
        ) = call(
            finish, sc, [in_other, f_last, c_last, late, *s_far, input_grad],
            [(input_grad.shape, F32), *[thin] * 8, broad, broad, three, three, three],
            [], 2, None, {0: (length, True)}, {8: 0}, cuts={0: 4}, out_cuts={0: 4},
        )
    else:
        input_grad = fill(input_grad, lax.ppermute(in_send, "tensor", swap_y))
        f1_sum, f2_sum = reduce_any(f1_keep, f1_send), reduce_any(f2_keep, f2_send)
        c_sum, s_sum = reduce_any(c_keep, c_send), reduce_any(s_keep, s_send)
        ffn_in_grad, ffn_out_grad = f2_sum, f1_sum
        cq, ck, cv, co = [c_sum[:, n * half : (n + 1) * half] for n in range(4)]
        sq, sk, sv, so = [s_sum[:, n * half : (n + 1) * half] for n in range(4)]
        gain_grad, shift_grad, scale_grad = [s_sum[:, 4 * half + 3 * n : 4 * half + 3 * n + 3].T for n in range(3)]
    return (
        output, input_grad, memory_grad, sq, sk, sv, so.T, cq, ck, cv, co.T, ffn_in_grad, ffn_out_grad.T,
        gain_grad, shift_grad, scale_grad,
    )


def solution(mesh):
    rows, cols = P("dp", None), P(None, "tensor")
    both, turned = P("dp", "tensor"), P("tensor", "dp")
    return jax.shard_map(
        functools.partial(local, n_dp=mesh.shape["dp"], n_tensor=mesh.shape["tensor"]),
        mesh=mesh,
        in_specs=(
            rows, rows, rows, rows, cols, cols, cols, turned_rows(), cols, cols, cols, turned_rows(), cols,
            turned_rows(), P(), P(), P(), rows,
        ),
        out_specs=(
            rows, both, both, both, both, both, turned, both, both, both, turned, both, turned,
            P(None, "dp"), P(None, "dp"), P(None, "dp"),
        ),
        check_vma=False,
    )


def turned_rows():
    return P("tensor", None)
```

```python
import functools
import math

import jax
import jax.numpy as jnp
from jax import lax
from jax.experimental import pallas as pl
from jax.experimental.pallas import tpu as pltpu
from jax.sharding import PartitionSpec as P

HEAD_DIM = 64
QB = 128
KC = 256
XC = 128
GW = 256
EPS = 1e-05
NEG = -1e30
F32 = jnp.float32
BF16 = jnp.bfloat16
MB = 512
SPARE = 12 * 1024 * 1024
FULL = 56 * 1024 * 1024
SEGMENTS = 32
FLOPS_PER_US = 5e9


def nn(left, right):
    return lax.dot_general(left, right, (((1,), (0,)), ((), ())), preferred_element_type=F32)


def nt(left, right):
    return lax.dot_general(left, right, (((1,), (1,)), ((), ())), preferred_element_type=F32)


def tn(left, right):
    return lax.dot_general(left, right, (((0,), (0,)), ((), ())), preferred_element_type=F32)


def iota(shape, dim):
    return lax.broadcasted_iota(jnp.int32, shape, dim)


def normalise(pre):
    center = jnp.mean(pre, axis=-1, keepdims=True)
    centered = pre - center
    rstd = lax.rsqrt(jnp.mean(centered * centered, axis=-1, keepdims=True) + EPS)
    return centered * rstd, rstd


def norm_back(grad, gain, xhat, rstd):
    scaled = grad * gain
    first = jnp.mean(scaled, axis=-1, keepdims=True)
    second = jnp.mean(scaled * xhat, axis=-1, keepdims=True)
    return rstd * (scaled - first - xhat * second)


def rows_at(block, size):
    return pl.ds(pl.multiple_of(block * size, size), size)


def stack_heads(block):
    head = iota((1, GW), 1) // HEAD_DIM
    return jnp.concatenate(
        [block * (head == h).astype(F32).astype(BF16) for h in range(GW // HEAD_DIM)], axis=0
    )


def unstack_heads(stacked, rows):
    low_half = iota((1, 128), 1) < HEAD_DIM
    tiles = []
    for tile in range(GW // 128):
        cols = slice(tile * 128, tile * 128 + 128)
        first, second = 2 * tile, 2 * tile + 1
        tiles.append(
            jnp.where(
                low_half,
                stacked[first * rows : (first + 1) * rows, cols],
                stacked[second * rows : (second + 1) * rows, cols],
            )
        )
    return jnp.concatenate(tiles, axis=1)


def each_more(units, where, body):
    if all(unit[where] is units[0][where] for unit in units):

        @pl.loop(1, units[0][where])
        def _(j):
            for n in range(len(units)):
                body(n, j)

    else:
        for n, unit in enumerate(units):

            @pl.loop(1, unit[where])
            def _(j):
                body(n, j)


def chunk_keys(first, j):
    if isinstance(j, int):
        return pl.ds(pl.multiple_of(first, 16), KC)
    return pl.ds(pl.multiple_of(first + (KC - XC) + j * XC, 16), XC)


def attend_units(units, s_scr, m_scr, l_scr, o_scr):
    heads = GW // HEAD_DIM
    stacks = [stack_heads(q[rows_at(i, QB), :]) for i, q, *_ in units]

    def scores(n, j):
        _, _, k, _, lo, hi, first, _ = units[n]
        keys, place = chunk_keys(first, j), chunk_keys(0, j)
        at = keys.start + iota((keys.size, QB), 0)
        allowed = (at >= lo) & (at < hi)
        s = nt(k[keys, :], stacks[n])
        peaks = []
        for h in range(heads):
            part = slice(h * QB, (h + 1) * QB)
            masked = jnp.where(allowed, s[:, part], NEG)
            s_scr[n, place, part] = masked
            peaks.append(jnp.max(masked, axis=0, keepdims=True))
        return jnp.concatenate(peaks, axis=1)

    for n in range(len(units)):
        m_scr[n : n + 1, :] = scores(n, 0)

    def more_scores(n, j):
        m_scr[n : n + 1, :] = jnp.maximum(m_scr[n : n + 1, :], scores(n, j))

    each_more(units, 7, more_scores)
    peaks = [m_scr[n : n + 1, :] for n in range(len(units))]

    def weigh(n, j):
        p = jnp.exp(s_scr[n, chunk_keys(0, j), :] - peaks[n])
        return jnp.sum(p, axis=0, keepdims=True), tn(units[n][3][chunk_keys(units[n][6], j), :], p.astype(BF16))

    for n in range(len(units)):
        l_scr[n : n + 1, :], o_scr[n] = weigh(n, 0)

    def more_weights(n, j):
        more_l, more_o = weigh(n, j)
        l_scr[n : n + 1, :] = l_scr[n : n + 1, :] + more_l
        o_scr[n] = o_scr[n] + more_o

    each_more(units, 7, more_weights)
    results = []
    for n in range(len(units)):
        total = l_scr[n : n + 1, :]
        log = peaks[n] + jnp.log(total)
        scale = 1.0 / total
        parts = [
            o_scr[n, h * HEAD_DIM : (h + 1) * HEAD_DIM, h * QB : (h + 1) * QB] * scale[:, h * QB : (h + 1) * QB]
            for h in range(heads)
        ]
        mixed = jnp.transpose(jnp.concatenate(parts, axis=0).astype(BF16))
        results.append((mixed, [log[:, h * QB : (h + 1) * QB] for h in range(heads)]))
    return results


def attend_back_units(units, r_scr):
    heads = GW // HEAD_DIM

    def chunk(n, j):
        i, q, k, v, do, lse, delta, lo, hi, first, _, _, dk, dv = units[n]
        rows = rows_at(i, QB)
        keys = chunk_keys(first, j)
        qs = stack_heads(q[rows, :])
        ds = stack_heads(do[rows, :])
        kg = k[keys, :]
        at = keys.start + iota((keys.size, QB), 0)
        allowed = (at >= lo) & (at < hi)
        st = nt(kg, qs)
        dp = nt(v[keys, :], ds)
        probs, grads = [], []
        for h in range(heads):
            part = slice(h * QB, (h + 1) * QB)
            p = jnp.where(allowed, jnp.exp(st[:, part] - lse[h : h + 1, rows]), 0.0)
            probs.append(p.astype(BF16))
            grads.append((p * (dp[:, part] - delta[h : h + 1, rows])).astype(BF16))
        prob = jnp.concatenate(probs, axis=1)
        grad = jnp.concatenate(grads, axis=1)
        dv[keys, :] += nn(prob, ds)
        dk[keys, :] += nn(grad, qs)
        return tn(grad, kg)

    for n in range(len(units)):
        r_scr[n] = chunk(n, 0)

    def more(n, j):
        r_scr[n] = r_scr[n] + chunk(n, j)

    each_more(units, 10, more)
    for n, unit in enumerate(units):
        unit[11][rows_at(unit[0], QB), :] = (unstack_heads(r_scr[n], QB) * HEAD_DIM**-0.5).astype(BF16)


def set_delta(rows, do, mixed, delta_scr):
    heads = do.shape[1] // HEAD_DIM
    product = do.astype(F32) * mixed.astype(F32)
    high = product.astype(BF16)
    rest = (product - high.astype(F32)).astype(BF16)
    pick = (iota((heads, do.shape[1]), 1) // HEAD_DIM == iota((heads, do.shape[1]), 0)).astype(F32).astype(BF16)
    delta_scr[:, rows] = nt(pick, high) + nt(pick, rest)


def put_transposed(rows, block, scr, chunk):
    turned = jnp.transpose(block)
    size = turned.shape[0]
    count = size // chunk
    for n in range(count):
        first = (n % 2 * 2 + n // 2 % 2) * (size // 4) + n // 4 * chunk if chunk else 0
        scr[first : first + chunk, rows] = turned[n * chunk : (n + 1) * chunk]


def add_sum(ref, row, value):
    ref[row : row + 1, :] += jnp.sum(value, axis=0, keepdims=True)


def project(rows, left, weight, out, factor=1.0):
    out[rows, :] = (nn(left, weight[...]) * factor).astype(BF16)


def unpack_square(mine, sib, weights):
    core = core_index()
    *cols, out = weights
    part, half = cols[0].shape[0] // 2, out.shape[0]
    small = half // 2
    for place, source in ((core, mine), (1 - core, sib)):
        for n, w in enumerate(cols):
            w[rows_at(place, part), :] = source[n * part : (n + 1) * part, :]
        base = len(cols) * part
        for n in range(out.shape[1] // half):
            out[rows_at(place, small), n * half : (n + 1) * half] = source[
                base + n * small : base + (n + 1) * small, :
            ]


def unpack_ffn(mine, sib, win, wout):
    core = core_index()
    part, rows, width = win.shape[0] // 2, wout.shape[0] // 2, wout.shape[1]
    tiles = win.shape[1] // width
    for place, source in ((core, mine), (1 - core, sib)):
        for n in range(tiles):
            win[rows_at(place, part), n * width : (n + 1) * width] = source[n * part : (n + 1) * part, :]
        wout[rows_at(place, rows), :] = source[tiles * part :, :]


def core_index():
    return lax.axis_index("dp") % 2


def set_ranges(tgt, src, brow, blocks):
    rows, length = tgt.shape
    mine = lax.axis_index("tensor")

    def row(ref):
        value = ref[0:1, :]
        for n in range(1, rows):
            value = jnp.where(mine == n, ref[n : n + 1, :], value)
        return value

    target, source = row(tgt), row(src)
    ids = iota((SEGMENTS, length), 0)

    def before(ids_of, limit):
        count = jnp.sum((ids_of < limit).astype(F32), axis=1, keepdims=True)
        return jnp.sum(jnp.where(ids == target, count, 0.0), axis=0, keepdims=True).astype(jnp.int32)

    values = [
        before(target, ids), iota((1, length), 1) + 1, before(source, ids), before(source, ids + 1)
    ]
    lane = iota((1, 128), 1)
    for n, value in enumerate(values):
        brow[n : n + 1, :] = value
        brow[n + 4 : n + 5, :] = value
    blocks[...] = jnp.zeros_like(blocks)
    for n in range(2):
        first = jnp.zeros((1, 128), jnp.int32)
        last = jnp.zeros((1, 128), jnp.int32)
        for i in range(length // QB):
            low, high = values[2 * n][:, i * QB : i * QB + 1], values[2 * n + 1][:, (i + 1) * QB - 1 : (i + 1) * QB]
            first = jnp.where(lane == i, low, first)
            last = jnp.where(lane == i, high, last)
        first = lax.shift_left(lax.shift_right_logical(first, 4), 4)
        more = lax.shift_right_logical(jnp.maximum(last - first - KC, 0) + (XC - 1), XC.bit_length() - 1)
        blocks[2 * n : 2 * n + 1, :] = jnp.minimum(first, length - KC - more * XC)
        blocks[2 * n + 1 : 2 * n + 2, :] = more + 1


def forward_units(sc, brow, i, which, groups):
    rows = rows_at(i, QB)
    first, count = sc[2 * which, i], sc[2 * which + 1, i]
    lo, hi = brow[2 * which : 2 * which + 1, rows], brow[2 * which + 1 : 2 * which + 2, rows]
    return [(i, q, k, v, lo, hi, first, count) for q, k, v in groups]


def put_logs(lse, i, logs):
    for h, log in enumerate(logs):
        lse[h : h + 1, rows_at(i, QB)] = log


def project_self(x, weights, outs):
    @pl.loop(0, x.chunks)
    def _(i):
        x.need(i)
        rows = rows_at(i, MB)
        block = x[rows, :]
        for weight, out, factor in zip(weights, outs, (HEAD_DIM**-0.5, 1.0, 1.0)):
            project(rows, block, weight, out, factor)
            out.put(i)


def self_forward_own(sc, qo, ko, vo, x, brow, q, k, v, mixed, lse, *scratch):
    need(qo, ko, vo)
    project_self(x, (qo, ko, vo), (q, k, v))
    need(brow)

    @pl.loop(0, x.shape[0] // QB // 2)
    def _(pair):
        pair_of = [2 * pair, 2 * pair + 1]
        units = [forward_units(sc, brow, i, 0, [(q, k, v)])[0] for i in pair_of]
        for i, (block, logs) in zip(pair_of, attend_units(units, *scratch)):
            mixed[rows_at(i, QB), :] = block
            put_logs(lse, i, logs)


def norm_rows(i, pre, xhat, rstd):
    @pl.loop(0, MB // QB)
    def _(n):
        rows = rows_at(i * (MB // QB) + n, QB)
        hat, inv = normalise(pre[rows_at(n, QB), :])
        xhat[rows, :] = hat
        rstd[rows, :] = jnp.broadcast_to(inv, (QB, rstd.shape[1]))

    xhat.put(i)
    rstd.put(i)


def self_forward_rest(
    sc, mine, sib, x, brow, mixed_own, oo, omega,
    q, k, v, mixed, lse, xhat, rstd, qx, kx, vx, ox, pre, *scratch,
):
    need(mine, sib)
    unpack_square(mine, sib, (qx, kx, vx, ox))
    project_self(x, (qx, kx, vx), (q, k, v))
    need(brow)

    @pl.loop(0, x.shape[0] // QB // 2)
    def _(pair):
        pair_of = [2 * pair, 2 * pair + 1]
        units = [forward_units(sc, brow, i, 0, [(q, k, v)])[0] for i in pair_of]
        for i, (block, logs) in zip(pair_of, attend_units(units, *scratch)):
            mixed[rows_at(i, QB), :] = block
            put_logs(lse, i, logs)

    need(mixed_own, oo, omega)

    @pl.loop(0, x.chunks)
    def _(i):
        rows = rows_at(i, MB)
        branch = nn(mixed_own[rows, :], oo[...]) + nn(mixed[rows, :], ox[...])
        pre[...] = omega[0:1] * x[rows, :].astype(F32) + branch
        norm_rows(i, pre, xhat, rstd)


def cross_forward(
    sc, mine, sib, qo, ko, vo, gain, shift, xhat1, mem, brow, oo, omega,
    q, k, v, mixed, lse, q_x, k_x, v_x, mixed_x, lse_x, xhat, rstd, qx, kx, vx, ox, pre, *scratch,
):
    need(mine, sib, qo, ko, vo, gain, shift)
    unpack_square(mine, sib, (qx, kx, vx, ox))

    @pl.loop(0, mem.chunks)
    def _(i):
        rows = rows_at(i, MB)
        xhat1.need(i)
        mem.need(i)
        low1 = (xhat1[rows, :] * gain[0:1] + shift[0:1]).astype(BF16)
        block = mem[rows, :]
        for weights, outs in (((qo, ko, vo), (q, k, v)), ((qx, kx, vx), (q_x, k_x, v_x))):
            project(rows, low1, weights[0], outs[0], HEAD_DIM**-0.5)
            project(rows, block, weights[1], outs[1])
            project(rows, block, weights[2], outs[2])
            for result in outs:
                result.put(i)

    need(brow)

    @pl.loop(0, mem.shape[0] // QB)
    def _(i):
        units = forward_units(sc, brow, i, 1, ((q, k, v), (q_x, k_x, v_x)))
        for (block, logs), out, lse_out in zip(attend_units(units, *scratch), (mixed, mixed_x), (lse, lse_x)):
            out[rows_at(i, QB), :] = block
            put_logs(lse_out, i, logs)

    need(oo, omega)

    @pl.loop(0, mem.chunks)
    def _(i):
        rows = rows_at(i, MB)
        branch = nn(mixed[rows, :], oo[...]) + nn(mixed_x[rows, :], ox[...])
        pre[...] = omega[1:2] * (xhat1[rows, :] * gain[0:1] + shift[0:1]) + branch
        norm_rows(i, pre, xhat, rstd)


def hidden_units(rows, low2, win, act, slope, width=512):
    for first in range(0, win.shape[1], width):
        place = slice(first, first + width)
        u = nn(low2, win[:, place])
        square = u * u
        t = jnp.tanh(u * (0.7978845608028654 + (0.7978845608028654 * 0.044715) * square))
        h = 0.5 + 0.5 * t
        a = u * h
        act[rows, place] = a.astype(BF16)
        steep = 2 * 0.7978845608028654 + (6 * 0.7978845608028654 * 0.044715) * square
        slope[rows, place] = (h + a * (1.0 - h) * steep).astype(BF16)


def ffn_forward_own(sc, io, gain, shift, xhat2, oo, omega, act, slope, pre):
    need(io, gain, shift)

    @pl.loop(0, xhat2.chunks)
    def _(i):
        rows = rows_at(i, MB)
        xhat2.need(i)
        norm2 = xhat2[rows, :] * gain[1:2] + shift[1:2]
        hidden_units(rows, norm2.astype(BF16), io, act, slope)
        act.put(i)
        slope.put(i)

    need(oo, omega)

    @pl.loop(0, xhat2.chunks)
    def _(i):
        rows = rows_at(i, MB)
        norm2 = xhat2[rows, :] * gain[1:2] + shift[1:2]
        pre[rows, :] = omega[2:3] * norm2 + nn(act[rows, :], oo[...])
        pre.put(i)


def ffn_forward_rest(
    sc, mine, sib, gain, shift, xhat2, pre, cot, act_own,
    out, out_all, slope, d_pre3, keep, send, sums, act, ix, ox, grad_t, grads, *, chunk,
):
    need(mine, sib, gain, shift)
    unpack_ffn(mine, sib, ix, ox)
    sums[...] = jnp.zeros_like(sums)
    width = 512
    half = ix.shape[1]

    @pl.loop(0, xhat2.chunks)
    def _(i):
        rows = rows_at(i, MB)
        xhat2.need(i)
        hidden_units(rows, (xhat2[rows, :] * gain[1:2] + shift[1:2]).astype(BF16), ix, act, slope)
        slope.put(i)
        pre.need(i)
        cot.need(i)
        pre[rows, :] += nn(act[rows, :], ox[...])

        @pl.loop(0, MB // QB)
        def _(n):
            small = rows_at(i * (MB // QB) + n, QB)
            hat, inv = normalise(pre[small, :])
            result = (hat * gain[2:3] + shift[2:3]).astype(BF16)
            out[small, :] = result
            out_all[small, :] = result
            grad = cot[small, :].astype(F32)
            d_pre = norm_back(grad, gain[2:3], hat, inv)
            d_pre3[small, :] = d_pre
            put_transposed(small, d_pre.astype(BF16), grad_t, chunk)
            add_sum(sums, 0, grad * hat)
            add_sum(sums, 1, grad)
            add_sum(sums, 2, d_pre * (xhat2[small, :] * gain[1:2] + shift[1:2]))

        for result in (out, out_all, d_pre3):
            result.put(i)

    need(act_own)
    for side, right in enumerate((act_own, act)):
        for first in range(0, half, width):
            grads[:, side * half + first : side * half + first + width] = nn(
                grad_t[...], right[:, first : first + width]
            ).astype(BF16)
    put_grads(grads, keep, send)


def put_grads(scr, keep, send):
    dp = lax.axis_index("dp")
    core, x = (dp % 2, dp // 2 % 2) if keep.dealt else (0, 0)
    size, width = scr.shape[0] // 4, keep.shape[1]
    parts = keep.shape[0] // size
    for out, row in ((keep, core), (send, 1 - core)):
        for n in range(parts):
            side = n * 2 // parts
            first = n % 2 * width if parts == 4 else 0
            place = row * 2 + (x if side == 0 else 1 - x)
            out.copy_part(scr.at[rows_at(place, size), first : first + width], n * size)


def ffn_backward(
    sc, oo, io, gain, shift, omega, d_pre3, slope_own, xhat2, slope_rest, mine, sib, rstd2,
    d_pre2, keep, send, sums, up_scr, norm_t, ix, ox, acc, grads, *, chunk,
):
    need(io, oo, gain, shift, omega, mine, sib)
    unpack_ffn(mine, sib, ix, ox)
    sums[...] = jnp.zeros_like(sums)
    half = io.shape[1]
    width = 512

    @pl.loop(0, xhat2.chunks)
    def _(i):
        rows = rows_at(i, MB)
        for argument in (d_pre3, slope_own, xhat2, slope_rest):
            argument.need(i)
        grad = d_pre3[rows, :]
        low = grad.astype(BF16)
        acc[...] = omega[2:3] * grad
        for side, (win, wout, slope) in enumerate(((io, oo, slope_own), (ix, ox, slope_rest))):
            for first in range(0, half, width):
                place = slice(side * half + first, side * half + first + width)
                up_scr[rows, place] = (
                    slope[rows, first : first + width].astype(F32) * nt(low, wout[first : first + width, :])
                ).astype(BF16)
            acc[...] += nt(up_scr[rows, side * half : (side + 1) * half], win[...])

        rstd2.need(i)

        @pl.loop(0, MB // QB)
        def _(n):
            small = rows_at(i * (MB // QB) + n, QB)
            total = acc[rows_at(n, QB), :]
            hat = xhat2[small, :]
            put_transposed(small, (hat * gain[1:2] + shift[1:2]).astype(BF16), norm_t, chunk)
            d_pre2[small, :] = norm_back(total, gain[1:2], hat, rstd2[small, 0:1])
            add_sum(sums, 0, total * hat)
            add_sum(sums, 1, total)

        d_pre2.put(i)

    for first in range(0, 2 * half, width):
        grads[:, first : first + width] = nn(norm_t[...], up_scr[:, first : first + width]).astype(BF16)
    put_grads(grads, keep, send)


def weight_grads(pairs, grads):
    width = grads.shape[1] // 2
    for n, (left, *rights) in enumerate(pairs):
        for side, right in enumerate(rights):
            half = right.shape[1]
            first = side * width + n * half
            grads[:, first : first + half] = nn(left[...], right[...]).astype(BF16)


def backward_units(sc, brow, i, which, groups):
    rows = rows_at(i, QB)
    first, count = sc[2 * which, i], sc[2 * which + 1, i]
    lo, hi = brow[2 * which : 2 * which + 1, rows], brow[2 * which + 1 : 2 * which + 2, rows]
    return [(i, *group[:6], lo, hi, first, count, *group[6:]) for group in groups]


def attention_grads(low, rows, outs):
    for out, weight, was, total in outs:
        value = nt(low, weight[...]).astype(BF16)
        out[rows, :] = value
        set_delta(rows, value, was[rows, :], total)


def cross_backward(
    sc, mine, sib, oo, gain, shift, omega, d_pre2, xhat1, mem, mixed, mixed_x, q, k, v, q_x, k_x, v_x, lse, lse_x,
    brow, qo, ko, vo, rstd1,
    d_pre1, mem_all, mem_send, keep, send, sums,
    qx, kx, vx, ox, do, do_x, delta, delta_x, dq, dq_x, dk, dk_x, dv, dv_x, dkb, dkb_x, dvb, dvb_x, r_scr,
    grad_t, norm_t, mem_t, acc, grads, *, chunk,
):
    need(mine, sib, oo, gain, shift, omega)
    unpack_square(mine, sib, (qx, kx, vx, ox))
    sums[...] = jnp.zeros_like(sums)
    half = qo.shape[1]
    blocks = mem.shape[0] // QB
    for ref in (dk, dk_x, dv, dv_x):
        ref[...] = jnp.zeros_like(ref)

    @pl.loop(0, mem.chunks)
    def _(i):
        rows = rows_at(i, MB)
        for argument in (d_pre2, xhat1, mem, mixed, mixed_x):
            argument.need(i)
        grad = d_pre2[rows, :]
        low = grad.astype(BF16)
        norm1 = xhat1[rows, :] * gain[0:1] + shift[0:1]
        put_transposed(rows, low, grad_t, chunk)
        put_transposed(rows, norm1.astype(BF16), norm_t, chunk)
        put_transposed(rows, mem[rows, :], mem_t, chunk)
        attention_grads(low, rows, ((do, oo, mixed, delta), (do_x, ox, mixed_x, delta_x)))
        add_sum(sums, 0, grad * norm1)

    need(q, k, v, q_x, k_x, v_x, lse, lse_x, brow)

    @pl.loop(0, blocks)
    def _(i):
        groups = (
            (q, k, v, do, lse, delta, dq, dk, dv), (q_x, k_x, v_x, do_x, lse_x, delta_x, dq_x, dk_x, dv_x)
        )
        attend_back_units(backward_units(sc, brow, i, 1, groups), r_scr)

    need(qo, ko, vo, rstd1)
    tensor = lax.axis_index("tensor")

    @pl.loop(0, mem.chunks)
    def _(i):
        rows = rows_at(i, MB)
        acc[...] = omega[1:2] * d_pre2[rows, :] + nt(dq[rows, :], qo[...]) + nt(dq_x[rows, :], qx[...])
        for low, wide in ((dkb, dk), (dkb_x, dk_x), (dvb, dv), (dvb_x, dv_x)):
            low[rows, :] = wide[rows, :].astype(BF16)

        def part(side):
            which = rows_at(side, half)
            return (
                nt(dkb[rows, :], ko[which, :]) + nt(dkb_x[rows, :], kx[which, :])
                + nt(dvb[rows, :], vo[which, :]) + nt(dvb_x[rows, :], vx[which, :])
            )

        mem_all[rows, :] = part(tensor)
        mem_send[rows, :] = part(1 - tensor).astype(BF16)

        @pl.loop(0, MB // QB)
        def _(n):
            small = rows_at(i * (MB // QB) + n, QB)
            total = acc[rows_at(n, QB), :]
            hat = xhat1[small, :]
            d_pre1[small, :] = norm_back(total, gain[0:1], hat, rstd1[small, 0:1])
            add_sum(sums, 1, total * hat)
            add_sum(sums, 2, total)

        for result in (d_pre1, mem_all, mem_send):
            result.put(i)

    weight_grads(
        ((norm_t, dq, dq_x), (mem_t, dkb, dkb_x), (mem_t, dvb, dvb_x), (grad_t, mixed, mixed_x)), grads
    )
    put_grads(grads, keep, send)


def self_backward(
    sc, mine, sib, oo, d_pre1, x, mixed, mixed_x, q, k, v, q_x, k_x, v_x, lse, lse_x, brow, sums1, sums2, sums3, out_other,
    dq, dq_x, dkb, dkb_x, dvb, dvb_x, keep, send, out_all,
    qx, kx, vx, ox, do, do_x, delta, delta_x, dk, dk_x, dv, dv_x, r_scr, grad_t, in_t, sums, all_sums, sums_t, grads, *, chunk,
):
    need(mine, sib, oo)
    unpack_square(mine, sib, (qx, kx, vx, ox))
    blocks = x.shape[0] // QB
    for ref in (sums, all_sums, dk, dk_x, dv, dv_x):
        ref[...] = jnp.zeros_like(ref)

    @pl.loop(0, x.chunks)
    def _(i):
        rows = rows_at(i, MB)
        for argument in (d_pre1, x, mixed, mixed_x):
            argument.need(i)
        grad = d_pre1[rows, :]
        low = grad.astype(BF16)
        block = x[rows, :]
        put_transposed(rows, low, grad_t, chunk)
        put_transposed(rows, block, in_t, chunk)
        attention_grads(low, rows, ((do, oo, mixed, delta), (do_x, ox, mixed_x, delta_x)))
        add_sum(sums, 0, grad * block.astype(F32))

    need(q, k, v, q_x, k_x, v_x, lse, lse_x, brow, sums1, sums2, sums3, out_other)
    out_all.copy_from(out_other.ref)

    @pl.loop(0, blocks)
    def _(i):
        groups = (
            (q, k, v, do, lse, delta, dq, dk, dv), (q_x, k_x, v_x, do_x, lse_x, delta_x, dq_x, dk_x, dv_x)
        )
        attend_back_units(backward_units(sc, brow, i, 0, groups), r_scr)

    for low, wide in ((dkb, dk), (dkb_x, dk_x), (dvb, dv), (dvb_x, dv_x)):
        low[...] = wide[...].astype(BF16)
    for row, source in enumerate(
        (sums1[1:2, :], sums2[0:1, :], sums3[0:1, :], sums1[2:3, :], sums2[1:2, :], sums3[1:2, :], sums[0:1, :],
         sums1[0:1, :], sums3[2:3, :])
    ):
        all_sums[row : row + 1, :] = source
    put_transposed(pl.ds(0, QB), all_sums[...].astype(BF16), sums_t, chunk)
    weight_grads(((in_t, dq, dq_x), (in_t, dkb, dkb_x), (in_t, dvb, dvb_x), (grad_t, mixed, mixed_x)), grads)
    width = grads.shape[1] // 2
    for side in range(2):
        grads[:, (side + 1) * width - QB : (side + 1) * width] = sums_t[...]
    put_grads(grads, keep, send)


def input_backward(
    sc, mine, sib, qo, ko, vo, omega, d_pre1, dq, dq_x, dk, dk_x, dv, dv_x, mem_other, in_all, in_send, mem_all,
    qx, kx, vx, ox,
):
    need(mine, sib, qo, ko, vo, omega)
    unpack_square(mine, sib, (qx, kx, vx, ox))
    half = qo.shape[1]
    tensor = lax.axis_index("tensor")

    @pl.loop(0, d_pre1.chunks)
    def _(i):
        rows = rows_at(i, MB)
        for argument in (d_pre1, dq, dq_x, dk, dk_x, dv, dv_x):
            argument.need(i)

        def part(side):
            which = rows_at(side, half)
            total = omega[0:1, which] * d_pre1[rows, which]
            for grad, weight in ((dq, qo), (dq_x, qx), (dk, ko), (dk_x, kx), (dv, vo), (dv_x, vx)):
                total = total + nt(grad[rows, :], weight[which, :])
            return total

        in_all[rows, :] = part(tensor)
        in_send[rows, :] = part(1 - tensor).astype(BF16)
        in_all.put(i)
        in_send.put(i)

    need(mem_other)
    mem_all[...] = mem_other[...].astype(F32)


def fill_kernel(sc, other, out):
    @pl.loop(0, other.chunks)
    def _(i):
        other.need(i)
        rows = rows_at(i, other.shape[0] // other.chunks)
        out[rows, :] = other[rows, :].astype(out.dtype)
        out.put(i)


def finish(
    sc, own_f, own_c, late, s0, s1, s2, s3, sq, sk, sv, so, cq, ck, cv, co, win, wout, gain, shift, omega
):
    need(own_f, own_c, late, s0, s1, s2, s3)
    half, hidden = sq.shape[1], win.shape[1]

    def late_sum(own, first, base, width):
        return own[:, first : first + width].astype(F32) + late[:, base + first : base + first + width].astype(F32)

    wout[...] = late_sum(own_f, 0, 0, hidden)
    win[...] = late_sum(own_f, hidden, 0, hidden)
    for n, out in enumerate((cq, ck, cv, co)):
        out[...] = late_sum(own_c, n * half, 2 * hidden, half)

    def soon_sum(first, width):
        cols = slice(first, first + width)
        return (s0[:, cols].astype(F32) + s1[:, cols].astype(F32)) + (s2[:, cols].astype(F32) + s3[:, cols].astype(F32))

    for n, out in enumerate((sq, sk, sv, so)):
        out[...] = soon_sum(n * half, half)
    sums = jnp.transpose(soon_sum(4 * half, QB))
    for n, out in enumerate((gain, shift, omega)):
        out[...] = sums[3 * n : 3 * n + 3]


class Buffer:
    def __init__(self, ref, far, sems, chunks):
        self.ref, self.far, self.sems, self.chunks = ref, far, sems, chunks
        self.shape, self.dtype = far.shape, far.dtype

    def __getitem__(self, index):
        return self.ref[index]

    def __setitem__(self, index, value):
        self.ref[index] = value

    def chunk(self, i):
        size = self.shape[0] // self.chunks
        if self.chunks == 1:
            return self.ref, self.far
        rows = rows_at(i, size)
        return self.ref.at[rows], self.far.at[rows]

    def load(self):
        for i in range(self.chunks):
            near, far = self.chunk(i)
            pltpu.make_async_copy(far, near, self.sems.at[i]).start()

    def need(self, i):
        near, far = self.chunk(i)
        pltpu.make_async_copy(far, near, self.sems.at[i]).wait()

    def put(self, i=0):
        near, far = self.chunk(i)
        pltpu.make_async_copy(near, far, self.sems.at[0]).start()

    def copy_part(self, near, first):
        far = self.far.at[first : first + near.shape[0]]
        pltpu.make_async_copy(near, far, self.sems.at[0]).start()

    def copy_from(self, near):
        pltpu.make_async_copy(near, self.far, self.sems.at[0]).start()

    def done(self):
        pltpu.make_async_copy(self.far, self.far, self.sems.at[0]).wait()


def need(*buffers):
    for buffer in buffers:
        for i in range(buffer.chunks):
            buffer.need(i)


def call(
    body, sc, args, outs, scratch, us, picks=None, puts=None, alias=None, cuts=None, out_cuts=None, bare=(), dealt=True,
    full=False,
):
    picks, puts, cuts, out_cuts = picks or {}, puts or {}, cuts or {}, out_cuts or {}

    def block(ref, pick):
        if pick is None:
            return ref
        rows, other = pick
        place = lax.axis_index("tensor")
        return ref.at[rows_at(1 - place if other else place, rows)]

    def size(shape, pick):
        return shape if pick is None else (pick[0], *shape[1:])

    alias = alias or {}
    loads = [n for n in range(len(args)) if n not in alias]
    buffers = [
        *[(size(args[n].shape, picks.get(n)), args[n].dtype) for n in loads],
        *[(size(shape, puts.get(n)), kind) for n, (shape, kind) in enumerate(outs) if n not in bare],
        *scratch,
    ]
    room = sum(math.prod(shape[:-1]) * max(shape[-1], 128) * jnp.dtype(kind).itemsize for shape, kind in buffers)

    def kernel(sc, *refs):
        refs = list(refs)
        ins = [refs.pop(0) for _ in args]
        far_outs = [refs.pop(0) for _ in outs]
        near_ins = [refs.pop(0) for _ in loads]
        near_outs = [None if n in bare else refs.pop(0) for n in range(len(outs))]
        in_sems = [refs.pop(0) for _ in loads]
        out_sems = [refs.pop(0) for _ in outs]
        arguments = [
            Buffer(near, block(ins[n], picks.get(n)), sems, cuts.get(n, 1))
            for n, near, sems in zip(loads, near_ins, in_sems)
        ]
        results = [
            Buffer(near, block(far, puts.get(n)), sems, out_cuts.get(n, 1))
            for n, (far, near, sems) in enumerate(zip(far_outs, near_outs, out_sems))
        ]
        for result in results:
            result.dealt = dealt
        for argument in arguments:
            argument.load()
        body(sc, *arguments, *results, *refs)
        for n, result in enumerate(results):
            if n not in out_cuts and n not in bare:
                result.put()
        for result in results:
            result.done()

    return pl.pallas_call(
        kernel,
        out_shape=[jax.ShapeDtypeStruct(shape, kind) for shape, kind in outs],
        grid_spec=pltpu.PrefetchScalarGridSpec(
            num_scalar_prefetch=1,
            grid=(1,),
            in_specs=[pl.BlockSpec(memory_space=pl.ANY)] * len(args),
            out_specs=[pl.BlockSpec(memory_space=pl.ANY)] * len(outs),
            scratch_shapes=[
                *[pltpu.VMEM(shape, kind) for shape, kind in buffers[: len(buffers) - len(scratch)]],
                *[pltpu.SemaphoreType.DMA((cuts.get(n, 1),)) for n in loads],
                *[pltpu.SemaphoreType.DMA((1,)) for _ in outs],
                *[pltpu.VMEM(shape, kind) for shape, kind in scratch],
            ],
        ),
        input_output_aliases={n + 1: out for n, out in alias.items()},
        cost_estimate=pl.CostEstimate(flops=int(us * FLOPS_PER_US), bytes_accessed=1024, transcendentals=0),
        compiler_params=pltpu.CompilerParams(vmem_limit_bytes=FULL if full else room + SPARE),
        name=(body.func if isinstance(body, functools.partial) else body).__name__,
    )(sc, *args)


def pack(weights, outs, moves, segments=None):
    extra = [] if segments is None else list(segments)
    length = extra[0].shape[1] if extra else 0
    ranges = [((8, length), jnp.int32), ((8, 128), jnp.int32)] if extra else []

    def pack_weights(*refs):
        refs = list(refs)
        sources = [refs.pop(0) for _ in weights]
        ids = [refs.pop(0) for _ in extra]
        targets = [refs.pop(0) for _ in outs]
        sem = refs.pop()
        core = core_index()
        copies = []
        for n, (which, rows, first, out, start) in enumerate(moves):
            width = outs[out][0][1]
            copies.append(
                pltpu.make_async_copy(
                    sources[which].at[rows_at(core, rows), first : first + width],
                    targets[out].at[start : start + rows, :],
                    sem.at[n],
                )
            )
        for copy in copies:
            copy.start()
        if ids:
            set_ranges(*ids, *refs)
        for copy in copies:
            copy.wait()

    near = pl.BlockSpec(memory_space=pltpu.VMEM)
    return pl.pallas_call(
        pack_weights,
        out_shape=[jax.ShapeDtypeStruct(shape, kind) for shape, kind in outs + ranges],
        in_specs=[pl.BlockSpec(memory_space=pltpu.HBM)] * len(weights) + [near] * len(extra),
        out_specs=[near] * len(outs + ranges),
        scratch_shapes=[pltpu.SemaphoreType.DMA((len(moves),))],
        cost_estimate=pl.CostEstimate(flops=int(FLOPS_PER_US), bytes_accessed=1024, transcendentals=0),
        compiler_params=pltpu.CompilerParams(vmem_limit_bytes=60 * 1024 * 1024),
        name="pack_weights",
    )(*weights, *extra)


def local(
    inputs, memory, tgt_seg, src_seg, self_query, self_key, self_value, self_out,
    cross_query, cross_key, cross_value, cross_out, ffn_in, ffn_out,
    norm_gain, norm_shift, residual_scale, cotangent, *, n_dp, n_tensor,
):
    d = lax.axis_index("dp")
    t = lax.axis_index("tensor")
    length = tgt_seg.shape[1]
    model = inputs.shape[1]
    half = model // n_tensor
    hidden = ffn_in.shape[1]
    blocks = length // QB
    chunk = model // n_dp
    dealt = chunk % 16 == 0 and n_dp & (n_dp - 1) == 0
    swap_y = [(0, 1), (1, 0)]

    def swap(n_bit):
        return [(i, i ^ n_bit) for i in range(n_dp)]

    def after(value, *others):
        return lax.optimization_barrier((value, others))[0]

    own_s = [self_query, self_key, self_value, self_out]
    own_c = [cross_query, cross_key, cross_value, cross_out]
    own_f = [ffn_in, ffn_out]
    square = ((4 * half, half), BF16)

    def square_moves(base, out):
        part = model // 2
        moves = [(base + n, part, 0, out, n * part) for n in range(3)]
        return moves + [(base + 3, half // 2, n * half, out, 3 * part + n * half // 2) for n in range(n_tensor)]

    (pack_s,) = pack(own_s, [square], square_moves(0, 0))
    tiles = hidden // model
    pack_c, pack_f, brow, sc = pack(
        own_c + own_f, [square, ((tiles * half + hidden // 2, model), BF16)],
        square_moves(0, 0)
        + [(4, model // 2, n * model, 1, n * model // 2) for n in range(tiles)]
        + [(5, hidden // 2, 0, 1, tiles * model // 2)],
        (tgt_seg, src_seg),
    )
    mine_s = lax.ppermute(pack_s, "tensor", swap_y)

    def fill(whole, other):
        (result,) = call(
            fill_kernel, sc, [whole, other], [(whole.shape, whole.dtype)], [], 1, None, {0: (length, True)}, {0: 0},
            cuts={1: 4}, out_cuts={0: 4},
        )
        return result

    def total(*parts):
        result = parts[0].astype(F32)
        for part in parts[1:]:
            result = result + part.astype(F32)
        return result

    size = model // 4

    def part_total(n, *arrays):
        return total(*[array[n * size : (n + 1) * size] for array in arrays]).astype(BF16)

    def z_send(part):
        far = n_dp // 4
        row = d // 4
        part = part.reshape(far, chunk, -1)
        parts = [lax.dynamic_index_in_dim(part, row, 0, keepdims=False)]
        for step in range(1, far):
            perm = [(i, i % 4 + (i // 4 + step) % far * 4) for i in range(n_dp)]
            out = lax.dynamic_index_in_dim(part, (row + step) % far, 0, keepdims=False)
            parts.append(lax.ppermute(out, "dp", perm))
        return parts

    def reduce_any(keep, send):
        grad = lax.psum_scatter(jnp.concatenate([keep, send]).astype(F32), "dp", scatter_dimension=0, tiled=True)
        width = grad.shape[1] // 2
        return grad[:, :width] + lax.ppermute(grad[:, width:], "tensor", swap_y)

    wide, side = (length, model), (length, half)
    heads = GW // HEAD_DIM
    group = [(side, BF16)] * 4 + [((half // HEAD_DIM, length), F32)]
    square_weights = [((model, half), BF16)] * 3 + [((half, model), BF16)]
    stats = [(wide, F32), ((length, 128), F32)]
    attend_scratch = [
        ((2, length, heads * QB), F32),
        ((2, heads * QB), F32),
        ((2, heads * QB), F32),
        ((2, GW, heads * QB), F32),
    ]
    block_wide = ((MB, model), F32)
    cut = length // MB
    norms = [norm_gain, norm_shift, residual_scale]
    s_own = call(
        self_forward_own, sc, [*own_s[:3], inputs, brow], group, attend_scratch, 7, {3: (length, False)},
        cuts={3: cut}, out_cuts={0: cut, 1: cut, 2: cut},
    )
    s_own, mine_s = lax.optimization_barrier((s_own, mine_s))
    sib_s = lax.ppermute(mine_s, "dp", swap(1))
    mine_c = lax.ppermute(after(pack_c, mine_s), "tensor", swap_y)
    s_rest_stats = call(
        self_forward_rest, sc, [mine_s, sib_s, inputs, brow, s_own[3], self_out, residual_scale], group + stats,
        [*square_weights, block_wide, *attend_scratch], 8, {2: (length, False)},
        cuts={2: cut}, out_cuts={n: cut for n in (0, 1, 2, 5, 6)},
    )
    s_rest_stats, mine_c = lax.optimization_barrier((s_rest_stats, mine_c))
    *s_rest, xhat1, rstd1 = s_rest_stats
    sib_c = lax.ppermute(mine_c, "dp", swap(1))
    mine_f = lax.ppermute(after(pack_f, mine_c), "tensor", swap_y)
    c_stats = call(
        cross_forward, sc,
        [mine_c, sib_c, *own_c[:3], norm_gain, norm_shift, xhat1, memory, brow, cross_out, residual_scale],
        group + group + stats,
        [*square_weights, block_wide, *attend_scratch], 14, {8: (length, False)}, cuts={7: cut, 8: cut},
        out_cuts={n: cut for n in (0, 1, 2, 5, 6, 7, 10, 11)},
    )
    *c_state, xhat2, rstd2 = c_stats
    sums_shape = ((8, model), F32)
    low_side, low_wide = ((length, hidden), BF16), ((length, n_tensor * hidden), BF16)
    f_weights = [((model, hidden), BF16), ((hidden, model), BF16)]
    f_own, mine_f = lax.optimization_barrier((
        call(
            ffn_forward_own, sc, [ffn_in, norm_gain, norm_shift, xhat2, ffn_out, residual_scale],
            [low_side, low_side, (wide, F32)], [], 8, cuts={3: cut}, out_cuts={n: cut for n in range(3)},
        ),
        mine_f,
    ))
    act_own, slope_own, pre_own = f_own
    sib_f = lax.ppermute(mine_f, "dp", swap(1))

    def grads(width, parts=2):
        return [((parts * size, 4 * width // parts), BF16)] * 2

    def core_swap(send):
        return lax.ppermute(send, "dp", swap(1)) if dealt else send

    turned = ((model, length), BF16)
    chunk_rows = chunk if dealt else model // 4
    out_row, output, slope_rest, d_pre3, f1_keep, f1_send, sums3 = call(
        functools.partial(ffn_forward_rest, chunk=chunk_rows), sc,
        [mine_f, sib_f, norm_gain, norm_shift, xhat2, pre_own, cotangent, act_own],
        [(wide, BF16), ((n_tensor * length, model), BF16), low_side, (wide, F32), *grads(hidden), sums_shape],
        [low_side, *f_weights, turned, ((model, 2 * hidden), BF16)], 11,
        {6: (length, False)}, {1: (length, False)}, cuts={4: cut, 5: cut, 6: cut}, out_cuts={n: cut for n in range(4)},
        bare=(4, 5), dealt=dealt,
    )
    out_other = lax.ppermute(out_row, "tensor", swap_y)
    f1_other = core_swap(f1_send)
    back, f1_other = lax.optimization_barrier((
        call(
            functools.partial(ffn_backward, chunk=chunk_rows), sc,
            [ffn_out, ffn_in, *norms, d_pre3, slope_own, xhat2, slope_rest, mine_f, sib_f, rstd2],
            [(wide, F32), *grads(hidden), sums_shape],
            [low_wide, turned, *f_weights, block_wide, ((model, 2 * hidden), BF16)], 12,
            cuts={n: cut for n in (5, 6, 7, 8, 11)}, out_cuts={0: cut}, bare=(1, 2), dealt=dealt,
        ),
        f1_other,
    ))
    d_pre2, f2_keep, f2_send, sums2 = back
    f2_other = core_swap(f2_send)
    if dealt:
        f_there = jnp.concatenate([part_total(1, f1_keep, f1_other), part_total(1, f2_keep, f2_other)], axis=1)
        d_pre2 = after(d_pre2, f_there)
        f_x = lax.ppermute(f_there, "dp", swap(2))
    else:
        f_x = sums2
    logs = ((half // HEAD_DIM, length), F32)
    halves = [((n_tensor * length, half), F32), (side, BF16)]
    back, f_x, out_other = lax.optimization_barrier((
        call(
            functools.partial(cross_backward, chunk=chunk_rows), sc,
            [mine_c, sib_c, cross_out, *norms, d_pre2, xhat1, memory, c_state[3], c_state[8],
             *c_state[:3], *c_state[5:8], c_state[4], c_state[9], brow, *own_c[:3], rstd1],
            [(wide, F32), *halves, *grads(4 * half), sums_shape],
            [*square_weights, *[(side, BF16)] * 2, logs, logs, *[(side, BF16)] * 2, *[(side, F32)] * 4,
             *[(side, BF16)] * 4, ((2, heads * QB, GW), F32), turned, turned, turned, block_wide,
             ((model, 8 * half), BF16)],
            23, {8: (length, False)}, {1: (length, False)}, cuts={n: cut for n in range(6, 11)},
            out_cuts={n: cut for n in range(3)}, bare=(3, 4), dealt=dealt,
        ),
        f_x, out_other,
    ))
    d_pre1, memory_grad, mem_send, c_keep, c_send, sums1 = back
    mem_other = lax.ppermute(mem_send, "tensor", swap_y)
    c_other = core_swap(c_send)
    c_x, f_z = sums1, sums1
    if dealt:
        f_part = jnp.concatenate(
            [
                part_total(
                    0, keep[:, first : first + hidden], other[:, first : first + hidden],
                    f_x[:, base + first : base + first + hidden],
                )
                for first in (0, hidden)
                for keep, other, base in ((f1_keep, f1_other, 0), (f2_keep, f2_other, 2 * hidden))
            ],
            axis=1,
        )
        f_z = z_send(f_part)
        c_there = part_total(1, c_keep, c_other)
        c_x = lax.ppermute(c_there, "dp", swap(2))
        d_pre1 = after(d_pre1, c_there, f_part)
    back, c_x, mem_other = lax.optimization_barrier((
        call(
            functools.partial(self_backward, chunk=chunk_rows), sc,
            [mine_s, sib_s, self_out, d_pre1, inputs, s_own[3], s_rest[3], *s_own[:3],
             *s_rest[:3], s_own[4], s_rest[4], brow, sums1, sums2, sums3, out_other, output],
            [*[(side, BF16)] * 6, *grads(4 * half + QB, 4 if dealt else 2), (output.shape, BF16)],
            [*square_weights, *[(side, BF16)] * 2, logs, logs, *[(side, F32)] * 4,
             ((2, heads * QB, GW), F32), turned, turned, ((8, model), F32), ((QB, model), F32), ((model, QB), BF16),
             ((model, 2 * (4 * half + QB)), BF16)],
            16, {4: (length, False)}, {8: (length, True)}, {20: 8}, cuts={n: cut for n in range(3, 7)},
            bare=(6, 7, 8), dealt=dealt,
        ),
        c_x, mem_other,
    ))
    *d_self, s_keep, s_send, output = back
    s_other = core_swap(s_send)
    if dealt:
        across = [(i * 2 + j, (i ^ 2) * 2 + 1 - j) for i in range(n_dp) for j in range(2)]
        s_near = [part_total(n, s_keep, s_other) for n in range(1, 4)]
        f_last = total(*f_z).astype(BF16)
        c_part = part_total(0, c_keep, c_other, c_x)
        d_self[0] = after(d_self[0], *s_near, f_last, c_part)
        s_near = [
            lax.ppermute(s_near[0], "tensor", swap_y), lax.ppermute(s_near[1], "dp", swap(2)),
            lax.ppermute(s_near[2], ("dp", "tensor"), across),
        ]
        c_z = z_send(c_part)
    input_grad, in_send, memory_grad = call(
        input_backward, sc,
        [mine_s, sib_s, *own_s[:3], residual_scale, d_pre1, *d_self, mem_other, memory_grad],
        [*halves, (memory_grad.shape, F32)], square_weights, 5, None, {0: (length, False), 2: (length, True)},
        {14: 2}, cuts={n: cut for n in range(6, 13)}, out_cuts={0: cut, 1: cut},
    )
    thin, broad = ((chunk, half), F32), ((chunk, hidden), F32)
    three = ((3, chunk), F32)
    if dealt:
        in_send, s_near, c_z = lax.optimization_barrier((in_send, s_near, c_z))
        in_other = lax.ppermute(in_send, "tensor", swap_y)
        s_far = z_send(part_total(0, s_keep, s_other, *s_near))
        c_last = total(*c_z).astype(BF16)
        late = lax.ppermute(
            jnp.concatenate([f_last[:, 2 * hidden :], c_last[:, 4 * half :]], axis=1), "tensor", swap_y
        )
        while len(s_far) < 4:
            s_far.append(jnp.zeros_like(s_far[0]))
        s_far = [*s_far[:3], s_far[3] if len(s_far) == 4 else total(*s_far[3:]).astype(BF16)]
        input_grad = fill(input_grad, in_other)
        sq, sk, sv, so, cq, ck, cv, co, ffn_in_grad, ffn_out_grad, gain_grad, shift_grad, scale_grad = call(
            finish, sc, [f_last, c_last, late, *s_far], [*[thin] * 8, broad, broad, three, three, three], [], 0.01
        )
    else:
        input_grad = fill(input_grad, lax.ppermute(in_send, "tensor", swap_y))
        f1_sum, f2_sum = reduce_any(f1_keep, f1_send), reduce_any(f2_keep, f2_send)
        c_sum, s_sum = reduce_any(c_keep, c_send), reduce_any(s_keep, s_send)
        ffn_in_grad, ffn_out_grad = f2_sum, f1_sum
        cq, ck, cv, co = [c_sum[:, n * half : (n + 1) * half] for n in range(4)]
        sq, sk, sv, so = [s_sum[:, n * half : (n + 1) * half] for n in range(4)]
        gain_grad, shift_grad, scale_grad = [s_sum[:, 4 * half + 3 * n : 4 * half + 3 * n + 3].T for n in range(3)]
    return (
        output, input_grad, memory_grad, sq, sk, sv, so.T, cq, ck, cv, co.T, ffn_in_grad, ffn_out_grad.T,
        gain_grad, shift_grad, scale_grad,
    )


def solution(mesh):
    rows, cols = P("dp", None), P(None, "tensor")
    both, turned = P("dp", "tensor"), P("tensor", "dp")
    return jax.shard_map(
        functools.partial(local, n_dp=mesh.shape["dp"], n_tensor=mesh.shape["tensor"]),
        mesh=mesh,
        in_specs=(
            rows, rows, rows, rows, cols, cols, cols, turned_rows(), cols, cols, cols, turned_rows(), cols,
            turned_rows(), P(), P(), P(), rows,
        ),
        out_specs=(
            rows, both, both, both, both, both, turned, both, both, both, turned, both, turned,
            P(None, "dp"), P(None, "dp"), P(None, "dp"),
        ),
        check_vma=False,
    )


def turned_rows():
    return P("tensor", None)
```

```python
import functools
import math

import jax
import jax.numpy as jnp
from jax import lax
from jax.experimental import pallas as pl
from jax.experimental.pallas import tpu as pltpu
from jax.sharding import PartitionSpec as P

HEAD_DIM = 64
QB = 128
KC = 256
XC = 128
GW = 256
EPS = 1e-05
NEG = -1e30
F32 = jnp.float32
BF16 = jnp.bfloat16
MB = 512
SPARE = 12 * 1024 * 1024
FULL = 56 * 1024 * 1024
SEGMENTS = 32
FLOPS_PER_US = 5e9


def nn(left, right):
    return lax.dot_general(left, right, (((1,), (0,)), ((), ())), preferred_element_type=F32)


def nt(left, right):
    return lax.dot_general(left, right, (((1,), (1,)), ((), ())), preferred_element_type=F32)


def tn(left, right):
    return lax.dot_general(left, right, (((0,), (0,)), ((), ())), preferred_element_type=F32)


def iota(shape, dim):
    return lax.broadcasted_iota(jnp.int32, shape, dim)


def normalise(pre):
    center = jnp.mean(pre, axis=-1, keepdims=True)
    centered = pre - center
    rstd = lax.rsqrt(jnp.mean(centered * centered, axis=-1, keepdims=True) + EPS)
    return centered * rstd, rstd


def norm_back(grad, gain, xhat, rstd):
    scaled = grad * gain
    first = jnp.mean(scaled, axis=-1, keepdims=True)
    second = jnp.mean(scaled * xhat, axis=-1, keepdims=True)
    return rstd * (scaled - first - xhat * second)


def rows_at(block, size):
    return pl.ds(pl.multiple_of(block * size, size), size)


def stack_heads(block):
    head = iota((1, GW), 1) // HEAD_DIM
    return jnp.concatenate(
        [block * (head == h).astype(F32).astype(BF16) for h in range(GW // HEAD_DIM)], axis=0
    )


def unstack_heads(stacked, rows):
    low_half = iota((1, 128), 1) < HEAD_DIM
    tiles = []
    for tile in range(GW // 128):
        cols = slice(tile * 128, tile * 128 + 128)
        first, second = 2 * tile, 2 * tile + 1
        tiles.append(
            jnp.where(
                low_half,
                stacked[first * rows : (first + 1) * rows, cols],
                stacked[second * rows : (second + 1) * rows, cols],
            )
        )
    return jnp.concatenate(tiles, axis=1)


def each_more(units, where, body):
    if all(unit[where] is units[0][where] for unit in units):

        @pl.loop(1, units[0][where])
        def _(j):
            for n in range(len(units)):
                body(n, j)

    else:
        for n, unit in enumerate(units):

            @pl.loop(1, unit[where])
            def _(j):
                body(n, j)


def chunk_keys(first, j):
    if isinstance(j, int):
        return pl.ds(pl.multiple_of(first, 16), KC)
    return pl.ds(pl.multiple_of(first + (KC - XC) + j * XC, 16), XC)


def attend_units(units, s_scr, m_scr, l_scr, o_scr):
    heads = GW // HEAD_DIM
    stacks = [stack_heads(q[rows_at(i, QB), :]) for i, q, *_ in units]

    def scores(n, j):
        _, _, k, _, lo, hi, first, _ = units[n]
        keys, place = chunk_keys(first, j), chunk_keys(0, j)
        at = keys.start + iota((keys.size, QB), 0)
        allowed = (at >= lo) & (at < hi)
        s = nt(k[keys, :], stacks[n])
        peaks = []
        for h in range(heads):
            part = slice(h * QB, (h + 1) * QB)
            masked = jnp.where(allowed, s[:, part], NEG)
            s_scr[n, place, part] = masked
            peaks.append(jnp.max(masked, axis=0, keepdims=True))
        return jnp.concatenate(peaks, axis=1)

    for n in range(len(units)):
        m_scr[n : n + 1, :] = scores(n, 0)

    def more_scores(n, j):
        m_scr[n : n + 1, :] = jnp.maximum(m_scr[n : n + 1, :], scores(n, j))

    each_more(units, 7, more_scores)
    peaks = [m_scr[n : n + 1, :] for n in range(len(units))]

    def weigh(n, j):
        p = jnp.exp(s_scr[n, chunk_keys(0, j), :] - peaks[n])
        return jnp.sum(p, axis=0, keepdims=True), tn(units[n][3][chunk_keys(units[n][6], j), :], p.astype(BF16))

    for n in range(len(units)):
        l_scr[n : n + 1, :], o_scr[n] = weigh(n, 0)

    def more_weights(n, j):
        more_l, more_o = weigh(n, j)
        l_scr[n : n + 1, :] = l_scr[n : n + 1, :] + more_l
        o_scr[n] = o_scr[n] + more_o

    each_more(units, 7, more_weights)
    results = []
    for n in range(len(units)):
        total = l_scr[n : n + 1, :]
        log = peaks[n] + jnp.log(total)
        scale = 1.0 / total
        parts = [
            o_scr[n, h * HEAD_DIM : (h + 1) * HEAD_DIM, h * QB : (h + 1) * QB] * scale[:, h * QB : (h + 1) * QB]
            for h in range(heads)
        ]
        mixed = jnp.transpose(jnp.concatenate(parts, axis=0).astype(BF16))
        results.append((mixed, [log[:, h * QB : (h + 1) * QB] for h in range(heads)]))
    return results


def attend_back_units(units, r_scr):
    heads = GW // HEAD_DIM

    def chunk(n, j):
        i, q, k, v, do, lse, delta, lo, hi, first, _, _, dk, dv = units[n]
        rows = rows_at(i, QB)
        keys = chunk_keys(first, j)
        qs = stack_heads(q[rows, :])
        ds = stack_heads(do[rows, :])
        kg = k[keys, :]
        at = keys.start + iota((keys.size, QB), 0)
        allowed = (at >= lo) & (at < hi)
        st = nt(kg, qs)
        dp = nt(v[keys, :], ds)
        probs, grads = [], []
        for h in range(heads):
            part = slice(h * QB, (h + 1) * QB)
            p = jnp.where(allowed, jnp.exp(st[:, part] - lse[h : h + 1, rows]), 0.0)
            probs.append(p.astype(BF16))
            grads.append((p * (dp[:, part] - delta[h : h + 1, rows])).astype(BF16))
        prob = jnp.concatenate(probs, axis=1)
        grad = jnp.concatenate(grads, axis=1)
        dv[keys, :] += nn(prob, ds)
        dk[keys, :] += nn(grad, qs)
        return tn(grad, kg)

    for n in range(len(units)):
        r_scr[n] = chunk(n, 0)

    def more(n, j):
        r_scr[n] = r_scr[n] + chunk(n, j)

    each_more(units, 10, more)
    for n, unit in enumerate(units):
        unit[11][rows_at(unit[0], QB), :] = (unstack_heads(r_scr[n], QB) * HEAD_DIM**-0.5).astype(BF16)


def set_delta(rows, do, mixed, delta_scr):
    heads = do.shape[1] // HEAD_DIM
    product = do.astype(F32) * mixed.astype(F32)
    high = product.astype(BF16)
    rest = (product - high.astype(F32)).astype(BF16)
    pick = (iota((heads, do.shape[1]), 1) // HEAD_DIM == iota((heads, do.shape[1]), 0)).astype(F32).astype(BF16)
    delta_scr[:, rows] = nt(pick, high) + nt(pick, rest)


def put_transposed(rows, block, scr, chunk):
    turned = jnp.transpose(block)
    size = turned.shape[0]
    count = size // chunk
    for n in range(count):
        first = (n % 2 * 2 + n // 2 % 2) * (size // 4) + n // 4 * chunk if chunk else 0
        scr[first : first + chunk, rows] = turned[n * chunk : (n + 1) * chunk]


def add_sum(ref, row, value):
    ref[row : row + 1, :] += jnp.sum(value, axis=0, keepdims=True)


def project(rows, left, weight, out, factor=1.0):
    out[rows, :] = (nn(left, weight[...]) * factor).astype(BF16)


def unpack_square(mine, sib, weights):
    core = core_index()
    *cols, out = weights
    part, half = cols[0].shape[0] // 2, out.shape[0]
    small = half // 2
    for place, source in ((core, mine), (1 - core, sib)):
        for n, w in enumerate(cols):
            w[rows_at(place, part), :] = source[n * part : (n + 1) * part, :]
        base = len(cols) * part
        for n in range(out.shape[1] // half):
            out[rows_at(place, small), n * half : (n + 1) * half] = source[
                base + n * small : base + (n + 1) * small, :
            ]


def unpack_ffn(mine, sib, win, wout):
    core = core_index()
    part, rows, width = win.shape[0] // 2, wout.shape[0] // 2, wout.shape[1]
    tiles = win.shape[1] // width
    for place, source in ((core, mine), (1 - core, sib)):
        for n in range(tiles):
            win[rows_at(place, part), n * width : (n + 1) * width] = source[n * part : (n + 1) * part, :]
        wout[rows_at(place, rows), :] = source[tiles * part :, :]


def core_index():
    return lax.axis_index("dp") % 2


def set_ranges(tgt, src, brow, blocks):
    rows, length = tgt.shape
    mine = lax.axis_index("tensor")

    def row(ref):
        value = ref[0:1, :]
        for n in range(1, rows):
            value = jnp.where(mine == n, ref[n : n + 1, :], value)
        return value

    target, source = row(tgt), row(src)
    ids = iota((SEGMENTS, length), 0)

    def before(ids_of, limit):
        count = jnp.sum((ids_of < limit).astype(F32), axis=1, keepdims=True)
        return jnp.sum(jnp.where(ids == target, count, 0.0), axis=0, keepdims=True).astype(jnp.int32)

    values = [
        before(target, ids), iota((1, length), 1) + 1, before(source, ids), before(source, ids + 1)
    ]
    lane = iota((1, 128), 1)
    for n, value in enumerate(values):
        brow[n : n + 1, :] = value
        brow[n + 4 : n + 5, :] = value
    blocks[...] = jnp.zeros_like(blocks)
    for n in range(2):
        first = jnp.zeros((1, 128), jnp.int32)
        last = jnp.zeros((1, 128), jnp.int32)
        for i in range(length // QB):
            low, high = values[2 * n][:, i * QB : i * QB + 1], values[2 * n + 1][:, (i + 1) * QB - 1 : (i + 1) * QB]
            first = jnp.where(lane == i, low, first)
            last = jnp.where(lane == i, high, last)
        first = lax.shift_left(lax.shift_right_logical(first, 4), 4)
        more = lax.shift_right_logical(jnp.maximum(last - first - KC, 0) + (XC - 1), XC.bit_length() - 1)
        blocks[2 * n : 2 * n + 1, :] = jnp.minimum(first, length - KC - more * XC)
        blocks[2 * n + 1 : 2 * n + 2, :] = more + 1


def forward_units(sc, brow, i, which, groups):
    rows = rows_at(i, QB)
    first, count = sc[2 * which, i], sc[2 * which + 1, i]
    lo, hi = brow[2 * which : 2 * which + 1, rows], brow[2 * which + 1 : 2 * which + 2, rows]
    return [(i, q, k, v, lo, hi, first, count) for q, k, v in groups]


def put_logs(lse, i, logs):
    for h, log in enumerate(logs):
        lse[h : h + 1, rows_at(i, QB)] = log


def project_self(x, weights, outs):
    @pl.loop(0, x.chunks)
    def _(i):
        x.need(i)
        rows = rows_at(i, MB)
        block = x[rows, :]
        for weight, out, factor in zip(weights, outs, (HEAD_DIM**-0.5, 1.0, 1.0)):
            project(rows, block, weight, out, factor)
            out.put(i)


def self_forward_own(sc, qo, ko, vo, x, brow, q, k, v, mixed, lse, *scratch):
    need(qo, ko, vo)
    project_self(x, (qo, ko, vo), (q, k, v))
    need(brow)

    @pl.loop(0, x.shape[0] // QB // 2)
    def _(pair):
        pair_of = [2 * pair, 2 * pair + 1]
        units = [forward_units(sc, brow, i, 0, [(q, k, v)])[0] for i in pair_of]
        for i, (block, logs) in zip(pair_of, attend_units(units, *scratch)):
            mixed[rows_at(i, QB), :] = block
            put_logs(lse, i, logs)


def norm_rows(i, pre, xhat, rstd):
    @pl.loop(0, MB // QB)
    def _(n):
        rows = rows_at(i * (MB // QB) + n, QB)
        hat, inv = normalise(pre[rows_at(n, QB), :])
        xhat[rows, :] = hat
        rstd[rows, :] = jnp.broadcast_to(inv, (QB, rstd.shape[1]))

    xhat.put(i)
    rstd.put(i)


def self_forward_rest(
    sc, mine, sib, x, brow, mixed_own, oo, omega,
    q, k, v, mixed, lse, xhat, rstd, qx, kx, vx, ox, pre, *scratch,
):
    need(mine, sib)
    unpack_square(mine, sib, (qx, kx, vx, ox))
    project_self(x, (qx, kx, vx), (q, k, v))
    need(brow)

    @pl.loop(0, x.shape[0] // QB // 2)
    def _(pair):
        pair_of = [2 * pair, 2 * pair + 1]
        units = [forward_units(sc, brow, i, 0, [(q, k, v)])[0] for i in pair_of]
        for i, (block, logs) in zip(pair_of, attend_units(units, *scratch)):
            mixed[rows_at(i, QB), :] = block
            put_logs(lse, i, logs)

    need(mixed_own, oo, omega)

    @pl.loop(0, x.chunks)
    def _(i):
        rows = rows_at(i, MB)
        branch = nn(mixed_own[rows, :], oo[...]) + nn(mixed[rows, :], ox[...])
        pre[...] = omega[0:1] * x[rows, :].astype(F32) + branch
        norm_rows(i, pre, xhat, rstd)


def cross_forward(
    sc, mine, sib, qo, ko, vo, gain, shift, xhat1, mem, brow, oo, omega,
    q, k, v, mixed, lse, q_x, k_x, v_x, mixed_x, lse_x, xhat, rstd, qx, kx, vx, ox, pre, *scratch,
):
    need(mine, sib, qo, ko, vo, gain, shift)
    unpack_square(mine, sib, (qx, kx, vx, ox))

    @pl.loop(0, mem.chunks)
    def _(i):
        rows = rows_at(i, MB)
        xhat1.need(i)
        mem.need(i)
        low1 = (xhat1[rows, :] * gain[0:1] + shift[0:1]).astype(BF16)
        block = mem[rows, :]
        for weights, outs in (((qo, ko, vo), (q, k, v)), ((qx, kx, vx), (q_x, k_x, v_x))):
            project(rows, low1, weights[0], outs[0], HEAD_DIM**-0.5)
            project(rows, block, weights[1], outs[1])
            project(rows, block, weights[2], outs[2])
            for result in outs:
                result.put(i)

    need(brow)

    @pl.loop(0, mem.shape[0] // QB)
    def _(i):
        units = forward_units(sc, brow, i, 1, ((q, k, v), (q_x, k_x, v_x)))
        for (block, logs), out, lse_out in zip(attend_units(units, *scratch), (mixed, mixed_x), (lse, lse_x)):
            out[rows_at(i, QB), :] = block
            put_logs(lse_out, i, logs)

    need(oo, omega)

    @pl.loop(0, mem.chunks)
    def _(i):
        rows = rows_at(i, MB)
        branch = nn(mixed[rows, :], oo[...]) + nn(mixed_x[rows, :], ox[...])
        pre[...] = omega[1:2] * (xhat1[rows, :] * gain[0:1] + shift[0:1]) + branch
        norm_rows(i, pre, xhat, rstd)


def hidden_units(rows, low2, win, act, slope, width=512):
    for first in range(0, win.shape[1], width):
        place = slice(first, first + width)
        u = nn(low2, win[:, place])
        square = u * u
        t = jnp.tanh(u * (0.7978845608028654 + (0.7978845608028654 * 0.044715) * square))
        h = 0.5 + 0.5 * t
        a = u * h
        act[rows, place] = a.astype(BF16)
        steep = 2 * 0.7978845608028654 + (6 * 0.7978845608028654 * 0.044715) * square
        slope[rows, place] = (h + a * (1.0 - h) * steep).astype(BF16)


def ffn_forward_own(sc, io, gain, shift, xhat2, oo, omega, act, slope, pre):
    need(io, gain, shift)

    @pl.loop(0, xhat2.chunks)
    def _(i):
        rows = rows_at(i, MB)
        xhat2.need(i)
        norm2 = xhat2[rows, :] * gain[1:2] + shift[1:2]
        hidden_units(rows, norm2.astype(BF16), io, act, slope)
        act.put(i)
        slope.put(i)

    need(oo, omega)

    @pl.loop(0, xhat2.chunks)
    def _(i):
        rows = rows_at(i, MB)
        norm2 = xhat2[rows, :] * gain[1:2] + shift[1:2]
        pre[rows, :] = omega[2:3] * norm2 + nn(act[rows, :], oo[...])
        pre.put(i)


def ffn_forward_rest(
    sc, mine, sib, gain, shift, xhat2, pre, cot, act_own,
    out, out_all, slope, d_pre3, keep, send, sums, act, ix, ox, grad_t, grads, *, chunk,
):
    need(mine, sib, gain, shift)
    unpack_ffn(mine, sib, ix, ox)
    sums[...] = jnp.zeros_like(sums)
    width = 512
    half = ix.shape[1]

    @pl.loop(0, xhat2.chunks)
    def _(i):
        rows = rows_at(i, MB)
        xhat2.need(i)
        hidden_units(rows, (xhat2[rows, :] * gain[1:2] + shift[1:2]).astype(BF16), ix, act, slope)
        slope.put(i)
        pre.need(i)
        cot.need(i)
        pre[rows, :] += nn(act[rows, :], ox[...])

        @pl.loop(0, MB // QB)
        def _(n):
            small = rows_at(i * (MB // QB) + n, QB)
            hat, inv = normalise(pre[small, :])
            result = (hat * gain[2:3] + shift[2:3]).astype(BF16)
            out[small, :] = result
            out_all[small, :] = result
            grad = cot[small, :].astype(F32)
            d_pre = norm_back(grad, gain[2:3], hat, inv)
            d_pre3[small, :] = d_pre
            put_transposed(small, d_pre.astype(BF16), grad_t, chunk)
            add_sum(sums, 0, grad * hat)
            add_sum(sums, 1, grad)
            add_sum(sums, 2, d_pre * (xhat2[small, :] * gain[1:2] + shift[1:2]))

        for result in (out, out_all, d_pre3):
            result.put(i)

    need(act_own)
    for side, right in enumerate((act_own, act)):
        for first in range(0, half, width):
            grads[:, side * half + first : side * half + first + width] = nn(
                grad_t[...], right[:, first : first + width]
            ).astype(BF16)
    put_grads(grads, keep, send)


def put_grads(scr, keep, send):
    dp = lax.axis_index("dp")
    core, x = (dp % 2, dp // 2 % 2) if keep.dealt else (0, 0)
    size, width = scr.shape[0] // 4, keep.shape[1]
    parts = keep.shape[0] // size
    for out, row in ((keep, core), (send, 1 - core)):
        for n in range(parts):
            side = n * 2 // parts
            first = n % 2 * width if parts == 4 else 0
            place = row * 2 + (x if side == 0 else 1 - x)
            out.copy_part(scr.at[rows_at(place, size), first : first + width], n * size)


def ffn_backward(
    sc, oo, io, gain, shift, omega, d_pre3, slope_own, xhat2, slope_rest, mine, sib, rstd2,
    d_pre2, keep, send, sums, up_scr, norm_t, ix, ox, acc, grads, *, chunk,
):
    need(io, oo, gain, shift, omega, mine, sib)
    unpack_ffn(mine, sib, ix, ox)
    sums[...] = jnp.zeros_like(sums)
    half = io.shape[1]
    width = 512

    @pl.loop(0, xhat2.chunks)
    def _(i):
        rows = rows_at(i, MB)
        for argument in (d_pre3, slope_own, xhat2, slope_rest):
            argument.need(i)
        grad = d_pre3[rows, :]
        low = grad.astype(BF16)
        acc[...] = omega[2:3] * grad
        for side, (win, wout, slope) in enumerate(((io, oo, slope_own), (ix, ox, slope_rest))):
            for first in range(0, half, width):
                place = slice(side * half + first, side * half + first + width)
                up_scr[rows, place] = (
                    slope[rows, first : first + width].astype(F32) * nt(low, wout[first : first + width, :])
                ).astype(BF16)
            acc[...] += nt(up_scr[rows, side * half : (side + 1) * half], win[...])

        rstd2.need(i)

        @pl.loop(0, MB // QB)
        def _(n):
            small = rows_at(i * (MB // QB) + n, QB)
            total = acc[rows_at(n, QB), :]
            hat = xhat2[small, :]
            put_transposed(small, (hat * gain[1:2] + shift[1:2]).astype(BF16), norm_t, chunk)
            d_pre2[small, :] = norm_back(total, gain[1:2], hat, rstd2[small, 0:1])
            add_sum(sums, 0, total * hat)
            add_sum(sums, 1, total)

        d_pre2.put(i)

    for first in range(0, 2 * half, width):
        grads[:, first : first + width] = nn(norm_t[...], up_scr[:, first : first + width]).astype(BF16)
    put_grads(grads, keep, send)


def weight_grads(pairs, grads):
    width = grads.shape[1] // 2
    for n, (left, *rights) in enumerate(pairs):
        for side, right in enumerate(rights):
            half = right.shape[1]
            first = side * width + n * half
            grads[:, first : first + half] = nn(left[...], right[...]).astype(BF16)


def backward_units(sc, brow, i, which, groups):
    rows = rows_at(i, QB)
    first, count = sc[2 * which, i], sc[2 * which + 1, i]
    lo, hi = brow[2 * which : 2 * which + 1, rows], brow[2 * which + 1 : 2 * which + 2, rows]
    return [(i, *group[:6], lo, hi, first, count, *group[6:]) for group in groups]


def attention_grads(low, rows, outs):
    for out, weight, was, total in outs:
        value = nt(low, weight[...]).astype(BF16)
        out[rows, :] = value
        set_delta(rows, value, was[rows, :], total)


def cross_backward(
    sc, mine, sib, oo, gain, shift, omega, d_pre2, xhat1, mem, mixed, mixed_x, q, k, v, q_x, k_x, v_x, lse, lse_x,
    brow, qo, ko, vo, rstd1,
    d_pre1, mem_all, mem_send, keep, send, sums,
    qx, kx, vx, ox, do, do_x, delta, delta_x, dq, dq_x, dk, dk_x, dv, dv_x, dkb, dkb_x, dvb, dvb_x, r_scr,
    grad_t, norm_t, mem_t, acc, grads, *, chunk,
):
    half = qo.shape[1]
    blocks = mem.shape[0] // QB
    for ref in (sums, dk, dk_x, dv, dv_x):
        ref[...] = jnp.zeros_like(ref)
    need(mine, sib, oo, gain, shift, omega)
    unpack_square(mine, sib, (qx, kx, vx, ox))

    @pl.loop(0, mem.chunks)
    def _(i):
        rows = rows_at(i, MB)
        for argument in (d_pre2, xhat1, mem, mixed, mixed_x):
            argument.need(i)
        grad = d_pre2[rows, :]
        low = grad.astype(BF16)
        norm1 = xhat1[rows, :] * gain[0:1] + shift[0:1]
        put_transposed(rows, low, grad_t, chunk)
        put_transposed(rows, norm1.astype(BF16), norm_t, chunk)
        put_transposed(rows, mem[rows, :], mem_t, chunk)
        attention_grads(low, rows, ((do, oo, mixed, delta), (do_x, ox, mixed_x, delta_x)))
        add_sum(sums, 0, grad * norm1)

    need(q, k, v, q_x, k_x, v_x, lse, lse_x, brow)

    @pl.loop(0, blocks)
    def _(i):
        groups = (
            (q, k, v, do, lse, delta, dq, dk, dv), (q_x, k_x, v_x, do_x, lse_x, delta_x, dq_x, dk_x, dv_x)
        )
        attend_back_units(backward_units(sc, brow, i, 1, groups), r_scr)

    need(qo, ko, vo, rstd1)
    tensor = lax.axis_index("tensor")

    @pl.loop(0, mem.chunks)
    def _(i):
        rows = rows_at(i, MB)
        acc[...] = omega[1:2] * d_pre2[rows, :] + nt(dq[rows, :], qo[...]) + nt(dq_x[rows, :], qx[...])
        for low, wide in ((dkb, dk), (dkb_x, dk_x), (dvb, dv), (dvb_x, dv_x)):
            low[rows, :] = wide[rows, :].astype(BF16)

        def part(side):
            which = rows_at(side, half)
            return (
                nt(dkb[rows, :], ko[which, :]) + nt(dkb_x[rows, :], kx[which, :])
                + nt(dvb[rows, :], vo[which, :]) + nt(dvb_x[rows, :], vx[which, :])
            )

        mem_all[rows, :] = part(tensor)
        mem_send[rows, :] = part(1 - tensor).astype(BF16)

        @pl.loop(0, MB // QB)
        def _(n):
            small = rows_at(i * (MB // QB) + n, QB)
            total = acc[rows_at(n, QB), :]
            hat = xhat1[small, :]
            d_pre1[small, :] = norm_back(total, gain[0:1], hat, rstd1[small, 0:1])
            add_sum(sums, 1, total * hat)
            add_sum(sums, 2, total)

        for result in (d_pre1, mem_all, mem_send):
            result.put(i)

    weight_grads(
        ((norm_t, dq, dq_x), (mem_t, dkb, dkb_x), (mem_t, dvb, dvb_x), (grad_t, mixed, mixed_x)), grads
    )
    put_grads(grads, keep, send)


def self_backward(
    sc, mine, sib, oo, d_pre1, x, mixed, mixed_x, q, k, v, q_x, k_x, v_x, lse, lse_x, brow, sums1, sums2, sums3, out_other,
    dq, dq_x, dkb, dkb_x, dvb, dvb_x, keep, send, out_all,
    qx, kx, vx, ox, do, do_x, delta, delta_x, dk, dk_x, dv, dv_x, r_scr, grad_t, in_t, sums, all_sums, sums_t, grads, *, chunk,
):
    blocks = x.shape[0] // QB
    for ref in (sums, all_sums, dk, dk_x, dv, dv_x):
        ref[...] = jnp.zeros_like(ref)
    need(mine, sib, oo)
    unpack_square(mine, sib, (qx, kx, vx, ox))

    @pl.loop(0, x.chunks)
    def _(i):
        rows = rows_at(i, MB)
        for argument in (d_pre1, x, mixed, mixed_x):
            argument.need(i)
        grad = d_pre1[rows, :]
        low = grad.astype(BF16)
        block = x[rows, :]
        put_transposed(rows, low, grad_t, chunk)
        put_transposed(rows, block, in_t, chunk)
        attention_grads(low, rows, ((do, oo, mixed, delta), (do_x, ox, mixed_x, delta_x)))
        add_sum(sums, 0, grad * block.astype(F32))

    need(q, k, v, q_x, k_x, v_x, lse, lse_x, brow, sums1, sums2, sums3, out_other)
    out_all.copy_from(out_other.ref)

    @pl.loop(0, blocks)
    def _(i):
        groups = (
            (q, k, v, do, lse, delta, dq, dk, dv), (q_x, k_x, v_x, do_x, lse_x, delta_x, dq_x, dk_x, dv_x)
        )
        attend_back_units(backward_units(sc, brow, i, 0, groups), r_scr)

    for low, wide in ((dkb, dk), (dkb_x, dk_x), (dvb, dv), (dvb_x, dv_x)):
        low[...] = wide[...].astype(BF16)
    for row, source in enumerate(
        (sums1[1:2, :], sums2[0:1, :], sums3[0:1, :], sums1[2:3, :], sums2[1:2, :], sums3[1:2, :], sums[0:1, :],
         sums1[0:1, :], sums3[2:3, :])
    ):
        all_sums[row : row + 1, :] = source
    put_transposed(pl.ds(0, QB), all_sums[...].astype(BF16), sums_t, chunk)
    weight_grads(((in_t, dq, dq_x), (in_t, dkb, dkb_x), (in_t, dvb, dvb_x), (grad_t, mixed, mixed_x)), grads)
    width = grads.shape[1] // 2
    for side in range(2):
        grads[:, (side + 1) * width - QB : (side + 1) * width] = sums_t[...]
    put_grads(grads, keep, send)


def input_backward(
    sc, mine, sib, qo, ko, vo, omega, d_pre1, dq, dq_x, dk, dk_x, dv, dv_x, mem_other, in_all, in_send, mem_all,
    qx, kx, vx, ox,
):
    need(mine, sib, qo, ko, vo, omega)
    unpack_square(mine, sib, (qx, kx, vx, ox))
    half = qo.shape[1]
    tensor = lax.axis_index("tensor")

    @pl.loop(0, d_pre1.chunks)
    def _(i):
        rows = rows_at(i, MB)
        for argument in (d_pre1, dq, dq_x, dk, dk_x, dv, dv_x):
            argument.need(i)

        def part(side):
            which = rows_at(side, half)
            total = omega[0:1, which] * d_pre1[rows, which]
            for grad, weight in ((dq, qo), (dq_x, qx), (dk, ko), (dk_x, kx), (dv, vo), (dv_x, vx)):
                total = total + nt(grad[rows, :], weight[which, :])
            return total

        in_all[rows, :] = part(tensor)
        in_send[rows, :] = part(1 - tensor).astype(BF16)
        in_all.put(i)
        in_send.put(i)

    need(mem_other)
    mem_all[...] = mem_other[...].astype(F32)


def fill_kernel(sc, other, out):
    @pl.loop(0, other.chunks)
    def _(i):
        other.need(i)
        rows = rows_at(i, other.shape[0] // other.chunks)
        out[rows, :] = other[rows, :].astype(out.dtype)
        out.put(i)


def finish(
    sc, own_f, own_c, late, s0, s1, s2, s3, sq, sk, sv, so, cq, ck, cv, co, win, wout, gain, shift, omega
):
    need(own_f, own_c, late, s0, s1, s2, s3)
    half, hidden = sq.shape[1], win.shape[1]

    def late_sum(own, first, base, width):
        return own[:, first : first + width].astype(F32) + late[:, base + first : base + first + width].astype(F32)

    wout[...] = late_sum(own_f, 0, 0, hidden)
    win[...] = late_sum(own_f, hidden, 0, hidden)
    for n, out in enumerate((cq, ck, cv, co)):
        out[...] = late_sum(own_c, n * half, 2 * hidden, half)

    def soon_sum(first, width):
        cols = slice(first, first + width)
        return (s0[:, cols].astype(F32) + s1[:, cols].astype(F32)) + (s2[:, cols].astype(F32) + s3[:, cols].astype(F32))

    for n, out in enumerate((sq, sk, sv, so)):
        out[...] = soon_sum(n * half, half)
    sums = jnp.transpose(soon_sum(4 * half, QB))
    for n, out in enumerate((gain, shift, omega)):
        out[...] = sums[3 * n : 3 * n + 3]


class Buffer:
    def __init__(self, ref, far, sems, chunks):
        self.ref, self.far, self.sems, self.chunks = ref, far, sems, chunks
        self.shape, self.dtype = far.shape, far.dtype

    def __getitem__(self, index):
        return self.ref[index]

    def __setitem__(self, index, value):
        self.ref[index] = value

    def chunk(self, i):
        size = self.shape[0] // self.chunks
        if self.chunks == 1:
            return self.ref, self.far
        rows = rows_at(i, size)
        return self.ref.at[rows], self.far.at[rows]

    def load(self):
        for i in range(self.chunks):
            near, far = self.chunk(i)
            pltpu.make_async_copy(far, near, self.sems.at[i]).start()

    def need(self, i):
        near, far = self.chunk(i)
        pltpu.make_async_copy(far, near, self.sems.at[i]).wait()

    def put(self, i=0):
        near, far = self.chunk(i)
        pltpu.make_async_copy(near, far, self.sems.at[0]).start()

    def copy_part(self, near, first):
        far = self.far.at[first : first + near.shape[0]]
        pltpu.make_async_copy(near, far, self.sems.at[0]).start()

    def copy_from(self, near):
        pltpu.make_async_copy(near, self.far, self.sems.at[0]).start()

    def done(self):
        pltpu.make_async_copy(self.far, self.far, self.sems.at[0]).wait()


def need(*buffers):
    for buffer in buffers:
        for i in range(buffer.chunks):
            buffer.need(i)


def call(
    body, sc, args, outs, scratch, us, picks=None, puts=None, alias=None, cuts=None, out_cuts=None, bare=(), dealt=True,
    full=False,
):
    picks, puts, cuts, out_cuts = picks or {}, puts or {}, cuts or {}, out_cuts or {}

    def block(ref, pick):
        if pick is None:
            return ref
        rows, other = pick
        place = lax.axis_index("tensor")
        return ref.at[rows_at(1 - place if other else place, rows)]

    def size(shape, pick):
        return shape if pick is None else (pick[0], *shape[1:])

    alias = alias or {}
    loads = [n for n in range(len(args)) if n not in alias]
    buffers = [
        *[(size(args[n].shape, picks.get(n)), args[n].dtype) for n in loads],
        *[(size(shape, puts.get(n)), kind) for n, (shape, kind) in enumerate(outs) if n not in bare],
        *scratch,
    ]
    room = sum(math.prod(shape[:-1]) * max(shape[-1], 128) * jnp.dtype(kind).itemsize for shape, kind in buffers)

    def kernel(sc, *refs):
        refs = list(refs)
        ins = [refs.pop(0) for _ in args]
        far_outs = [refs.pop(0) for _ in outs]
        near_ins = [refs.pop(0) for _ in loads]
        near_outs = [None if n in bare else refs.pop(0) for n in range(len(outs))]
        in_sems = [refs.pop(0) for _ in loads]
        out_sems = [refs.pop(0) for _ in outs]
        arguments = [
            Buffer(near, block(ins[n], picks.get(n)), sems, cuts.get(n, 1))
            for n, near, sems in zip(loads, near_ins, in_sems)
        ]
        results = [
            Buffer(near, block(far, puts.get(n)), sems, out_cuts.get(n, 1))
            for n, (far, near, sems) in enumerate(zip(far_outs, near_outs, out_sems))
        ]
        for result in results:
            result.dealt = dealt
        for argument in arguments:
            argument.load()
        body(sc, *arguments, *results, *refs)
        for n, result in enumerate(results):
            if n not in out_cuts and n not in bare:
                result.put()
        for result in results:
            result.done()

    return pl.pallas_call(
        kernel,
        out_shape=[jax.ShapeDtypeStruct(shape, kind) for shape, kind in outs],
        grid_spec=pltpu.PrefetchScalarGridSpec(
            num_scalar_prefetch=1,
            grid=(1,),
            in_specs=[pl.BlockSpec(memory_space=pl.ANY)] * len(args),
            out_specs=[pl.BlockSpec(memory_space=pl.ANY)] * len(outs),
            scratch_shapes=[
                *[pltpu.VMEM(shape, kind) for shape, kind in buffers[: len(buffers) - len(scratch)]],
                *[pltpu.SemaphoreType.DMA((cuts.get(n, 1),)) for n in loads],
                *[pltpu.SemaphoreType.DMA((1,)) for _ in outs],
                *[pltpu.VMEM(shape, kind) for shape, kind in scratch],
            ],
        ),
        input_output_aliases={n + 1: out for n, out in alias.items()},
        cost_estimate=pl.CostEstimate(flops=int(us * FLOPS_PER_US), bytes_accessed=1024, transcendentals=0),
        compiler_params=pltpu.CompilerParams(vmem_limit_bytes=FULL if full else room + SPARE),
        name=(body.func if isinstance(body, functools.partial) else body).__name__,
    )(sc, *args)


def pack(weights, outs, moves, segments=None):
    extra = [] if segments is None else list(segments)
    length = extra[0].shape[1] if extra else 0
    ranges = [((8, length), jnp.int32), ((8, 128), jnp.int32)] if extra else []

    def pack_weights(*refs):
        refs = list(refs)
        sources = [refs.pop(0) for _ in weights]
        ids = [refs.pop(0) for _ in extra]
        targets = [refs.pop(0) for _ in outs]
        sem = refs.pop()
        core = core_index()
        copies = []
        for n, (which, rows, first, out, start) in enumerate(moves):
            width = outs[out][0][1]
            copies.append(
                pltpu.make_async_copy(
                    sources[which].at[rows_at(core, rows), first : first + width],
                    targets[out].at[start : start + rows, :],
                    sem.at[n],
                )
            )
        for copy in copies:
            copy.start()
        if ids:
            set_ranges(*ids, *refs)
        for copy in copies:
            copy.wait()

    near = pl.BlockSpec(memory_space=pltpu.VMEM)
    return pl.pallas_call(
        pack_weights,
        out_shape=[jax.ShapeDtypeStruct(shape, kind) for shape, kind in outs + ranges],
        in_specs=[pl.BlockSpec(memory_space=pltpu.HBM)] * len(weights) + [near] * len(extra),
        out_specs=[near] * len(outs + ranges),
        scratch_shapes=[pltpu.SemaphoreType.DMA((len(moves),))],
        cost_estimate=pl.CostEstimate(flops=int(FLOPS_PER_US), bytes_accessed=1024, transcendentals=0),
        compiler_params=pltpu.CompilerParams(vmem_limit_bytes=60 * 1024 * 1024),
        name="pack_weights",
    )(*weights, *extra)


def local(
    inputs, memory, tgt_seg, src_seg, self_query, self_key, self_value, self_out,
    cross_query, cross_key, cross_value, cross_out, ffn_in, ffn_out,
    norm_gain, norm_shift, residual_scale, cotangent, *, n_dp, n_tensor,
):
    d = lax.axis_index("dp")
    t = lax.axis_index("tensor")
    length = tgt_seg.shape[1]
    model = inputs.shape[1]
    half = model // n_tensor
    hidden = ffn_in.shape[1]
    blocks = length // QB
    chunk = model // n_dp
    dealt = chunk % 16 == 0 and n_dp & (n_dp - 1) == 0
    swap_y = [(0, 1), (1, 0)]

    def swap(n_bit):
        return [(i, i ^ n_bit) for i in range(n_dp)]

    def after(value, *others):
        return lax.optimization_barrier((value, others))[0]

    own_s = [self_query, self_key, self_value, self_out]
    own_c = [cross_query, cross_key, cross_value, cross_out]
    own_f = [ffn_in, ffn_out]
    square = ((4 * half, half), BF16)

    def square_moves(base, out):
        part = model // 2
        moves = [(base + n, part, 0, out, n * part) for n in range(3)]
        return moves + [(base + 3, half // 2, n * half, out, 3 * part + n * half // 2) for n in range(n_tensor)]

    (pack_s,) = pack(own_s, [square], square_moves(0, 0))
    tiles = hidden // model
    pack_c, pack_f, brow, sc = pack(
        own_c + own_f, [square, ((tiles * half + hidden // 2, model), BF16)],
        square_moves(0, 0)
        + [(4, model // 2, n * model, 1, n * model // 2) for n in range(tiles)]
        + [(5, hidden // 2, 0, 1, tiles * model // 2)],
        (tgt_seg, src_seg),
    )
    mine_s = lax.ppermute(pack_s, "tensor", swap_y)

    def fill(whole, other):
        (result,) = call(
            fill_kernel, sc, [whole, other], [(whole.shape, whole.dtype)], [], 1, None, {0: (length, True)}, {0: 0},
            cuts={1: 4}, out_cuts={0: 4},
        )
        return result

    def total(*parts):
        result = parts[0].astype(F32)
        for part in parts[1:]:
            result = result + part.astype(F32)
        return result

    size = model // 4

    def part_total(n, *arrays):
        return total(*[array[n * size : (n + 1) * size] for array in arrays]).astype(BF16)

    def z_send(part):
        far = n_dp // 4
        row = d // 4
        part = part.reshape(far, chunk, -1)
        parts = [lax.dynamic_index_in_dim(part, row, 0, keepdims=False)]
        for step in range(1, far):
            perm = [(i, i % 4 + (i // 4 + step) % far * 4) for i in range(n_dp)]
            out = lax.dynamic_index_in_dim(part, (row + step) % far, 0, keepdims=False)
            parts.append(lax.ppermute(out, "dp", perm))
        return parts

    def reduce_any(keep, send):
        grad = lax.psum_scatter(jnp.concatenate([keep, send]).astype(F32), "dp", scatter_dimension=0, tiled=True)
        width = grad.shape[1] // 2
        return grad[:, :width] + lax.ppermute(grad[:, width:], "tensor", swap_y)

    wide, side = (length, model), (length, half)
    heads = GW // HEAD_DIM
    group = [(side, BF16)] * 4 + [((half // HEAD_DIM, length), F32)]
    square_weights = [((model, half), BF16)] * 3 + [((half, model), BF16)]
    stats = [(wide, F32), ((length, 128), F32)]
    attend_scratch = [
        ((2, length, heads * QB), F32),
        ((2, heads * QB), F32),
        ((2, heads * QB), F32),
        ((2, GW, heads * QB), F32),
    ]
    block_wide = ((MB, model), F32)
    cut = length // MB
    norms = [norm_gain, norm_shift, residual_scale]
    s_own = call(
        self_forward_own, sc, [*own_s[:3], inputs, brow], group, attend_scratch, 7, {3: (length, False)},
        cuts={3: cut}, out_cuts={0: cut, 1: cut, 2: cut},
    )
    s_own, mine_s = lax.optimization_barrier((s_own, mine_s))
    sib_s = lax.ppermute(mine_s, "dp", swap(1))
    mine_c = lax.ppermute(after(pack_c, mine_s), "tensor", swap_y)
    s_rest_stats = call(
        self_forward_rest, sc, [mine_s, sib_s, inputs, brow, s_own[3], self_out, residual_scale], group + stats,
        [*square_weights, block_wide, *attend_scratch], 8, {2: (length, False)},
        cuts={2: cut}, out_cuts={n: cut for n in (0, 1, 2, 5, 6)},
    )
    s_rest_stats, mine_c = lax.optimization_barrier((s_rest_stats, mine_c))
    *s_rest, xhat1, rstd1 = s_rest_stats
    sib_c = lax.ppermute(mine_c, "dp", swap(1))
    mine_f = lax.ppermute(after(pack_f, mine_c), "tensor", swap_y)
    c_stats = call(
        cross_forward, sc,
        [mine_c, sib_c, *own_c[:3], norm_gain, norm_shift, xhat1, memory, brow, cross_out, residual_scale],
        group + group + stats,
        [*square_weights, block_wide, *attend_scratch], 14, {8: (length, False)}, cuts={7: cut, 8: cut},
        out_cuts={n: cut for n in (0, 1, 2, 5, 6, 7, 10, 11)},
    )
    *c_state, xhat2, rstd2 = c_stats
    sums_shape = ((8, model), F32)
    low_side, low_wide = ((length, hidden), BF16), ((length, n_tensor * hidden), BF16)
    f_weights = [((model, hidden), BF16), ((hidden, model), BF16)]
    f_own, mine_f = lax.optimization_barrier((
        call(
            ffn_forward_own, sc, [ffn_in, norm_gain, norm_shift, xhat2, ffn_out, residual_scale],
            [low_side, low_side, (wide, F32)], [], 8, cuts={3: cut}, out_cuts={n: cut for n in range(3)},
        ),
        mine_f,
    ))
    act_own, slope_own, pre_own = f_own
    sib_f = lax.ppermute(mine_f, "dp", swap(1))

    def grads(width, parts=2):
        return [((parts * size, 4 * width // parts), BF16)] * 2

    def core_swap(send):
        return lax.ppermute(send, "dp", swap(1)) if dealt else send

    turned = ((model, length), BF16)
    chunk_rows = chunk if dealt else model // 4
    out_row, output, slope_rest, d_pre3, f1_keep, f1_send, sums3 = call(
        functools.partial(ffn_forward_rest, chunk=chunk_rows), sc,
        [mine_f, sib_f, norm_gain, norm_shift, xhat2, pre_own, cotangent, act_own],
        [(wide, BF16), ((n_tensor * length, model), BF16), low_side, (wide, F32), *grads(hidden), sums_shape],
        [low_side, *f_weights, turned, ((model, 2 * hidden), BF16)], 11,
        {6: (length, False)}, {1: (length, False)}, cuts={4: cut, 5: cut, 6: cut}, out_cuts={n: cut for n in range(4)},
        bare=(4, 5), dealt=dealt,
    )
    out_other = lax.ppermute(out_row, "tensor", swap_y)
    f1_other = core_swap(f1_send)
    back, f1_other = lax.optimization_barrier((
        call(
            functools.partial(ffn_backward, chunk=chunk_rows), sc,
            [ffn_out, ffn_in, *norms, d_pre3, slope_own, xhat2, slope_rest, mine_f, sib_f, rstd2],
            [(wide, F32), *grads(hidden), sums_shape],
            [low_wide, turned, *f_weights, block_wide, ((model, 2 * hidden), BF16)], 12,
            cuts={n: cut for n in (5, 6, 7, 8, 11)}, out_cuts={0: cut}, bare=(1, 2), dealt=dealt,
        ),
        f1_other,
    ))
    d_pre2, f2_keep, f2_send, sums2 = back
    f2_other = core_swap(f2_send)
    if dealt:
        f_there = jnp.concatenate([part_total(1, f1_keep, f1_other), part_total(1, f2_keep, f2_other)], axis=1)
        d_pre2 = after(d_pre2, f_there)
        f_x = lax.ppermute(f_there, "dp", swap(2))
    else:
        f_x = sums2
    logs = ((half // HEAD_DIM, length), F32)
    halves = [((n_tensor * length, half), F32), (side, BF16)]
    back, f_x, out_other = lax.optimization_barrier((
        call(
            functools.partial(cross_backward, chunk=chunk_rows), sc,
            [mine_c, sib_c, cross_out, *norms, d_pre2, xhat1, memory, c_state[3], c_state[8],
             *c_state[:3], *c_state[5:8], c_state[4], c_state[9], brow, *own_c[:3], rstd1],
            [(wide, F32), *halves, *grads(4 * half), sums_shape],
            [*square_weights, *[(side, BF16)] * 2, logs, logs, *[(side, BF16)] * 2, *[(side, F32)] * 4,
             *[(side, BF16)] * 4, ((2, heads * QB, GW), F32), turned, turned, turned, block_wide,
             ((model, 8 * half), BF16)],
            23, {8: (length, False)}, {1: (length, False)}, cuts={n: cut for n in range(6, 11)},
            out_cuts={n: cut for n in range(3)}, bare=(3, 4), dealt=dealt, full=True,
        ),
        f_x, out_other,
    ))
    d_pre1, memory_grad, mem_send, c_keep, c_send, sums1 = back
    mem_other = lax.ppermute(mem_send, "tensor", swap_y)
    c_other = core_swap(c_send)
    c_x, f_z = sums1, sums1
    if dealt:
        f_part = jnp.concatenate(
            [
                part_total(
                    0, keep[:, first : first + hidden], other[:, first : first + hidden],
                    f_x[:, base + first : base + first + hidden],
                )
                for first in (0, hidden)
                for keep, other, base in ((f1_keep, f1_other, 0), (f2_keep, f2_other, 2 * hidden))
            ],
            axis=1,
        )
        f_z = z_send(f_part)
        c_there = part_total(1, c_keep, c_other)
        c_x = lax.ppermute(c_there, "dp", swap(2))
        d_pre1 = after(d_pre1, c_there, f_part)
    back, c_x, mem_other = lax.optimization_barrier((
        call(
            functools.partial(self_backward, chunk=chunk_rows), sc,
            [mine_s, sib_s, self_out, d_pre1, inputs, s_own[3], s_rest[3], *s_own[:3],
             *s_rest[:3], s_own[4], s_rest[4], brow, sums1, sums2, sums3, out_other, output],
            [*[(side, BF16)] * 6, *grads(4 * half + QB, 4 if dealt else 2), (output.shape, BF16)],
            [*square_weights, *[(side, BF16)] * 2, logs, logs, *[(side, F32)] * 4,
             ((2, heads * QB, GW), F32), turned, turned, ((8, model), F32), ((QB, model), F32), ((model, QB), BF16),
             ((model, 2 * (4 * half + QB)), BF16)],
            16, {4: (length, False)}, {8: (length, True)}, {20: 8}, cuts={n: cut for n in range(3, 7)},
            bare=(6, 7, 8), dealt=dealt,
        ),
        c_x, mem_other,
    ))
    *d_self, s_keep, s_send, output = back
    s_other = core_swap(s_send)
    if dealt:
        across = [(i * 2 + j, (i ^ 2) * 2 + 1 - j) for i in range(n_dp) for j in range(2)]
        s_near = [part_total(n, s_keep, s_other) for n in range(1, 4)]
        f_last = total(*f_z).astype(BF16)
        c_part = part_total(0, c_keep, c_other, c_x)
        d_self[0] = after(d_self[0], *s_near, f_last, c_part)
        s_near = [
            lax.ppermute(s_near[0], "tensor", swap_y), lax.ppermute(s_near[1], "dp", swap(2)),
            lax.ppermute(s_near[2], ("dp", "tensor"), across),
        ]
    input_grad, in_send, memory_grad = call(
        input_backward, sc,
        [mine_s, sib_s, *own_s[:3], residual_scale, d_pre1, *d_self, mem_other, memory_grad],
        [*halves, (memory_grad.shape, F32)], square_weights, 5, None, {0: (length, False), 2: (length, True)},
        {14: 2}, cuts={n: cut for n in range(6, 13)}, out_cuts={0: cut, 1: cut},
    )
    thin, broad = ((chunk, half), F32), ((chunk, hidden), F32)
    three = ((3, chunk), F32)
    if dealt:
        in_send, c_part = lax.optimization_barrier((in_send, c_part))
        in_other = lax.ppermute(in_send, "tensor", swap_y)
        c_z = z_send(c_part)
        in_other, c_z = lax.optimization_barrier((in_other, c_z))
        s_far = z_send(part_total(0, s_keep, s_other, *s_near))
        c_last = total(*c_z).astype(BF16)
        late = lax.ppermute(
            jnp.concatenate([f_last[:, 2 * hidden :], c_last[:, 4 * half :]], axis=1), "tensor", swap_y
        )
        while len(s_far) < 4:
            s_far.append(jnp.zeros_like(s_far[0]))
        s_far = [*s_far[:3], s_far[3] if len(s_far) == 4 else total(*s_far[3:]).astype(BF16)]
        input_grad = fill(input_grad, in_other)
        sq, sk, sv, so, cq, ck, cv, co, ffn_in_grad, ffn_out_grad, gain_grad, shift_grad, scale_grad = call(
            finish, sc, [f_last, c_last, late, *s_far], [*[thin] * 8, broad, broad, three, three, three], [], 0.01
        )
    else:
        input_grad = fill(input_grad, lax.ppermute(in_send, "tensor", swap_y))
        f1_sum, f2_sum = reduce_any(f1_keep, f1_send), reduce_any(f2_keep, f2_send)
        c_sum, s_sum = reduce_any(c_keep, c_send), reduce_any(s_keep, s_send)
        ffn_in_grad, ffn_out_grad = f2_sum, f1_sum
        cq, ck, cv, co = [c_sum[:, n * half : (n + 1) * half] for n in range(4)]
        sq, sk, sv, so = [s_sum[:, n * half : (n + 1) * half] for n in range(4)]
        gain_grad, shift_grad, scale_grad = [s_sum[:, 4 * half + 3 * n : 4 * half + 3 * n + 3].T for n in range(3)]
    return (
        output, input_grad, memory_grad, sq, sk, sv, so.T, cq, ck, cv, co.T, ffn_in_grad, ffn_out_grad.T,
        gain_grad, shift_grad, scale_grad,
    )


def solution(mesh):
    rows, cols = P("dp", None), P(None, "tensor")
    both, turned = P("dp", "tensor"), P("tensor", "dp")
    return jax.shard_map(
        functools.partial(local, n_dp=mesh.shape["dp"], n_tensor=mesh.shape["tensor"]),
        mesh=mesh,
        in_specs=(
            rows, rows, rows, rows, cols, cols, cols, turned_rows(), cols, cols, cols, turned_rows(), cols,
            turned_rows(), P(), P(), P(), rows,
        ),
        out_specs=(
            rows, both, both, both, both, both, turned, both, both, both, turned, both, turned,
            P(None, "dp"), P(None, "dp"), P(None, "dp"),
        ),
        check_vma=False,
    )


def turned_rows():
    return P("tensor", None)
```

```python
import functools
import math

import jax
import jax.numpy as jnp
from jax import lax
from jax.experimental import pallas as pl
from jax.experimental.pallas import tpu as pltpu
from jax.sharding import PartitionSpec as P

HEAD_DIM = 64
QB = 128
KC = 256
XC = 128
GW = 256
EPS = 1e-05
NEG = -1e30
F32 = jnp.float32
BF16 = jnp.bfloat16
MB = 512
SPARE = 12 * 1024 * 1024
FULL = 56 * 1024 * 1024
SEGMENTS = 32
FLOPS_PER_US = 5e9


def nn(left, right):
    return lax.dot_general(left, right, (((1,), (0,)), ((), ())), preferred_element_type=F32)


def nt(left, right):
    return lax.dot_general(left, right, (((1,), (1,)), ((), ())), preferred_element_type=F32)


def tn(left, right):
    return lax.dot_general(left, right, (((0,), (0,)), ((), ())), preferred_element_type=F32)


def iota(shape, dim):
    return lax.broadcasted_iota(jnp.int32, shape, dim)


def normalise(pre):
    center = jnp.mean(pre, axis=-1, keepdims=True)
    centered = pre - center
    rstd = lax.rsqrt(jnp.mean(centered * centered, axis=-1, keepdims=True) + EPS)
    return centered * rstd, rstd


def norm_back(grad, gain, xhat, rstd):
    scaled = grad * gain
    first = jnp.mean(scaled, axis=-1, keepdims=True)
    second = jnp.mean(scaled * xhat, axis=-1, keepdims=True)
    return rstd * (scaled - first - xhat * second)


def rows_at(block, size):
    return pl.ds(pl.multiple_of(block * size, size), size)


def stack_heads(block):
    head = iota((1, GW), 1) // HEAD_DIM
    return jnp.concatenate(
        [block * (head == h).astype(F32).astype(BF16) for h in range(GW // HEAD_DIM)], axis=0
    )


def unstack_heads(stacked, rows):
    low_half = iota((1, 128), 1) < HEAD_DIM
    tiles = []
    for tile in range(GW // 128):
        cols = slice(tile * 128, tile * 128 + 128)
        first, second = 2 * tile, 2 * tile + 1
        tiles.append(
            jnp.where(
                low_half,
                stacked[first * rows : (first + 1) * rows, cols],
                stacked[second * rows : (second + 1) * rows, cols],
            )
        )
    return jnp.concatenate(tiles, axis=1)


def each_more(units, where, body):
    for count in {id(unit[where]): unit[where] for unit in units}.values():

        @pl.loop(1, count)
        def _(j):
            for n, unit in enumerate(units):
                if unit[where] is count:
                    body(n, j)


def chunk_keys(first, j):
    if isinstance(j, int):
        return pl.ds(pl.multiple_of(first, 16), KC)
    return pl.ds(pl.multiple_of(first + (KC - XC) + j * XC, 16), XC)


def attend_units(units, s_scr, m_scr, l_scr, o_scr):
    heads = GW // HEAD_DIM
    stacks = [stack_heads(q[rows_at(i, QB), :]) for i, q, *_ in units]

    def scores(n, j):
        _, _, k, _, lo, hi, first, _ = units[n]
        keys, place = chunk_keys(first, j), chunk_keys(0, j)
        at = keys.start + iota((keys.size, QB), 0)
        allowed = (at >= lo) & (at < hi)
        s = nt(k[keys, :], stacks[n])
        peaks = []
        for h in range(heads):
            part = slice(h * QB, (h + 1) * QB)
            masked = jnp.where(allowed, s[:, part], NEG)
            s_scr[n, place, part] = masked
            peaks.append(jnp.max(masked, axis=0, keepdims=True))
        return jnp.concatenate(peaks, axis=1)

    for n in range(len(units)):
        m_scr[n : n + 1, :] = scores(n, 0)

    def more_scores(n, j):
        m_scr[n : n + 1, :] = jnp.maximum(m_scr[n : n + 1, :], scores(n, j))

    each_more(units, 7, more_scores)
    peaks = [m_scr[n : n + 1, :] for n in range(len(units))]

    def weigh(n, j):
        p = jnp.exp(s_scr[n, chunk_keys(0, j), :] - peaks[n])
        return jnp.sum(p, axis=0, keepdims=True), tn(units[n][3][chunk_keys(units[n][6], j), :], p.astype(BF16))

    for n in range(len(units)):
        l_scr[n : n + 1, :], o_scr[n] = weigh(n, 0)

    def more_weights(n, j):
        more_l, more_o = weigh(n, j)
        l_scr[n : n + 1, :] = l_scr[n : n + 1, :] + more_l
        o_scr[n] = o_scr[n] + more_o

    each_more(units, 7, more_weights)
    results = []
    for n in range(len(units)):
        total = l_scr[n : n + 1, :]
        log = peaks[n] + jnp.log(total)
        scale = 1.0 / total
        parts = [
            o_scr[n, h * HEAD_DIM : (h + 1) * HEAD_DIM, h * QB : (h + 1) * QB] * scale[:, h * QB : (h + 1) * QB]
            for h in range(heads)
        ]
        mixed = jnp.transpose(jnp.concatenate(parts, axis=0).astype(BF16))
        results.append((mixed, [log[:, h * QB : (h + 1) * QB] for h in range(heads)]))
    return results


def attend_back_units(units, r_scr):
    heads = GW // HEAD_DIM

    def chunk(n, j):
        i, q, k, v, do, lse, delta, lo, hi, first, _, _, dk, dv = units[n]
        rows = rows_at(i, QB)
        keys = chunk_keys(first, j)
        qs = stack_heads(q[rows, :])
        ds = stack_heads(do[rows, :])
        kg = k[keys, :]
        at = keys.start + iota((keys.size, QB), 0)
        allowed = (at >= lo) & (at < hi)
        st = nt(kg, qs)
        dp = nt(v[keys, :], ds)
        probs, grads = [], []
        for h in range(heads):
            part = slice(h * QB, (h + 1) * QB)
            p = jnp.where(allowed, jnp.exp(st[:, part] - lse[h : h + 1, rows]), 0.0)
            probs.append(p.astype(BF16))
            grads.append((p * (dp[:, part] - delta[h : h + 1, rows])).astype(BF16))
        prob = jnp.concatenate(probs, axis=1)
        grad = jnp.concatenate(grads, axis=1)
        dv[keys, :] += nn(prob, ds)
        dk[keys, :] += nn(grad, qs)
        return tn(grad, kg)

    for n in range(len(units)):
        r_scr[n] = chunk(n, 0)

    def more(n, j):
        r_scr[n] = r_scr[n] + chunk(n, j)

    each_more(units, 10, more)
    for n, unit in enumerate(units):
        unit[11][rows_at(unit[0], QB), :] = (unstack_heads(r_scr[n], QB) * HEAD_DIM**-0.5).astype(BF16)


def set_delta(rows, do, mixed, delta_scr):
    heads = do.shape[1] // HEAD_DIM
    product = do.astype(F32) * mixed.astype(F32)
    high = product.astype(BF16)
    rest = (product - high.astype(F32)).astype(BF16)
    pick = (iota((heads, do.shape[1]), 1) // HEAD_DIM == iota((heads, do.shape[1]), 0)).astype(F32).astype(BF16)
    delta_scr[:, rows] = nt(pick, high) + nt(pick, rest)


def put_transposed(rows, block, scr, chunk):
    turned = jnp.transpose(block)
    size = turned.shape[0]
    count = size // chunk
    for n in range(count):
        first = (n % 2 * 2 + n // 2 % 2) * (size // 4) + n // 4 * chunk if chunk else 0
        scr[first : first + chunk, rows] = turned[n * chunk : (n + 1) * chunk]


def add_sum(ref, row, value):
    ref[row : row + 1, :] += jnp.sum(value, axis=0, keepdims=True)


def project(rows, left, weight, out, factor=1.0):
    out[rows, :] = (nn(left, weight[...]) * factor).astype(BF16)


def unpack_square(mine, sib, weights):
    core = core_index()
    *cols, out = weights
    part, half = cols[0].shape[0] // 2, out.shape[0]
    small = half // 2
    for place, source in ((core, mine), (1 - core, sib)):
        for n, w in enumerate(cols):
            w[rows_at(place, part), :] = source[n * part : (n + 1) * part, :]
        base = len(cols) * part
        for n in range(out.shape[1] // half):
            out[rows_at(place, small), n * half : (n + 1) * half] = source[
                base + n * small : base + (n + 1) * small, :
            ]


def unpack_ffn(mine, sib, win, wout):
    core = core_index()
    part, rows, width = win.shape[0] // 2, wout.shape[0] // 2, wout.shape[1]
    tiles = win.shape[1] // width
    for place, source in ((core, mine), (1 - core, sib)):
        for n in range(tiles):
            win[rows_at(place, part), n * width : (n + 1) * width] = source[n * part : (n + 1) * part, :]
        wout[rows_at(place, rows), :] = source[tiles * part :, :]


def core_index():
    return lax.axis_index("dp") % 2


def set_ranges(tgt, src, brow, blocks):
    rows, length = tgt.shape
    mine = lax.axis_index("tensor")

    def row(ref):
        value = ref[0:1, :]
        for n in range(1, rows):
            value = jnp.where(mine == n, ref[n : n + 1, :], value)
        return value

    target, source = row(tgt), row(src)
    ids = iota((SEGMENTS, length), 0)

    def before(ids_of, limit):
        count = jnp.sum((ids_of < limit).astype(F32), axis=1, keepdims=True)
        return jnp.sum(jnp.where(ids == target, count, 0.0), axis=0, keepdims=True).astype(jnp.int32)

    values = [
        before(target, ids), iota((1, length), 1) + 1, before(source, ids), before(source, ids + 1)
    ]
    lane = iota((1, 128), 1)
    for n, value in enumerate(values):
        brow[n : n + 1, :] = value
        brow[n + 4 : n + 5, :] = value
    blocks[...] = jnp.zeros_like(blocks)
    for n in range(2):
        first = jnp.zeros((1, 128), jnp.int32)
        last = jnp.zeros((1, 128), jnp.int32)
        for i in range(length // QB):
            low, high = values[2 * n][:, i * QB : i * QB + 1], values[2 * n + 1][:, (i + 1) * QB - 1 : (i + 1) * QB]
            first = jnp.where(lane == i, low, first)
            last = jnp.where(lane == i, high, last)
        first = lax.shift_left(lax.shift_right_logical(first, 4), 4)
        more = lax.shift_right_logical(jnp.maximum(last - first - KC, 0) + (XC - 1), XC.bit_length() - 1)
        blocks[2 * n : 2 * n + 1, :] = jnp.minimum(first, length - KC - more * XC)
        blocks[2 * n + 1 : 2 * n + 2, :] = more + 1


def forward_units(sc, brow, i, which, groups):
    rows = rows_at(i, QB)
    first, count = sc[2 * which, i], sc[2 * which + 1, i]
    lo, hi = brow[2 * which : 2 * which + 1, rows], brow[2 * which + 1 : 2 * which + 2, rows]
    return [(i, q, k, v, lo, hi, first, count) for q, k, v in groups]


def put_logs(lse, i, logs):
    for h, log in enumerate(logs):
        lse[h : h + 1, rows_at(i, QB)] = log


def project_self(x, weights, outs):
    @pl.loop(0, x.chunks)
    def _(i):
        x.need(i)
        rows = rows_at(i, MB)
        block = x[rows, :]
        for weight, out, factor in zip(weights, outs, (HEAD_DIM**-0.5, 1.0, 1.0)):
            project(rows, block, weight, out, factor)
            out.put(i)


def self_forward_own(sc, qo, ko, vo, x, brow, q, k, v, mixed, lse, *scratch):
    need(qo, ko, vo)
    project_self(x, (qo, ko, vo), (q, k, v))
    need(brow)

    @pl.loop(0, x.shape[0] // QB // 2)
    def _(pair):
        pair_of = [2 * pair, 2 * pair + 1]
        units = [forward_units(sc, brow, i, 0, [(q, k, v)])[0] for i in pair_of]
        for i, (block, logs) in zip(pair_of, attend_units(units, *scratch)):
            mixed[rows_at(i, QB), :] = block
            put_logs(lse, i, logs)


def norm_rows(i, pre, xhat, rstd):
    @pl.loop(0, MB // QB)
    def _(n):
        rows = rows_at(i * (MB // QB) + n, QB)
        hat, inv = normalise(pre[rows_at(n, QB), :])
        xhat[rows, :] = hat
        rstd[rows, :] = jnp.broadcast_to(inv, (QB, rstd.shape[1]))

    xhat.put(i)
    rstd.put(i)


def self_forward_rest(
    sc, mine, sib, x, brow, mixed_own, oo, omega,
    q, k, v, mixed, lse, xhat, rstd, qx, kx, vx, ox, pre, *scratch,
):
    need(mine, sib)
    unpack_square(mine, sib, (qx, kx, vx, ox))
    project_self(x, (qx, kx, vx), (q, k, v))
    need(brow)

    @pl.loop(0, x.shape[0] // QB // 2)
    def _(pair):
        pair_of = [2 * pair, 2 * pair + 1]
        units = [forward_units(sc, brow, i, 0, [(q, k, v)])[0] for i in pair_of]
        for i, (block, logs) in zip(pair_of, attend_units(units, *scratch)):
            mixed[rows_at(i, QB), :] = block
            put_logs(lse, i, logs)

    need(mixed_own, oo, omega)

    @pl.loop(0, x.chunks)
    def _(i):
        rows = rows_at(i, MB)
        branch = nn(mixed_own[rows, :], oo[...]) + nn(mixed[rows, :], ox[...])
        pre[...] = omega[0:1] * x[rows, :].astype(F32) + branch
        norm_rows(i, pre, xhat, rstd)


def cross_forward(
    sc, mine, sib, qo, ko, vo, gain, shift, xhat1, mem, brow, oo, omega,
    q, k, v, mixed, lse, q_x, k_x, v_x, mixed_x, lse_x, xhat, rstd, qx, kx, vx, ox, pre, *scratch,
):
    need(mine, sib, qo, ko, vo, gain, shift)
    unpack_square(mine, sib, (qx, kx, vx, ox))

    @pl.loop(0, mem.chunks)
    def _(i):
        rows = rows_at(i, MB)
        xhat1.need(i)
        mem.need(i)
        low1 = (xhat1[rows, :] * gain[0:1] + shift[0:1]).astype(BF16)
        block = mem[rows, :]
        for weights, outs in (((qo, ko, vo), (q, k, v)), ((qx, kx, vx), (q_x, k_x, v_x))):
            project(rows, low1, weights[0], outs[0], HEAD_DIM**-0.5)
            project(rows, block, weights[1], outs[1])
            project(rows, block, weights[2], outs[2])
            for result in outs:
                result.put(i)

    need(brow)

    @pl.loop(0, mem.shape[0] // QB)
    def _(i):
        units = forward_units(sc, brow, i, 1, ((q, k, v), (q_x, k_x, v_x)))
        for (block, logs), out, lse_out in zip(attend_units(units, *scratch), (mixed, mixed_x), (lse, lse_x)):
            out[rows_at(i, QB), :] = block
            put_logs(lse_out, i, logs)

    need(oo, omega)

    @pl.loop(0, mem.chunks)
    def _(i):
        rows = rows_at(i, MB)
        branch = nn(mixed[rows, :], oo[...]) + nn(mixed_x[rows, :], ox[...])
        pre[...] = omega[1:2] * (xhat1[rows, :] * gain[0:1] + shift[0:1]) + branch
        norm_rows(i, pre, xhat, rstd)


def hidden_units(rows, low2, win, act, slope, width=512):
    for first in range(0, win.shape[1], width):
        place = slice(first, first + width)
        u = nn(low2, win[:, place])
        square = u * u
        t = jnp.tanh(u * (0.7978845608028654 + (0.7978845608028654 * 0.044715) * square))
        h = 0.5 + 0.5 * t
        a = u * h
        act[rows, place] = a.astype(BF16)
        steep = 2 * 0.7978845608028654 + (6 * 0.7978845608028654 * 0.044715) * square
        slope[rows, place] = (h + a * (1.0 - h) * steep).astype(BF16)


def ffn_forward_own(sc, io, gain, shift, xhat2, oo, omega, act, slope, pre):
    need(io, gain, shift)

    @pl.loop(0, xhat2.chunks)
    def _(i):
        rows = rows_at(i, MB)
        xhat2.need(i)
        norm2 = xhat2[rows, :] * gain[1:2] + shift[1:2]
        hidden_units(rows, norm2.astype(BF16), io, act, slope)
        act.put(i)
        slope.put(i)

    need(oo, omega)

    @pl.loop(0, xhat2.chunks)
    def _(i):
        rows = rows_at(i, MB)
        norm2 = xhat2[rows, :] * gain[1:2] + shift[1:2]
        pre[rows, :] = omega[2:3] * norm2 + nn(act[rows, :], oo[...])
        pre.put(i)


def ffn_forward_rest(
    sc, mine, sib, gain, shift, xhat2, pre, cot, act_own,
    out, out_all, slope, d_pre3, keep, send, sums, act, ix, ox, grad_t, grads, *, chunk,
):
    need(mine, sib, gain, shift)
    unpack_ffn(mine, sib, ix, ox)
    sums[...] = jnp.zeros_like(sums)
    width = 512
    half = ix.shape[1]

    @pl.loop(0, xhat2.chunks)
    def _(i):
        rows = rows_at(i, MB)
        xhat2.need(i)
        hidden_units(rows, (xhat2[rows, :] * gain[1:2] + shift[1:2]).astype(BF16), ix, act, slope)
        slope.put(i)
        pre.need(i)
        cot.need(i)
        pre[rows, :] += nn(act[rows, :], ox[...])

        @pl.loop(0, MB // QB)
        def _(n):
            small = rows_at(i * (MB // QB) + n, QB)
            hat, inv = normalise(pre[small, :])
            result = (hat * gain[2:3] + shift[2:3]).astype(BF16)
            out[small, :] = result
            out_all[small, :] = result
            grad = cot[small, :].astype(F32)
            d_pre = norm_back(grad, gain[2:3], hat, inv)
            d_pre3[small, :] = d_pre
            put_transposed(small, d_pre.astype(BF16), grad_t, chunk)
            add_sum(sums, 0, grad * hat)
            add_sum(sums, 1, grad)
            add_sum(sums, 2, d_pre * (xhat2[small, :] * gain[1:2] + shift[1:2]))

        for result in (out, out_all, d_pre3):
            result.put(i)

    need(act_own)
    for side, right in enumerate((act_own, act)):
        for first in range(0, half, width):
            grads[:, side * half + first : side * half + first + width] = nn(
                grad_t[...], right[:, first : first + width]
            ).astype(BF16)
    put_grads(grads, keep, send)


def put_grads(scr, keep, send):
    dp = lax.axis_index("dp")
    core, x = (dp % 2, dp // 2 % 2) if keep.dealt else (0, 0)
    size, width = scr.shape[0] // 4, keep.shape[1]
    parts = keep.shape[0] // size
    for out, row in ((keep, core), (send, 1 - core)):
        for n in range(parts):
            side = n * 2 // parts
            first = n % 2 * width if parts == 4 else 0
            place = row * 2 + (x if side == 0 else 1 - x)
            out.copy_part(scr.at[rows_at(place, size), first : first + width], n * size)


def ffn_backward(
    sc, oo, io, gain, shift, omega, d_pre3, slope_own, xhat2, slope_rest, mine, sib, rstd2,
    d_pre2, keep, send, sums, up_scr, norm_t, ix, ox, acc, grads, *, chunk,
):
    need(io, oo, gain, shift, omega, mine, sib)
    unpack_ffn(mine, sib, ix, ox)
    sums[...] = jnp.zeros_like(sums)
    half = io.shape[1]
    width = 512

    @pl.loop(0, xhat2.chunks)
    def _(i):
        rows = rows_at(i, MB)
        for argument in (d_pre3, slope_own, xhat2, slope_rest):
            argument.need(i)
        grad = d_pre3[rows, :]
        low = grad.astype(BF16)
        acc[...] = omega[2:3] * grad
        for side, (win, wout, slope) in enumerate(((io, oo, slope_own), (ix, ox, slope_rest))):
            for first in range(0, half, width):
                place = slice(side * half + first, side * half + first + width)
                up_scr[rows, place] = (
                    slope[rows, first : first + width].astype(F32) * nt(low, wout[first : first + width, :])
                ).astype(BF16)
            acc[...] += nt(up_scr[rows, side * half : (side + 1) * half], win[...])

        rstd2.need(i)

        @pl.loop(0, MB // QB)
        def _(n):
            small = rows_at(i * (MB // QB) + n, QB)
            total = acc[rows_at(n, QB), :]
            hat = xhat2[small, :]
            put_transposed(small, (hat * gain[1:2] + shift[1:2]).astype(BF16), norm_t, chunk)
            d_pre2[small, :] = norm_back(total, gain[1:2], hat, rstd2[small, 0:1])
            add_sum(sums, 0, total * hat)
            add_sum(sums, 1, total)

        d_pre2.put(i)

    for first in range(0, 2 * half, width):
        grads[:, first : first + width] = nn(norm_t[...], up_scr[:, first : first + width]).astype(BF16)
    put_grads(grads, keep, send)


def weight_grads(pairs, grads):
    width = grads.shape[1] // 2
    for n, (left, *rights) in enumerate(pairs):
        for side, right in enumerate(rights):
            half = right.shape[1]
            first = side * width + n * half
            grads[:, first : first + half] = nn(left[...], right[...]).astype(BF16)


def backward_units(sc, brow, i, which, groups):
    rows = rows_at(i, QB)
    first, count = sc[2 * which, i], sc[2 * which + 1, i]
    lo, hi = brow[2 * which : 2 * which + 1, rows], brow[2 * which + 1 : 2 * which + 2, rows]
    return [(i, *group[:6], lo, hi, first, count, *group[6:]) for group in groups]


def attention_grads(low, rows, outs):
    for out, weight, was, total in outs:
        value = nt(low, weight[...]).astype(BF16)
        out[rows, :] = value
        set_delta(rows, value, was[rows, :], total)


def cross_backward(
    sc, mine, sib, oo, gain, shift, omega, d_pre2, xhat1, mem, mixed, mixed_x, q, k, v, q_x, k_x, v_x, lse, lse_x,
    brow, qo, ko, vo, rstd1,
    d_pre1, mem_all, mem_send, keep, send, sums,
    qx, kx, vx, ox, do, do_x, delta, delta_x, dq, dq_x, dk, dk_x, dv, dv_x, dkb, dkb_x, dvb, dvb_x, r_scr,
    grad_t, norm_t, mem_t, acc, grads, *, chunk,
):
    half = qo.shape[1]
    blocks = mem.shape[0] // QB
    for ref in (sums, dk, dk_x, dv, dv_x):
        ref[...] = jnp.zeros_like(ref)
    need(mine, sib, oo, gain, shift, omega)
    unpack_square(mine, sib, (qx, kx, vx, ox))

    @pl.loop(0, mem.chunks)
    def _(i):
        rows = rows_at(i, MB)
        for argument in (d_pre2, xhat1, mem, mixed, mixed_x):
            argument.need(i)
        grad = d_pre2[rows, :]
        low = grad.astype(BF16)
        norm1 = xhat1[rows, :] * gain[0:1] + shift[0:1]
        put_transposed(rows, low, grad_t, chunk)
        put_transposed(rows, norm1.astype(BF16), norm_t, chunk)
        put_transposed(rows, mem[rows, :], mem_t, chunk)
        attention_grads(low, rows, ((do, oo, mixed, delta), (do_x, ox, mixed_x, delta_x)))
        add_sum(sums, 0, grad * norm1)

    need(q, k, v, q_x, k_x, v_x, lse, lse_x, brow)

    @pl.loop(0, blocks // 2)
    def _(pair):
        groups = (
            (q, k, v, do, lse, delta, dq, dk, dv), (q_x, k_x, v_x, do_x, lse_x, delta_x, dq_x, dk_x, dv_x)
        )
        units = []
        for i in (2 * pair, 2 * pair + 1):
            units += backward_units(sc, brow, i, 1, groups)
        attend_back_units(units, r_scr)

    need(qo, ko, vo, rstd1)
    tensor = lax.axis_index("tensor")

    @pl.loop(0, mem.chunks)
    def _(i):
        rows = rows_at(i, MB)
        acc[...] = omega[1:2] * d_pre2[rows, :] + nt(dq[rows, :], qo[...]) + nt(dq_x[rows, :], qx[...])
        for low, wide in ((dkb, dk), (dkb_x, dk_x), (dvb, dv), (dvb_x, dv_x)):
            low[rows, :] = wide[rows, :].astype(BF16)

        def part(side):
            which = rows_at(side, half)
            return (
                nt(dkb[rows, :], ko[which, :]) + nt(dkb_x[rows, :], kx[which, :])
                + nt(dvb[rows, :], vo[which, :]) + nt(dvb_x[rows, :], vx[which, :])
            )

        mem_all[rows, :] = part(tensor)
        mem_send[rows, :] = part(1 - tensor).astype(BF16)

        @pl.loop(0, MB // QB)
        def _(n):
            small = rows_at(i * (MB // QB) + n, QB)
            total = acc[rows_at(n, QB), :]
            hat = xhat1[small, :]
            d_pre1[small, :] = norm_back(total, gain[0:1], hat, rstd1[small, 0:1])
            add_sum(sums, 1, total * hat)
            add_sum(sums, 2, total)

        for result in (d_pre1, mem_all, mem_send):
            result.put(i)

    weight_grads(
        ((norm_t, dq, dq_x), (mem_t, dkb, dkb_x), (mem_t, dvb, dvb_x), (grad_t, mixed, mixed_x)), grads
    )
    put_grads(grads, keep, send)


def self_backward(
    sc, mine, sib, oo, d_pre1, x, mixed, mixed_x, q, k, v, q_x, k_x, v_x, lse, lse_x, brow, sums1, sums2, sums3, out_other,
    dq, dq_x, dkb, dkb_x, dvb, dvb_x, keep, send, out_all,
    qx, kx, vx, ox, do, do_x, delta, delta_x, dk, dk_x, dv, dv_x, r_scr, grad_t, in_t, sums, all_sums, sums_t, grads, *, chunk,
):
    blocks = x.shape[0] // QB
    for ref in (sums, all_sums, dk, dk_x, dv, dv_x):
        ref[...] = jnp.zeros_like(ref)
    need(mine, sib, oo)
    unpack_square(mine, sib, (qx, kx, vx, ox))

    @pl.loop(0, x.chunks)
    def _(i):
        rows = rows_at(i, MB)
        for argument in (d_pre1, x, mixed, mixed_x):
            argument.need(i)
        grad = d_pre1[rows, :]
        low = grad.astype(BF16)
        block = x[rows, :]
        put_transposed(rows, low, grad_t, chunk)
        put_transposed(rows, block, in_t, chunk)
        attention_grads(low, rows, ((do, oo, mixed, delta), (do_x, ox, mixed_x, delta_x)))
        add_sum(sums, 0, grad * block.astype(F32))

    need(q, k, v, q_x, k_x, v_x, lse, lse_x, brow, sums1, sums2, sums3, out_other)
    out_all.copy_from(out_other.ref)

    @pl.loop(0, blocks // 2)
    def _(pair):
        groups = (
            (q, k, v, do, lse, delta, dq, dk, dv), (q_x, k_x, v_x, do_x, lse_x, delta_x, dq_x, dk_x, dv_x)
        )
        units = []
        for i in (2 * pair, 2 * pair + 1):
            units += backward_units(sc, brow, i, 0, groups)
        attend_back_units(units, r_scr)

    for low, wide in ((dkb, dk), (dkb_x, dk_x), (dvb, dv), (dvb_x, dv_x)):
        low[...] = wide[...].astype(BF16)
    for row, source in enumerate(
        (sums1[1:2, :], sums2[0:1, :], sums3[0:1, :], sums1[2:3, :], sums2[1:2, :], sums3[1:2, :], sums[0:1, :],
         sums1[0:1, :], sums3[2:3, :])
    ):
        all_sums[row : row + 1, :] = source
    put_transposed(pl.ds(0, QB), all_sums[...].astype(BF16), sums_t, chunk)
    weight_grads(((in_t, dq, dq_x), (in_t, dkb, dkb_x), (in_t, dvb, dvb_x), (grad_t, mixed, mixed_x)), grads)
    width = grads.shape[1] // 2
    for side in range(2):
        grads[:, (side + 1) * width - QB : (side + 1) * width] = sums_t[...]
    put_grads(grads, keep, send)


def input_backward(
    sc, mine, sib, qo, ko, vo, omega, d_pre1, dq, dq_x, dk, dk_x, dv, dv_x, mem_other, in_all, in_send, mem_all,
    qx, kx, vx, ox,
):
    need(mine, sib, qo, ko, vo, omega)
    unpack_square(mine, sib, (qx, kx, vx, ox))
    half = qo.shape[1]
    tensor = lax.axis_index("tensor")

    @pl.loop(0, d_pre1.chunks)
    def _(i):
        rows = rows_at(i, MB)
        for argument in (d_pre1, dq, dq_x, dk, dk_x, dv, dv_x):
            argument.need(i)

        def part(side):
            which = rows_at(side, half)
            total = omega[0:1, which] * d_pre1[rows, which]
            for grad, weight in ((dq, qo), (dq_x, qx), (dk, ko), (dk_x, kx), (dv, vo), (dv_x, vx)):
                total = total + nt(grad[rows, :], weight[which, :])
            return total

        in_all[rows, :] = part(tensor)
        in_send[rows, :] = part(1 - tensor).astype(BF16)
        in_all.put(i)
        in_send.put(i)

    need(mem_other)
    mem_all[...] = mem_other[...].astype(F32)


def fill_kernel(sc, other, out):
    @pl.loop(0, other.chunks)
    def _(i):
        other.need(i)
        rows = rows_at(i, other.shape[0] // other.chunks)
        out[rows, :] = other[rows, :].astype(out.dtype)
        out.put(i)


def finish(
    sc, own_f, own_c, late, s0, s1, s2, s3, sq, sk, sv, so, cq, ck, cv, co, win, wout, gain, shift, omega
):
    need(own_f, own_c, late, s0, s1, s2, s3)
    half, hidden = sq.shape[1], win.shape[1]

    def late_sum(own, first, base, width):
        return own[:, first : first + width].astype(F32) + late[:, base + first : base + first + width].astype(F32)

    wout[...] = late_sum(own_f, 0, 0, hidden)
    win[...] = late_sum(own_f, hidden, 0, hidden)
    for n, out in enumerate((cq, ck, cv, co)):
        out[...] = late_sum(own_c, n * half, 2 * hidden, half)

    def soon_sum(first, width):
        cols = slice(first, first + width)
        return (s0[:, cols].astype(F32) + s1[:, cols].astype(F32)) + (s2[:, cols].astype(F32) + s3[:, cols].astype(F32))

    for n, out in enumerate((sq, sk, sv, so)):
        out[...] = soon_sum(n * half, half)
    sums = jnp.transpose(soon_sum(4 * half, QB))
    for n, out in enumerate((gain, shift, omega)):
        out[...] = sums[3 * n : 3 * n + 3]


class Buffer:
    def __init__(self, ref, far, sems, chunks):
        self.ref, self.far, self.sems, self.chunks = ref, far, sems, chunks
        self.shape, self.dtype = far.shape, far.dtype

    def __getitem__(self, index):
        return self.ref[index]

    def __setitem__(self, index, value):
        self.ref[index] = value

    def chunk(self, i):
        size = self.shape[0] // self.chunks
        if self.chunks == 1:
            return self.ref, self.far
        rows = rows_at(i, size)
        return self.ref.at[rows], self.far.at[rows]

    def load(self):
        for i in range(self.chunks):
            near, far = self.chunk(i)
            pltpu.make_async_copy(far, near, self.sems.at[i]).start()

    def need(self, i):
        near, far = self.chunk(i)
        pltpu.make_async_copy(far, near, self.sems.at[i]).wait()

    def put(self, i=0):
        near, far = self.chunk(i)
        pltpu.make_async_copy(near, far, self.sems.at[0]).start()

    def copy_part(self, near, first):
        far = self.far.at[first : first + near.shape[0]]
        pltpu.make_async_copy(near, far, self.sems.at[0]).start()

    def copy_from(self, near):
        pltpu.make_async_copy(near, self.far, self.sems.at[0]).start()

    def done(self):
        pltpu.make_async_copy(self.far, self.far, self.sems.at[0]).wait()


def need(*buffers):
    for buffer in buffers:
        for i in range(buffer.chunks):
            buffer.need(i)


def call(
    body, sc, args, outs, scratch, us, picks=None, puts=None, alias=None, cuts=None, out_cuts=None, bare=(), dealt=True,
    full=False,
):
    picks, puts, cuts, out_cuts = picks or {}, puts or {}, cuts or {}, out_cuts or {}

    def block(ref, pick):
        if pick is None:
            return ref
        rows, other = pick
        place = lax.axis_index("tensor")
        return ref.at[rows_at(1 - place if other else place, rows)]

    def size(shape, pick):
        return shape if pick is None else (pick[0], *shape[1:])

    alias = alias or {}
    loads = [n for n in range(len(args)) if n not in alias]
    buffers = [
        *[(size(args[n].shape, picks.get(n)), args[n].dtype) for n in loads],
        *[(size(shape, puts.get(n)), kind) for n, (shape, kind) in enumerate(outs) if n not in bare],
        *scratch,
    ]
    room = sum(math.prod(shape[:-1]) * max(shape[-1], 128) * jnp.dtype(kind).itemsize for shape, kind in buffers)

    def kernel(sc, *refs):
        refs = list(refs)
        ins = [refs.pop(0) for _ in args]
        far_outs = [refs.pop(0) for _ in outs]
        near_ins = [refs.pop(0) for _ in loads]
        near_outs = [None if n in bare else refs.pop(0) for n in range(len(outs))]
        in_sems = [refs.pop(0) for _ in loads]
        out_sems = [refs.pop(0) for _ in outs]
        arguments = [
            Buffer(near, block(ins[n], picks.get(n)), sems, cuts.get(n, 1))
            for n, near, sems in zip(loads, near_ins, in_sems)
        ]
        results = [
            Buffer(near, block(far, puts.get(n)), sems, out_cuts.get(n, 1))
            for n, (far, near, sems) in enumerate(zip(far_outs, near_outs, out_sems))
        ]
        for result in results:
            result.dealt = dealt
        for argument in arguments:
            argument.load()
        body(sc, *arguments, *results, *refs)
        for n, result in enumerate(results):
            if n not in out_cuts and n not in bare:
                result.put()
        for result in results:
            result.done()

    return pl.pallas_call(
        kernel,
        out_shape=[jax.ShapeDtypeStruct(shape, kind) for shape, kind in outs],
        grid_spec=pltpu.PrefetchScalarGridSpec(
            num_scalar_prefetch=1,
            grid=(1,),
            in_specs=[pl.BlockSpec(memory_space=pl.ANY)] * len(args),
            out_specs=[pl.BlockSpec(memory_space=pl.ANY)] * len(outs),
            scratch_shapes=[
                *[pltpu.VMEM(shape, kind) for shape, kind in buffers[: len(buffers) - len(scratch)]],
                *[pltpu.SemaphoreType.DMA((cuts.get(n, 1),)) for n in loads],
                *[pltpu.SemaphoreType.DMA((1,)) for _ in outs],
                *[pltpu.VMEM(shape, kind) for shape, kind in scratch],
            ],
        ),
        input_output_aliases={n + 1: out for n, out in alias.items()},
        cost_estimate=pl.CostEstimate(flops=int(us * FLOPS_PER_US), bytes_accessed=1024, transcendentals=0),
        compiler_params=pltpu.CompilerParams(vmem_limit_bytes=FULL if full else room + SPARE),
        name=(body.func if isinstance(body, functools.partial) else body).__name__,
    )(sc, *args)


def pack(weights, outs, moves, segments=None):
    extra = [] if segments is None else list(segments)
    length = extra[0].shape[1] if extra else 0
    ranges = [((8, length), jnp.int32), ((8, 128), jnp.int32)] if extra else []

    def pack_weights(*refs):
        refs = list(refs)
        sources = [refs.pop(0) for _ in weights]
        ids = [refs.pop(0) for _ in extra]
        targets = [refs.pop(0) for _ in outs]
        sem = refs.pop()
        core = core_index()
        copies = []
        for n, (which, rows, first, out, start) in enumerate(moves):
            width = outs[out][0][1]
            copies.append(
                pltpu.make_async_copy(
                    sources[which].at[rows_at(core, rows), first : first + width],
                    targets[out].at[start : start + rows, :],
                    sem.at[n],
                )
            )
        for copy in copies:
            copy.start()
        if ids:
            set_ranges(*ids, *refs)
        for copy in copies:
            copy.wait()

    near = pl.BlockSpec(memory_space=pltpu.VMEM)
    return pl.pallas_call(
        pack_weights,
        out_shape=[jax.ShapeDtypeStruct(shape, kind) for shape, kind in outs + ranges],
        in_specs=[pl.BlockSpec(memory_space=pltpu.HBM)] * len(weights) + [near] * len(extra),
        out_specs=[near] * len(outs + ranges),
        scratch_shapes=[pltpu.SemaphoreType.DMA((len(moves),))],
        cost_estimate=pl.CostEstimate(flops=int(FLOPS_PER_US), bytes_accessed=1024, transcendentals=0),
        compiler_params=pltpu.CompilerParams(vmem_limit_bytes=60 * 1024 * 1024),
        name="pack_weights",
    )(*weights, *extra)


def local(
    inputs, memory, tgt_seg, src_seg, self_query, self_key, self_value, self_out,
    cross_query, cross_key, cross_value, cross_out, ffn_in, ffn_out,
    norm_gain, norm_shift, residual_scale, cotangent, *, n_dp, n_tensor,
):
    d = lax.axis_index("dp")
    t = lax.axis_index("tensor")
    length = tgt_seg.shape[1]
    model = inputs.shape[1]
    half = model // n_tensor
    hidden = ffn_in.shape[1]
    blocks = length // QB
    chunk = model // n_dp
    dealt = chunk % 16 == 0 and n_dp & (n_dp - 1) == 0
    swap_y = [(0, 1), (1, 0)]

    def swap(n_bit):
        return [(i, i ^ n_bit) for i in range(n_dp)]

    def after(value, *others):
        return lax.optimization_barrier((value, others))[0]

    own_s = [self_query, self_key, self_value, self_out]
    own_c = [cross_query, cross_key, cross_value, cross_out]
    own_f = [ffn_in, ffn_out]
    square = ((4 * half, half), BF16)

    def square_moves(base, out):
        part = model // 2
        moves = [(base + n, part, 0, out, n * part) for n in range(3)]
        return moves + [(base + 3, half // 2, n * half, out, 3 * part + n * half // 2) for n in range(n_tensor)]

    (pack_s,) = pack(own_s, [square], square_moves(0, 0))
    tiles = hidden // model
    pack_c, pack_f, brow, sc = pack(
        own_c + own_f, [square, ((tiles * half + hidden // 2, model), BF16)],
        square_moves(0, 0)
        + [(4, model // 2, n * model, 1, n * model // 2) for n in range(tiles)]
        + [(5, hidden // 2, 0, 1, tiles * model // 2)],
        (tgt_seg, src_seg),
    )
    mine_s = lax.ppermute(pack_s, "tensor", swap_y)

    def fill(whole, other):
        (result,) = call(
            fill_kernel, sc, [whole, other], [(whole.shape, whole.dtype)], [], 1, None, {0: (length, True)}, {0: 0},
            cuts={1: 4}, out_cuts={0: 4},
        )
        return result

    def total(*parts):
        result = parts[0].astype(F32)
        for part in parts[1:]:
            result = result + part.astype(F32)
        return result

    size = model // 4

    def part_total(n, *arrays):
        return total(*[array[n * size : (n + 1) * size] for array in arrays]).astype(BF16)

    def z_send(part):
        far = n_dp // 4
        row = d // 4
        part = part.reshape(far, chunk, -1)
        parts = [lax.dynamic_index_in_dim(part, row, 0, keepdims=False)]
        for step in range(1, far):
            perm = [(i, i % 4 + (i // 4 + step) % far * 4) for i in range(n_dp)]
            out = lax.dynamic_index_in_dim(part, (row + step) % far, 0, keepdims=False)
            parts.append(lax.ppermute(out, "dp", perm))
        return parts

    def reduce_any(keep, send):
        grad = lax.psum_scatter(jnp.concatenate([keep, send]).astype(F32), "dp", scatter_dimension=0, tiled=True)
        width = grad.shape[1] // 2
        return grad[:, :width] + lax.ppermute(grad[:, width:], "tensor", swap_y)

    wide, side = (length, model), (length, half)
    heads = GW // HEAD_DIM
    group = [(side, BF16)] * 4 + [((half // HEAD_DIM, length), F32)]
    square_weights = [((model, half), BF16)] * 3 + [((half, model), BF16)]
    stats = [(wide, F32), ((length, 128), F32)]
    attend_scratch = [
        ((2, length, heads * QB), F32),
        ((2, heads * QB), F32),
        ((2, heads * QB), F32),
        ((2, GW, heads * QB), F32),
    ]
    block_wide = ((MB, model), F32)
    cut = length // MB
    norms = [norm_gain, norm_shift, residual_scale]
    s_own = call(
        self_forward_own, sc, [*own_s[:3], inputs, brow], group, attend_scratch, 7, {3: (length, False)},
        cuts={3: cut}, out_cuts={0: cut, 1: cut, 2: cut},
    )
    s_own, mine_s = lax.optimization_barrier((s_own, mine_s))
    sib_s = lax.ppermute(mine_s, "dp", swap(1))
    mine_c = lax.ppermute(after(pack_c, mine_s), "tensor", swap_y)
    s_rest_stats = call(
        self_forward_rest, sc, [mine_s, sib_s, inputs, brow, s_own[3], self_out, residual_scale], group + stats,
        [*square_weights, block_wide, *attend_scratch], 8, {2: (length, False)},
        cuts={2: cut}, out_cuts={n: cut for n in (0, 1, 2, 5, 6)},
    )
    s_rest_stats, mine_c = lax.optimization_barrier((s_rest_stats, mine_c))
    *s_rest, xhat1, rstd1 = s_rest_stats
    sib_c = lax.ppermute(mine_c, "dp", swap(1))
    mine_f = lax.ppermute(after(pack_f, mine_c), "tensor", swap_y)
    c_stats = call(
        cross_forward, sc,
        [mine_c, sib_c, *own_c[:3], norm_gain, norm_shift, xhat1, memory, brow, cross_out, residual_scale],
        group + group + stats,
        [*square_weights, block_wide, *attend_scratch], 14, {8: (length, False)}, cuts={7: cut, 8: cut},
        out_cuts={n: cut for n in (0, 1, 2, 5, 6, 7, 10, 11)},
    )
    *c_state, xhat2, rstd2 = c_stats
    sums_shape = ((8, model), F32)
    low_side, low_wide = ((length, hidden), BF16), ((length, n_tensor * hidden), BF16)
    f_weights = [((model, hidden), BF16), ((hidden, model), BF16)]
    f_own, mine_f = lax.optimization_barrier((
        call(
            ffn_forward_own, sc, [ffn_in, norm_gain, norm_shift, xhat2, ffn_out, residual_scale],
            [low_side, low_side, (wide, F32)], [], 8, cuts={3: cut}, out_cuts={n: cut for n in range(3)},
        ),
        mine_f,
    ))
    act_own, slope_own, pre_own = f_own
    sib_f = lax.ppermute(mine_f, "dp", swap(1))

    def grads(width, parts=2):
        return [((parts * size, 4 * width // parts), BF16)] * 2

    def core_swap(send):
        return lax.ppermute(send, "dp", swap(1)) if dealt else send

    turned = ((model, length), BF16)
    chunk_rows = chunk if dealt else model // 4
    out_row, output, slope_rest, d_pre3, f1_keep, f1_send, sums3 = call(
        functools.partial(ffn_forward_rest, chunk=chunk_rows), sc,
        [mine_f, sib_f, norm_gain, norm_shift, xhat2, pre_own, cotangent, act_own],
        [(wide, BF16), ((n_tensor * length, model), BF16), low_side, (wide, F32), *grads(hidden), sums_shape],
        [low_side, *f_weights, turned, ((model, 2 * hidden), BF16)], 11,
        {6: (length, False)}, {1: (length, False)}, cuts={4: cut, 5: cut, 6: cut}, out_cuts={n: cut for n in range(4)},
        bare=(4, 5), dealt=dealt,
    )
    out_other = lax.ppermute(out_row, "tensor", swap_y)
    f1_other = core_swap(f1_send)
    back, f1_other = lax.optimization_barrier((
        call(
            functools.partial(ffn_backward, chunk=chunk_rows), sc,
            [ffn_out, ffn_in, *norms, d_pre3, slope_own, xhat2, slope_rest, mine_f, sib_f, rstd2],
            [(wide, F32), *grads(hidden), sums_shape],
            [low_wide, turned, *f_weights, block_wide, ((model, 2 * hidden), BF16)], 12,
            cuts={n: cut for n in (5, 6, 7, 8, 11)}, out_cuts={0: cut}, bare=(1, 2), dealt=dealt,
        ),
        f1_other,
    ))
    d_pre2, f2_keep, f2_send, sums2 = back
    f2_other = core_swap(f2_send)
    if dealt:
        f_there = jnp.concatenate([part_total(1, f1_keep, f1_other), part_total(1, f2_keep, f2_other)], axis=1)
        d_pre2 = after(d_pre2, f_there)
        f_x = lax.ppermute(f_there, "dp", swap(2))
    else:
        f_x = sums2
    logs = ((half // HEAD_DIM, length), F32)
    halves = [((n_tensor * length, half), F32), (side, BF16)]
    back, f_x, out_other = lax.optimization_barrier((
        call(
            functools.partial(cross_backward, chunk=chunk_rows), sc,
            [mine_c, sib_c, cross_out, *norms, d_pre2, xhat1, memory, c_state[3], c_state[8],
             *c_state[:3], *c_state[5:8], c_state[4], c_state[9], brow, *own_c[:3], rstd1],
            [(wide, F32), *halves, *grads(4 * half), sums_shape],
            [*square_weights, *[(side, BF16)] * 2, logs, logs, *[(side, BF16)] * 2, *[(side, F32)] * 4,
             *[(side, BF16)] * 4, ((4, heads * QB, GW), F32), turned, turned, turned, block_wide,
             ((model, 8 * half), BF16)],
            23, {8: (length, False)}, {1: (length, False)}, cuts={n: cut for n in range(6, 11)},
            out_cuts={n: cut for n in range(3)}, bare=(3, 4), dealt=dealt, full=True,
        ),
        f_x, out_other,
    ))
    d_pre1, memory_grad, mem_send, c_keep, c_send, sums1 = back
    mem_other = lax.ppermute(mem_send, "tensor", swap_y)
    c_other = core_swap(c_send)
    c_x, f_z = sums1, sums1
    if dealt:
        f_part = jnp.concatenate(
            [
                part_total(
                    0, keep[:, first : first + hidden], other[:, first : first + hidden],
                    f_x[:, base + first : base + first + hidden],
                )
                for first in (0, hidden)
                for keep, other, base in ((f1_keep, f1_other, 0), (f2_keep, f2_other, 2 * hidden))
            ],
            axis=1,
        )
        f_z = z_send(f_part)
        c_there = part_total(1, c_keep, c_other)
        c_x = lax.ppermute(c_there, "dp", swap(2))
        d_pre1 = after(d_pre1, c_there, f_part)
    back, c_x, mem_other = lax.optimization_barrier((
        call(
            functools.partial(self_backward, chunk=chunk_rows), sc,
            [mine_s, sib_s, self_out, d_pre1, inputs, s_own[3], s_rest[3], *s_own[:3],
             *s_rest[:3], s_own[4], s_rest[4], brow, sums1, sums2, sums3, out_other, output],
            [*[(side, BF16)] * 6, *grads(4 * half + QB, 4 if dealt else 2), (output.shape, BF16)],
            [*square_weights, *[(side, BF16)] * 2, logs, logs, *[(side, F32)] * 4,
             ((4, heads * QB, GW), F32), turned, turned, ((8, model), F32), ((QB, model), F32), ((model, QB), BF16),
             ((model, 2 * (4 * half + QB)), BF16)],
            16, {4: (length, False)}, {8: (length, True)}, {20: 8}, cuts={n: cut for n in range(3, 7)},
            bare=(6, 7, 8), dealt=dealt,
        ),
        c_x, mem_other,
    ))
    *d_self, s_keep, s_send, output = back
    s_other = core_swap(s_send)
    if dealt:
        across = [(i * 2 + j, (i ^ 2) * 2 + 1 - j) for i in range(n_dp) for j in range(2)]
        s_near = [part_total(n, s_keep, s_other) for n in range(1, 4)]
        f_last = total(*f_z).astype(BF16)
        c_part = part_total(0, c_keep, c_other, c_x)
        d_self[0] = after(d_self[0], *s_near, f_last, c_part)
        s_near = [
            lax.ppermute(s_near[0], "tensor", swap_y), lax.ppermute(s_near[1], "dp", swap(2)),
            lax.ppermute(s_near[2], ("dp", "tensor"), across),
        ]
    input_grad, in_send, memory_grad = call(
        input_backward, sc,
        [mine_s, sib_s, *own_s[:3], residual_scale, d_pre1, *d_self, mem_other, memory_grad],
        [*halves, (memory_grad.shape, F32)], square_weights, 5, None, {0: (length, False), 2: (length, True)},
        {14: 2}, cuts={n: cut for n in range(6, 13)}, out_cuts={0: cut, 1: cut},
    )
    thin, broad = ((chunk, half), F32), ((chunk, hidden), F32)
    three = ((3, chunk), F32)
    if dealt:
        in_send, c_part = lax.optimization_barrier((in_send, c_part))
        in_other = lax.ppermute(in_send, "tensor", swap_y)
        c_z = z_send(c_part)
        in_other, c_z = lax.optimization_barrier((in_other, c_z))
        s_far = z_send(part_total(0, s_keep, s_other, *s_near))
        c_last = total(*c_z).astype(BF16)
        late = lax.ppermute(
            jnp.concatenate([f_last[:, 2 * hidden :], c_last[:, 4 * half :]], axis=1), "tensor", swap_y
        )
        while len(s_far) < 4:
            s_far.append(jnp.zeros_like(s_far[0]))
        s_far = [*s_far[:3], s_far[3] if len(s_far) == 4 else total(*s_far[3:]).astype(BF16)]
        input_grad = fill(input_grad, in_other)
        sq, sk, sv, so, cq, ck, cv, co, ffn_in_grad, ffn_out_grad, gain_grad, shift_grad, scale_grad = call(
            finish, sc, [f_last, c_last, late, *s_far], [*[thin] * 8, broad, broad, three, three, three], [], 0.01
        )
    else:
        input_grad = fill(input_grad, lax.ppermute(in_send, "tensor", swap_y))
        f1_sum, f2_sum = reduce_any(f1_keep, f1_send), reduce_any(f2_keep, f2_send)
        c_sum, s_sum = reduce_any(c_keep, c_send), reduce_any(s_keep, s_send)
        ffn_in_grad, ffn_out_grad = f2_sum, f1_sum
        cq, ck, cv, co = [c_sum[:, n * half : (n + 1) * half] for n in range(4)]
        sq, sk, sv, so = [s_sum[:, n * half : (n + 1) * half] for n in range(4)]
        gain_grad, shift_grad, scale_grad = [s_sum[:, 4 * half + 3 * n : 4 * half + 3 * n + 3].T for n in range(3)]
    return (
        output, input_grad, memory_grad, sq, sk, sv, so.T, cq, ck, cv, co.T, ffn_in_grad, ffn_out_grad.T,
        gain_grad, shift_grad, scale_grad,
    )


def solution(mesh):
    rows, cols = P("dp", None), P(None, "tensor")
    both, turned = P("dp", "tensor"), P("tensor", "dp")
    return jax.shard_map(
        functools.partial(local, n_dp=mesh.shape["dp"], n_tensor=mesh.shape["tensor"]),
        mesh=mesh,
        in_specs=(
            rows, rows, rows, rows, cols, cols, cols, turned_rows(), cols, cols, cols, turned_rows(), cols,
            turned_rows(), P(), P(), P(), rows,
        ),
        out_specs=(
            rows, both, both, both, both, both, turned, both, both, both, turned, both, turned,
            P(None, "dp"), P(None, "dp"), P(None, "dp"),
        ),
        check_vma=False,
    )


def turned_rows():
    return P("tensor", None)
```

```python
import functools
import math

import jax
import jax.numpy as jnp
from jax import lax
from jax.experimental import pallas as pl
from jax.experimental.pallas import tpu as pltpu
from jax.sharding import PartitionSpec as P

HEAD_DIM = 64
QB = 128
KC = 256
XC = 128
GW = 256
EPS = 1e-05
NEG = -1e30
F32 = jnp.float32
BF16 = jnp.bfloat16
MB = 512
SPARE = 12 * 1024 * 1024
FULL = 56 * 1024 * 1024
SEGMENTS = 32
FLOPS_PER_US = 5e9


def nn(left, right):
    return lax.dot_general(left, right, (((1,), (0,)), ((), ())), preferred_element_type=F32)


def nt(left, right):
    return lax.dot_general(left, right, (((1,), (1,)), ((), ())), preferred_element_type=F32)


def tn(left, right):
    return lax.dot_general(left, right, (((0,), (0,)), ((), ())), preferred_element_type=F32)


def iota(shape, dim):
    return lax.broadcasted_iota(jnp.int32, shape, dim)


def normalise(pre):
    center = jnp.mean(pre, axis=-1, keepdims=True)
    centered = pre - center
    rstd = lax.rsqrt(jnp.mean(centered * centered, axis=-1, keepdims=True) + EPS)
    return centered * rstd, rstd


def norm_back(grad, gain, xhat, rstd):
    scaled = grad * gain
    first = jnp.mean(scaled, axis=-1, keepdims=True)
    second = jnp.mean(scaled * xhat, axis=-1, keepdims=True)
    return rstd * (scaled - first - xhat * second)


def rows_at(block, size):
    return pl.ds(pl.multiple_of(block * size, size), size)


def stack_heads(block):
    head = iota((1, GW), 1) // HEAD_DIM
    return jnp.concatenate(
        [block * (head == h).astype(F32).astype(BF16) for h in range(GW // HEAD_DIM)], axis=0
    )


def unstack_heads(stacked, rows):
    low_half = iota((1, 128), 1) < HEAD_DIM
    tiles = []
    for tile in range(GW // 128):
        cols = slice(tile * 128, tile * 128 + 128)
        first, second = 2 * tile, 2 * tile + 1
        tiles.append(
            jnp.where(
                low_half,
                stacked[first * rows : (first + 1) * rows, cols],
                stacked[second * rows : (second + 1) * rows, cols],
            )
        )
    return jnp.concatenate(tiles, axis=1)


def each_more(units, where, body):
    for count in {id(unit[where]): unit[where] for unit in units}.values():

        @pl.loop(1, count)
        def _(j):
            for n, unit in enumerate(units):
                if unit[where] is count:
                    body(n, j)


def chunk_keys(first, j):
    if isinstance(j, int):
        return pl.ds(pl.multiple_of(first, 16), KC)
    return pl.ds(pl.multiple_of(first + (KC - XC) + j * XC, 16), XC)


def attend_units(units, s_scr, m_scr, l_scr, o_scr):
    heads = GW // HEAD_DIM
    stacks = [stack_heads(q[rows_at(i, QB), :]) for i, q, *_ in units]

    def scores(n, j):
        _, _, k, _, lo, hi, first, _ = units[n]
        keys, place = chunk_keys(first, j), chunk_keys(0, j)
        at = keys.start + iota((keys.size, QB), 0)
        allowed = (at >= lo) & (at < hi)
        s = nt(k[keys, :], stacks[n])
        peaks = []
        for h in range(heads):
            part = slice(h * QB, (h + 1) * QB)
            masked = jnp.where(allowed, s[:, part], NEG)
            s_scr[n, place, part] = masked
            peaks.append(jnp.max(masked, axis=0, keepdims=True))
        return jnp.concatenate(peaks, axis=1)

    for n in range(len(units)):
        m_scr[n : n + 1, :] = scores(n, 0)

    def more_scores(n, j):
        m_scr[n : n + 1, :] = jnp.maximum(m_scr[n : n + 1, :], scores(n, j))

    each_more(units, 7, more_scores)
    peaks = [m_scr[n : n + 1, :] for n in range(len(units))]

    def weigh(n, j):
        p = jnp.exp(s_scr[n, chunk_keys(0, j), :] - peaks[n])
        return jnp.sum(p, axis=0, keepdims=True), tn(units[n][3][chunk_keys(units[n][6], j), :], p.astype(BF16))

    for n in range(len(units)):
        l_scr[n : n + 1, :], o_scr[n] = weigh(n, 0)

    def more_weights(n, j):
        more_l, more_o = weigh(n, j)
        l_scr[n : n + 1, :] = l_scr[n : n + 1, :] + more_l
        o_scr[n] = o_scr[n] + more_o

    each_more(units, 7, more_weights)
    results = []
    for n in range(len(units)):
        total = l_scr[n : n + 1, :]
        log = peaks[n] + jnp.log(total)
        scale = 1.0 / total
        parts = [
            o_scr[n, h * HEAD_DIM : (h + 1) * HEAD_DIM, h * QB : (h + 1) * QB] * scale[:, h * QB : (h + 1) * QB]
            for h in range(heads)
        ]
        mixed = jnp.transpose(jnp.concatenate(parts, axis=0).astype(BF16))
        results.append((mixed, [log[:, h * QB : (h + 1) * QB] for h in range(heads)]))
    return results


def attend_back_units(units, r_scr):
    heads = GW // HEAD_DIM

    def chunk(n, j):
        i, q, k, v, do, lse, delta, lo, hi, first, _, _, dk, dv = units[n]
        rows = rows_at(i, QB)
        keys = chunk_keys(first, j)
        qs = stack_heads(q[rows, :])
        ds = stack_heads(do[rows, :])
        kg = k[keys, :]
        at = keys.start + iota((keys.size, QB), 0)
        allowed = (at >= lo) & (at < hi)
        st = nt(kg, qs)
        dp = nt(v[keys, :], ds)
        probs, grads = [], []
        for h in range(heads):
            part = slice(h * QB, (h + 1) * QB)
            p = jnp.where(allowed, jnp.exp(st[:, part] - lse[h : h + 1, rows]), 0.0)
            probs.append(p.astype(BF16))
            grads.append((p * (dp[:, part] - delta[h : h + 1, rows])).astype(BF16))
        prob = jnp.concatenate(probs, axis=1)
        grad = jnp.concatenate(grads, axis=1)
        dv[keys, :] += nn(prob, ds)
        dk[keys, :] += nn(grad, qs)
        return tn(grad, kg)

    for n in range(len(units)):
        r_scr[n] = chunk(n, 0)

    def more(n, j):
        r_scr[n] = r_scr[n] + chunk(n, j)

    each_more(units, 10, more)
    for n, unit in enumerate(units):
        unit[11][rows_at(unit[0], QB), :] = (unstack_heads(r_scr[n], QB) * HEAD_DIM**-0.5).astype(BF16)


def set_delta(rows, do, mixed, delta_scr):
    heads = do.shape[1] // HEAD_DIM
    product = do.astype(F32) * mixed.astype(F32)
    high = product.astype(BF16)
    rest = (product - high.astype(F32)).astype(BF16)
    pick = (iota((heads, do.shape[1]), 1) // HEAD_DIM == iota((heads, do.shape[1]), 0)).astype(F32).astype(BF16)
    delta_scr[:, rows] = nt(pick, high) + nt(pick, rest)


def put_transposed(rows, block, scr, chunk):
    turned = jnp.transpose(block)
    size = turned.shape[0]
    count = size // chunk
    for n in range(count):
        first = (n % 2 * 2 + n // 2 % 2) * (size // 4) + n // 4 * chunk if chunk else 0
        scr[first : first + chunk, rows] = turned[n * chunk : (n + 1) * chunk]


def add_sum(ref, row, value):
    ref[row : row + 1, :] += jnp.sum(value, axis=0, keepdims=True)


def project(rows, left, weight, out, factor=1.0):
    out[rows, :] = (nn(left, weight[...]) * factor).astype(BF16)


def unpack_square(mine, sib, weights):
    core = core_index()
    *cols, out = weights
    part, half = cols[0].shape[0] // 2, out.shape[0]
    small = half // 2
    for place, source in ((core, mine), (1 - core, sib)):
        for n, w in enumerate(cols):
            w[rows_at(place, part), :] = source[n * part : (n + 1) * part, :]
        base = len(cols) * part
        for n in range(out.shape[1] // half):
            out[rows_at(place, small), n * half : (n + 1) * half] = source[
                base + n * small : base + (n + 1) * small, :
            ]


def unpack_ffn(mine, sib, win, wout):
    core = core_index()
    part, rows, width = win.shape[0] // 2, wout.shape[0] // 2, wout.shape[1]
    tiles = win.shape[1] // width
    for place, source in ((core, mine), (1 - core, sib)):
        for n in range(tiles):
            win[rows_at(place, part), n * width : (n + 1) * width] = source[n * part : (n + 1) * part, :]
        wout[rows_at(place, rows), :] = source[tiles * part :, :]


def core_index():
    return lax.axis_index("dp") % 2


def set_ranges(tgt, src, brow, blocks):
    rows, length = tgt.shape
    mine = lax.axis_index("tensor")

    def row(ref):
        value = ref[0:1, :]
        for n in range(1, rows):
            value = jnp.where(mine == n, ref[n : n + 1, :], value)
        return value

    target, source = row(tgt), row(src)
    ids = iota((SEGMENTS, length), 0)

    def before(ids_of, limit):
        count = jnp.sum((ids_of < limit).astype(F32), axis=1, keepdims=True)
        return jnp.sum(jnp.where(ids == target, count, 0.0), axis=0, keepdims=True).astype(jnp.int32)

    values = [
        before(target, ids), iota((1, length), 1) + 1, before(source, ids), before(source, ids + 1)
    ]
    lane = iota((1, 128), 1)
    for n, value in enumerate(values):
        brow[n : n + 1, :] = value
        brow[n + 4 : n + 5, :] = value
    blocks[...] = jnp.zeros_like(blocks)
    for n in range(2):
        first = jnp.zeros((1, 128), jnp.int32)
        last = jnp.zeros((1, 128), jnp.int32)
        for i in range(length // QB):
            low, high = values[2 * n][:, i * QB : i * QB + 1], values[2 * n + 1][:, (i + 1) * QB - 1 : (i + 1) * QB]
            first = jnp.where(lane == i, low, first)
            last = jnp.where(lane == i, high, last)
        first = lax.shift_left(lax.shift_right_logical(first, 4), 4)
        more = lax.shift_right_logical(jnp.maximum(last - first - KC, 0) + (XC - 1), XC.bit_length() - 1)
        blocks[2 * n : 2 * n + 1, :] = jnp.minimum(first, length - KC - more * XC)
        blocks[2 * n + 1 : 2 * n + 2, :] = more + 1


def forward_units(sc, brow, i, which, groups):
    rows = rows_at(i, QB)
    first, count = sc[2 * which, i], sc[2 * which + 1, i]
    lo, hi = brow[2 * which : 2 * which + 1, rows], brow[2 * which + 1 : 2 * which + 2, rows]
    return [(i, q, k, v, lo, hi, first, count) for q, k, v in groups]


def put_logs(lse, i, logs):
    for h, log in enumerate(logs):
        lse[h : h + 1, rows_at(i, QB)] = log


def project_self(x, weights, outs):
    @pl.loop(0, x.chunks)
    def _(i):
        x.need(i)
        rows = rows_at(i, MB)
        block = x[rows, :]
        for weight, out, factor in zip(weights, outs, (HEAD_DIM**-0.5, 1.0, 1.0)):
            project(rows, block, weight, out, factor)
            out.put(i)


def self_forward_own(sc, qo, ko, vo, x, brow, q, k, v, mixed, lse, *scratch):
    need(qo, ko, vo)
    project_self(x, (qo, ko, vo), (q, k, v))
    need(brow)

    @pl.loop(0, x.shape[0] // QB // 2)
    def _(pair):
        pair_of = [2 * pair, 2 * pair + 1]
        units = [forward_units(sc, brow, i, 0, [(q, k, v)])[0] for i in pair_of]
        for i, (block, logs) in zip(pair_of, attend_units(units, *scratch)):
            mixed[rows_at(i, QB), :] = block
            put_logs(lse, i, logs)


def norm_rows(i, pre, xhat, rstd):
    @pl.loop(0, MB // QB)
    def _(n):
        rows = rows_at(i * (MB // QB) + n, QB)
        hat, inv = normalise(pre[rows_at(n, QB), :])
        xhat[rows, :] = hat
        rstd[rows, :] = jnp.broadcast_to(inv, (QB, rstd.shape[1]))

    xhat.put(i)
    rstd.put(i)


def self_forward_rest(
    sc, mine, sib, x, brow, mixed_own, oo, omega,
    q, k, v, mixed, lse, xhat, rstd, qx, kx, vx, ox, pre, *scratch,
):
    need(mine, sib)
    unpack_square(mine, sib, (qx, kx, vx, ox))
    project_self(x, (qx, kx, vx), (q, k, v))
    need(brow)

    @pl.loop(0, x.shape[0] // QB // 2)
    def _(pair):
        pair_of = [2 * pair, 2 * pair + 1]
        units = [forward_units(sc, brow, i, 0, [(q, k, v)])[0] for i in pair_of]
        for i, (block, logs) in zip(pair_of, attend_units(units, *scratch)):
            mixed[rows_at(i, QB), :] = block
            put_logs(lse, i, logs)

    need(mixed_own, oo, omega)

    @pl.loop(0, x.chunks)
    def _(i):
        rows = rows_at(i, MB)
        branch = nn(mixed_own[rows, :], oo[...]) + nn(mixed[rows, :], ox[...])
        pre[...] = omega[0:1] * x[rows, :].astype(F32) + branch
        norm_rows(i, pre, xhat, rstd)


def cross_forward(
    sc, mine, sib, qo, ko, vo, gain, shift, xhat1, mem, brow, oo, omega,
    q, k, v, mixed, lse, q_x, k_x, v_x, mixed_x, lse_x, xhat, rstd, qx, kx, vx, ox, pre, *scratch,
):
    need(mine, sib, qo, ko, vo, gain, shift)
    unpack_square(mine, sib, (qx, kx, vx, ox))

    @pl.loop(0, mem.chunks)
    def _(i):
        rows = rows_at(i, MB)
        xhat1.need(i)
        mem.need(i)
        low1 = (xhat1[rows, :] * gain[0:1] + shift[0:1]).astype(BF16)
        block = mem[rows, :]
        for weights, outs in (((qo, ko, vo), (q, k, v)), ((qx, kx, vx), (q_x, k_x, v_x))):
            project(rows, low1, weights[0], outs[0], HEAD_DIM**-0.5)
            project(rows, block, weights[1], outs[1])
            project(rows, block, weights[2], outs[2])
            for result in outs:
                result.put(i)

    need(brow)

    @pl.loop(0, mem.shape[0] // QB)
    def _(i):
        units = forward_units(sc, brow, i, 1, ((q, k, v), (q_x, k_x, v_x)))
        for (block, logs), out, lse_out in zip(attend_units(units, *scratch), (mixed, mixed_x), (lse, lse_x)):
            out[rows_at(i, QB), :] = block
            put_logs(lse_out, i, logs)

    need(oo, omega)

    @pl.loop(0, mem.chunks)
    def _(i):
        rows = rows_at(i, MB)
        branch = nn(mixed[rows, :], oo[...]) + nn(mixed_x[rows, :], ox[...])
        pre[...] = omega[1:2] * (xhat1[rows, :] * gain[0:1] + shift[0:1]) + branch
        norm_rows(i, pre, xhat, rstd)


def hidden_units(rows, low2, win, act, slope, width=512):
    for first in range(0, win.shape[1], width):
        place = slice(first, first + width)
        u = nn(low2, win[:, place])
        square = u * u
        t = jnp.tanh(u * (0.7978845608028654 + (0.7978845608028654 * 0.044715) * square))
        h = 0.5 + 0.5 * t
        a = u * h
        act[rows, place] = a.astype(BF16)
        steep = 2 * 0.7978845608028654 + (6 * 0.7978845608028654 * 0.044715) * square
        slope[rows, place] = (h + a * (1.0 - h) * steep).astype(BF16)


def ffn_forward_own(sc, io, gain, shift, xhat2, oo, omega, act, slope, pre):
    need(io, gain, shift)

    @pl.loop(0, xhat2.chunks)
    def _(i):
        rows = rows_at(i, MB)
        xhat2.need(i)
        norm2 = xhat2[rows, :] * gain[1:2] + shift[1:2]
        hidden_units(rows, norm2.astype(BF16), io, act, slope)
        act.put(i)
        slope.put(i)

    need(oo, omega)

    @pl.loop(0, xhat2.chunks)
    def _(i):
        rows = rows_at(i, MB)
        norm2 = xhat2[rows, :] * gain[1:2] + shift[1:2]
        pre[rows, :] = omega[2:3] * norm2 + nn(act[rows, :], oo[...])
        pre.put(i)


def ffn_forward_rest(
    sc, mine, sib, gain, shift, xhat2, pre, cot, act_own,
    out, out_all, slope, d_pre3, keep, send, sums, act, ix, ox, grad_t, grads, *, chunk,
):
    need(mine, sib, gain, shift)
    unpack_ffn(mine, sib, ix, ox)
    sums[...] = jnp.zeros_like(sums)
    width = 512
    half = ix.shape[1]

    @pl.loop(0, xhat2.chunks)
    def _(i):
        rows = rows_at(i, MB)
        xhat2.need(i)
        hidden_units(rows, (xhat2[rows, :] * gain[1:2] + shift[1:2]).astype(BF16), ix, act, slope)
        slope.put(i)
        pre.need(i)
        cot.need(i)
        pre[rows, :] += nn(act[rows, :], ox[...])

        @pl.loop(0, MB // QB)
        def _(n):
            small = rows_at(i * (MB // QB) + n, QB)
            hat, inv = normalise(pre[small, :])
            result = (hat * gain[2:3] + shift[2:3]).astype(BF16)
            out[small, :] = result
            out_all[small, :] = result
            grad = cot[small, :].astype(F32)
            d_pre = norm_back(grad, gain[2:3], hat, inv)
            d_pre3[small, :] = d_pre
            put_transposed(small, d_pre.astype(BF16), grad_t, chunk)
            add_sum(sums, 0, grad * hat)
            add_sum(sums, 1, grad)
            add_sum(sums, 2, d_pre * (xhat2[small, :] * gain[1:2] + shift[1:2]))

        for result in (out, out_all, d_pre3):
            result.put(i)

    need(act_own)
    for side, right in enumerate((act_own, act)):
        for first in range(0, half, width):
            grads[:, side * half + first : side * half + first + width] = nn(
                grad_t[...], right[:, first : first + width]
            ).astype(BF16)
    put_grads(grads, keep, send)


def put_grads(scr, keep, send):
    dp = lax.axis_index("dp")
    core, x = (dp % 2, dp // 2 % 2) if keep.dealt else (0, 0)
    size, width = scr.shape[0] // 4, keep.shape[1]
    parts = keep.shape[0] // size
    for out, row in ((keep, core), (send, 1 - core)):
        for n in range(parts):
            side = n * 2 // parts
            first = n % 2 * width if parts == 4 else 0
            place = row * 2 + (x if side == 0 else 1 - x)
            out.copy_part(scr.at[rows_at(place, size), first : first + width], n * size)


def ffn_backward(
    sc, oo, io, gain, shift, omega, d_pre3, slope_own, xhat2, slope_rest, mine, sib, rstd2,
    d_pre2, keep, send, sums, up_scr, norm_t, ix, ox, acc, grads, *, chunk,
):
    need(io, oo, gain, shift, omega, mine, sib)
    unpack_ffn(mine, sib, ix, ox)
    sums[...] = jnp.zeros_like(sums)
    half = io.shape[1]
    width = 512

    @pl.loop(0, xhat2.chunks)
    def _(i):
        rows = rows_at(i, MB)
        for argument in (d_pre3, slope_own, xhat2, slope_rest):
            argument.need(i)
        grad = d_pre3[rows, :]
        low = grad.astype(BF16)
        acc[...] = omega[2:3] * grad
        for side, (win, wout, slope) in enumerate(((io, oo, slope_own), (ix, ox, slope_rest))):
            for first in range(0, half, width):
                place = slice(side * half + first, side * half + first + width)
                up_scr[rows, place] = (
                    slope[rows, first : first + width].astype(F32) * nt(low, wout[first : first + width, :])
                ).astype(BF16)
            acc[...] += nt(up_scr[rows, side * half : (side + 1) * half], win[...])

        rstd2.need(i)

        @pl.loop(0, MB // QB)
        def _(n):
            small = rows_at(i * (MB // QB) + n, QB)
            total = acc[rows_at(n, QB), :]
            hat = xhat2[small, :]
            put_transposed(small, (hat * gain[1:2] + shift[1:2]).astype(BF16), norm_t, chunk)
            d_pre2[small, :] = norm_back(total, gain[1:2], hat, rstd2[small, 0:1])
            add_sum(sums, 0, total * hat)
            add_sum(sums, 1, total)

        d_pre2.put(i)

    for first in range(0, 2 * half, width):
        grads[:, first : first + width] = nn(norm_t[...], up_scr[:, first : first + width]).astype(BF16)
    put_grads(grads, keep, send)


def weight_grads(pairs, grads):
    width = grads.shape[1] // 2
    for n, (left, *rights) in enumerate(pairs):
        for side, right in enumerate(rights):
            half = right.shape[1]
            first = side * width + n * half
            grads[:, first : first + half] = nn(left[...], right[...]).astype(BF16)


def backward_units(sc, brow, i, which, groups):
    rows = rows_at(i, QB)
    first, count = sc[2 * which, i], sc[2 * which + 1, i]
    lo, hi = brow[2 * which : 2 * which + 1, rows], brow[2 * which + 1 : 2 * which + 2, rows]
    return [(i, *group[:6], lo, hi, first, count, *group[6:]) for group in groups]


def attention_grads(low, rows, outs):
    for out, weight, was, total in outs:
        value = nt(low, weight[...]).astype(BF16)
        out[rows, :] = value
        set_delta(rows, value, was[rows, :], total)


def cross_backward(
    sc, mine, sib, oo, gain, shift, omega, d_pre2, xhat1, mem, mixed, mixed_x, q, k, v, q_x, k_x, v_x, lse, lse_x,
    brow, qo, ko, vo, rstd1,
    d_pre1, mem_all, mem_send, keep, send, sums,
    qx, kx, vx, ox, do, do_x, delta, delta_x, dq, dq_x, dk, dk_x, dv, dv_x, dkb, dkb_x, dvb, dvb_x, r_scr,
    grad_t, norm_t, mem_t, acc, grads, *, chunk,
):
    half = qo.shape[1]
    blocks = mem.shape[0] // QB
    for ref in (sums, dk, dk_x, dv, dv_x):
        ref[...] = jnp.zeros_like(ref)
    need(mine, sib, oo, gain, shift, omega)
    unpack_square(mine, sib, (qx, kx, vx, ox))

    @pl.loop(0, mem.chunks)
    def _(i):
        rows = rows_at(i, MB)
        for argument in (d_pre2, xhat1, mem, mixed, mixed_x):
            argument.need(i)
        grad = d_pre2[rows, :]
        low = grad.astype(BF16)
        norm1 = xhat1[rows, :] * gain[0:1] + shift[0:1]
        put_transposed(rows, low, grad_t, chunk)
        put_transposed(rows, norm1.astype(BF16), norm_t, chunk)
        put_transposed(rows, mem[rows, :], mem_t, chunk)
        attention_grads(low, rows, ((do, oo, mixed, delta), (do_x, ox, mixed_x, delta_x)))
        add_sum(sums, 0, grad * norm1)

    need(q, k, v, q_x, k_x, v_x, lse, lse_x, brow)

    @pl.loop(0, blocks // 2)
    def _(pair):
        groups = (
            (q, k, v, do, lse, delta, dq, dk, dv), (q_x, k_x, v_x, do_x, lse_x, delta_x, dq_x, dk_x, dv_x)
        )
        units = []
        for i in (2 * pair, 2 * pair + 1):
            units += backward_units(sc, brow, i, 1, groups)
        attend_back_units(units, r_scr)

    need(qo, ko, vo, rstd1)
    tensor = lax.axis_index("tensor")

    @pl.loop(0, mem.chunks)
    def _(i):
        rows = rows_at(i, MB)
        acc[...] = omega[1:2] * d_pre2[rows, :] + nt(dq[rows, :], qo[...]) + nt(dq_x[rows, :], qx[...])
        for low, wide in ((dkb, dk), (dkb_x, dk_x), (dvb, dv), (dvb_x, dv_x)):
            low[rows, :] = wide[rows, :].astype(BF16)

        def part(side):
            which = rows_at(side, half)
            return (
                nt(dkb[rows, :], ko[which, :]) + nt(dkb_x[rows, :], kx[which, :])
                + nt(dvb[rows, :], vo[which, :]) + nt(dvb_x[rows, :], vx[which, :])
            )

        mem_all[rows, :] = part(tensor)
        mem_send[rows, :] = part(1 - tensor).astype(BF16)

        @pl.loop(0, MB // QB)
        def _(n):
            small = rows_at(i * (MB // QB) + n, QB)
            total = acc[rows_at(n, QB), :]
            hat = xhat1[small, :]
            d_pre1[small, :] = norm_back(total, gain[0:1], hat, rstd1[small, 0:1])
            add_sum(sums, 1, total * hat)
            add_sum(sums, 2, total)

        for result in (d_pre1, mem_all, mem_send):
            result.put(i)

    weight_grads(
        ((norm_t, dq, dq_x), (mem_t, dkb, dkb_x), (mem_t, dvb, dvb_x), (grad_t, mixed, mixed_x)), grads
    )
    put_grads(grads, keep, send)


def self_backward(
    sc, mine, sib, oo, d_pre1, x, mixed, mixed_x, q, k, v, q_x, k_x, v_x, lse, lse_x, brow, sums1, sums2, sums3, out_other,
    dq, dq_x, dkb, dkb_x, dvb, dvb_x, keep, send, out_all,
    qx, kx, vx, ox, do, do_x, delta, delta_x, dk, dk_x, dv, dv_x, r_scr, grad_t, in_t, sums, all_sums, sums_t, grads, *, chunk,
):
    blocks = x.shape[0] // QB
    for ref in (sums, all_sums, dk, dk_x, dv, dv_x):
        ref[...] = jnp.zeros_like(ref)
    need(mine, sib, oo)
    unpack_square(mine, sib, (qx, kx, vx, ox))

    @pl.loop(0, x.chunks)
    def _(i):
        rows = rows_at(i, MB)
        for argument in (d_pre1, x, mixed, mixed_x):
            argument.need(i)
        grad = d_pre1[rows, :]
        low = grad.astype(BF16)
        block = x[rows, :]
        put_transposed(rows, low, grad_t, chunk)
        put_transposed(rows, block, in_t, chunk)
        attention_grads(low, rows, ((do, oo, mixed, delta), (do_x, ox, mixed_x, delta_x)))
        add_sum(sums, 0, grad * block.astype(F32))

    need(q, k, v, q_x, k_x, v_x, lse, lse_x, brow, sums1, sums2, sums3, out_other)
    out_all.copy_from(out_other.ref)

    @pl.loop(0, blocks // 2)
    def _(pair):
        groups = (
            (q, k, v, do, lse, delta, dq, dk, dv), (q_x, k_x, v_x, do_x, lse_x, delta_x, dq_x, dk_x, dv_x)
        )
        units = []
        for i in (2 * pair, 2 * pair + 1):
            units += backward_units(sc, brow, i, 0, groups)
        attend_back_units(units, r_scr)

    for low, wide in ((dkb, dk), (dkb_x, dk_x), (dvb, dv), (dvb_x, dv_x)):
        low[...] = wide[...].astype(BF16)
    for row, source in enumerate(
        (sums1[1:2, :], sums2[0:1, :], sums3[0:1, :], sums1[2:3, :], sums2[1:2, :], sums3[1:2, :], sums[0:1, :],
         sums1[0:1, :], sums3[2:3, :])
    ):
        all_sums[row : row + 1, :] = source
    put_transposed(pl.ds(0, QB), all_sums[...].astype(BF16), sums_t, chunk)
    weight_grads(((in_t, dq, dq_x), (in_t, dkb, dkb_x), (in_t, dvb, dvb_x), (grad_t, mixed, mixed_x)), grads)
    width = grads.shape[1] // 2
    for side in range(2):
        grads[:, (side + 1) * width - QB : (side + 1) * width] = sums_t[...]
    put_grads(grads, keep, send)


def input_backward(
    sc, mine, sib, qo, ko, vo, omega, d_pre1, dq, dq_x, dk, dk_x, dv, dv_x, mem_other, in_all, in_send, mem_all,
    qx, kx, vx, ox,
):
    need(mine, sib, qo, ko, vo, omega)
    unpack_square(mine, sib, (qx, kx, vx, ox))
    half = qo.shape[1]
    tensor = lax.axis_index("tensor")

    @pl.loop(0, d_pre1.chunks)
    def _(i):
        rows = rows_at(i, MB)
        for argument in (d_pre1, dq, dq_x, dk, dk_x, dv, dv_x):
            argument.need(i)

        def part(side):
            which = rows_at(side, half)
            total = omega[0:1, which] * d_pre1[rows, which]
            for grad, weight in ((dq, qo), (dq_x, qx), (dk, ko), (dk_x, kx), (dv, vo), (dv_x, vx)):
                total = total + nt(grad[rows, :], weight[which, :])
            return total

        in_all[rows, :] = part(tensor)
        in_send[rows, :] = part(1 - tensor).astype(BF16)
        in_all.put(i)
        in_send.put(i)

    need(mem_other)
    mem_all[...] = mem_other[...].astype(F32)


def fill_kernel(sc, other, out):
    @pl.loop(0, other.chunks)
    def _(i):
        other.need(i)
        rows = rows_at(i, other.shape[0] // other.chunks)
        out[rows, :] = other[rows, :].astype(out.dtype)
        out.put(i)


def finish(
    sc, own_f, own_c, late, s0, s1, s2, s3, sq, sk, sv, so, cq, ck, cv, co, win, wout, gain, shift, omega
):
    need(own_f, own_c, late, s0, s1, s2, s3)
    half, hidden = sq.shape[1], win.shape[1]

    def late_sum(own, first, base, width):
        return own[:, first : first + width].astype(F32) + late[:, base + first : base + first + width].astype(F32)

    wout[...] = late_sum(own_f, 0, 0, hidden)
    win[...] = late_sum(own_f, hidden, 0, hidden)
    for n, out in enumerate((cq, ck, cv, co)):
        out[...] = late_sum(own_c, n * half, 2 * hidden, half)

    def soon_sum(first, width):
        cols = slice(first, first + width)
        return (s0[:, cols].astype(F32) + s1[:, cols].astype(F32)) + (s2[:, cols].astype(F32) + s3[:, cols].astype(F32))

    for n, out in enumerate((sq, sk, sv, so)):
        out[...] = soon_sum(n * half, half)
    sums = jnp.transpose(soon_sum(4 * half, QB))
    for n, out in enumerate((gain, shift, omega)):
        out[...] = sums[3 * n : 3 * n + 3]


class Buffer:
    def __init__(self, ref, far, sems, chunks):
        self.ref, self.far, self.sems, self.chunks = ref, far, sems, chunks
        self.shape, self.dtype = far.shape, far.dtype

    def __getitem__(self, index):
        return self.ref[index]

    def __setitem__(self, index, value):
        self.ref[index] = value

    def chunk(self, i):
        size = self.shape[0] // self.chunks
        if self.chunks == 1:
            return self.ref, self.far
        rows = rows_at(i, size)
        return self.ref.at[rows], self.far.at[rows]

    def load(self):
        for i in range(self.chunks):
            near, far = self.chunk(i)
            pltpu.make_async_copy(far, near, self.sems.at[i]).start()

    def need(self, i):
        near, far = self.chunk(i)
        pltpu.make_async_copy(far, near, self.sems.at[i]).wait()

    def put(self, i=0):
        near, far = self.chunk(i)
        pltpu.make_async_copy(near, far, self.sems.at[0]).start()

    def copy_part(self, near, first):
        far = self.far.at[first : first + near.shape[0]]
        pltpu.make_async_copy(near, far, self.sems.at[0]).start()

    def copy_from(self, near):
        pltpu.make_async_copy(near, self.far, self.sems.at[0]).start()

    def done(self):
        pltpu.make_async_copy(self.far, self.far, self.sems.at[0]).wait()


def need(*buffers):
    for buffer in buffers:
        for i in range(buffer.chunks):
            buffer.need(i)


def call(
    body, sc, args, outs, scratch, us, picks=None, puts=None, alias=None, cuts=None, out_cuts=None, bare=(), dealt=True,
    full=False,
):
    picks, puts, cuts, out_cuts = picks or {}, puts or {}, cuts or {}, out_cuts or {}

    def block(ref, pick):
        if pick is None:
            return ref
        rows, other = pick
        place = lax.axis_index("tensor")
        return ref.at[rows_at(1 - place if other else place, rows)]

    def size(shape, pick):
        return shape if pick is None else (pick[0], *shape[1:])

    alias = alias or {}
    loads = [n for n in range(len(args)) if n not in alias]
    buffers = [
        *[(size(args[n].shape, picks.get(n)), args[n].dtype) for n in loads],
        *[(size(shape, puts.get(n)), kind) for n, (shape, kind) in enumerate(outs) if n not in bare],
        *scratch,
    ]
    room = sum(math.prod(shape[:-1]) * max(shape[-1], 128) * jnp.dtype(kind).itemsize for shape, kind in buffers)

    def kernel(sc, *refs):
        refs = list(refs)
        ins = [refs.pop(0) for _ in args]
        far_outs = [refs.pop(0) for _ in outs]
        near_ins = [refs.pop(0) for _ in loads]
        near_outs = [None if n in bare else refs.pop(0) for n in range(len(outs))]
        in_sems = [refs.pop(0) for _ in loads]
        out_sems = [refs.pop(0) for _ in outs]
        arguments = [
            Buffer(near, block(ins[n], picks.get(n)), sems, cuts.get(n, 1))
            for n, near, sems in zip(loads, near_ins, in_sems)
        ]
        results = [
            Buffer(near, block(far, puts.get(n)), sems, out_cuts.get(n, 1))
            for n, (far, near, sems) in enumerate(zip(far_outs, near_outs, out_sems))
        ]
        for result in results:
            result.dealt = dealt
        for argument in arguments:
            argument.load()
        body(sc, *arguments, *results, *refs)
        for n, result in enumerate(results):
            if n not in out_cuts and n not in bare:
                result.put()
        for result in results:
            result.done()

    return pl.pallas_call(
        kernel,
        out_shape=[jax.ShapeDtypeStruct(shape, kind) for shape, kind in outs],
        grid_spec=pltpu.PrefetchScalarGridSpec(
            num_scalar_prefetch=1,
            grid=(1,),
            in_specs=[pl.BlockSpec(memory_space=pl.ANY)] * len(args),
            out_specs=[pl.BlockSpec(memory_space=pl.ANY)] * len(outs),
            scratch_shapes=[
                *[pltpu.VMEM(shape, kind) for shape, kind in buffers[: len(buffers) - len(scratch)]],
                *[pltpu.SemaphoreType.DMA((cuts.get(n, 1),)) for n in loads],
                *[pltpu.SemaphoreType.DMA((1,)) for _ in outs],
                *[pltpu.VMEM(shape, kind) for shape, kind in scratch],
            ],
        ),
        input_output_aliases={n + 1: out for n, out in alias.items()},
        cost_estimate=pl.CostEstimate(flops=int(us * FLOPS_PER_US), bytes_accessed=1024, transcendentals=0),
        compiler_params=pltpu.CompilerParams(vmem_limit_bytes=FULL if full else room + SPARE),
        name=(body.func if isinstance(body, functools.partial) else body).__name__,
    )(sc, *args)


def pack(weights, outs, moves, segments=None):
    extra = [] if segments is None else list(segments)
    length = extra[0].shape[1] if extra else 0
    ranges = [((8, length), jnp.int32), ((8, 128), jnp.int32)] if extra else []

    def pack_weights(*refs):
        refs = list(refs)
        sources = [refs.pop(0) for _ in weights]
        ids = [refs.pop(0) for _ in extra]
        targets = [refs.pop(0) for _ in outs]
        sem = refs.pop()
        core = core_index()
        copies = []
        for n, (which, rows, first, out, start) in enumerate(moves):
            width = outs[out][0][1]
            copies.append(
                pltpu.make_async_copy(
                    sources[which].at[rows_at(core, rows), first : first + width],
                    targets[out].at[start : start + rows, :],
                    sem.at[n],
                )
            )
        for copy in copies:
            copy.start()
        if ids:
            set_ranges(*ids, *refs)
        for copy in copies:
            copy.wait()

    near = pl.BlockSpec(memory_space=pltpu.VMEM)
    return pl.pallas_call(
        pack_weights,
        out_shape=[jax.ShapeDtypeStruct(shape, kind) for shape, kind in outs + ranges],
        in_specs=[pl.BlockSpec(memory_space=pltpu.HBM)] * len(weights) + [near] * len(extra),
        out_specs=[near] * len(outs + ranges),
        scratch_shapes=[pltpu.SemaphoreType.DMA((len(moves),))],
        cost_estimate=pl.CostEstimate(flops=int(FLOPS_PER_US), bytes_accessed=1024, transcendentals=0),
        compiler_params=pltpu.CompilerParams(vmem_limit_bytes=60 * 1024 * 1024),
        name="pack_weights",
    )(*weights, *extra)


def local(
    inputs, memory, tgt_seg, src_seg, self_query, self_key, self_value, self_out,
    cross_query, cross_key, cross_value, cross_out, ffn_in, ffn_out,
    norm_gain, norm_shift, residual_scale, cotangent, *, n_dp, n_tensor,
):
    d = lax.axis_index("dp")
    t = lax.axis_index("tensor")
    length = tgt_seg.shape[1]
    model = inputs.shape[1]
    half = model // n_tensor
    hidden = ffn_in.shape[1]
    blocks = length // QB
    chunk = model // n_dp
    dealt = chunk % 16 == 0 and n_dp & (n_dp - 1) == 0
    swap_y = [(0, 1), (1, 0)]

    def swap(n_bit):
        return [(i, i ^ n_bit) for i in range(n_dp)]

    def after(value, *others):
        return lax.optimization_barrier((value, others))[0]

    own_s = [self_query, self_key, self_value, self_out]
    own_c = [cross_query, cross_key, cross_value, cross_out]
    own_f = [ffn_in, ffn_out]
    square = ((4 * half, half), BF16)

    def square_moves(base, out):
        part = model // 2
        moves = [(base + n, part, 0, out, n * part) for n in range(3)]
        return moves + [(base + 3, half // 2, n * half, out, 3 * part + n * half // 2) for n in range(n_tensor)]

    (pack_s,) = pack(own_s, [square], square_moves(0, 0))
    tiles = hidden // model
    pack_c, pack_f, brow, sc = pack(
        own_c + own_f, [square, ((tiles * half + hidden // 2, model), BF16)],
        square_moves(0, 0)
        + [(4, model // 2, n * model, 1, n * model // 2) for n in range(tiles)]
        + [(5, hidden // 2, 0, 1, tiles * model // 2)],
        (tgt_seg, src_seg),
    )
    mine_s = lax.ppermute(pack_s, "tensor", swap_y)

    def fill(whole, other):
        (result,) = call(
            fill_kernel, sc, [whole, other], [(whole.shape, whole.dtype)], [], 1, None, {0: (length, True)}, {0: 0},
            cuts={1: 4}, out_cuts={0: 4},
        )
        return result

    def total(*parts):
        result = parts[0].astype(F32)
        for part in parts[1:]:
            result = result + part.astype(F32)
        return result

    size = model // 4

    def part_total(n, *arrays):
        return total(*[array[n * size : (n + 1) * size] for array in arrays]).astype(BF16)

    def z_send(part):
        far = n_dp // 4
        row = d // 4
        part = part.reshape(far, chunk, -1)
        parts = [lax.dynamic_index_in_dim(part, row, 0, keepdims=False)]
        for step in range(1, far):
            perm = [(i, i % 4 + (i // 4 + step) % far * 4) for i in range(n_dp)]
            out = lax.dynamic_index_in_dim(part, (row + step) % far, 0, keepdims=False)
            parts.append(lax.ppermute(out, "dp", perm))
        return parts

    def reduce_any(keep, send):
        grad = lax.psum_scatter(jnp.concatenate([keep, send]).astype(F32), "dp", scatter_dimension=0, tiled=True)
        width = grad.shape[1] // 2
        return grad[:, :width] + lax.ppermute(grad[:, width:], "tensor", swap_y)

    wide, side = (length, model), (length, half)
    heads = GW // HEAD_DIM
    group = [(side, BF16)] * 4 + [((half // HEAD_DIM, length), F32)]
    square_weights = [((model, half), BF16)] * 3 + [((half, model), BF16)]
    stats = [(wide, F32), ((length, 128), F32)]
    attend_scratch = [
        ((2, length, heads * QB), F32),
        ((2, heads * QB), F32),
        ((2, heads * QB), F32),
        ((2, GW, heads * QB), F32),
    ]
    block_wide = ((MB, model), F32)
    cut = length // MB
    norms = [norm_gain, norm_shift, residual_scale]
    s_own = call(
        self_forward_own, sc, [*own_s[:3], inputs, brow], group, attend_scratch, 7, {3: (length, False)},
        cuts={3: cut}, out_cuts={0: cut, 1: cut, 2: cut}, full=True,
    )
    s_own, mine_s = lax.optimization_barrier((s_own, mine_s))
    sib_s = lax.ppermute(mine_s, "dp", swap(1))
    mine_c = lax.ppermute(after(pack_c, mine_s), "tensor", swap_y)
    s_rest_stats = call(
        self_forward_rest, sc, [mine_s, sib_s, inputs, brow, s_own[3], self_out, residual_scale], group + stats,
        [*square_weights, block_wide, *attend_scratch], 8, {2: (length, False)},
        cuts={2: cut}, out_cuts={n: cut for n in (0, 1, 2, 5, 6)},
    )
    s_rest_stats, mine_c = lax.optimization_barrier((s_rest_stats, mine_c))
    *s_rest, xhat1, rstd1 = s_rest_stats
    sib_c = lax.ppermute(mine_c, "dp", swap(1))
    mine_f = lax.ppermute(after(pack_f, mine_c), "tensor", swap_y)
    c_stats = call(
        cross_forward, sc,
        [mine_c, sib_c, *own_c[:3], norm_gain, norm_shift, xhat1, memory, brow, cross_out, residual_scale],
        group + group + stats,
        [*square_weights, block_wide, *attend_scratch], 14, {8: (length, False)}, cuts={7: cut, 8: cut},
        out_cuts={n: cut for n in (0, 1, 2, 5, 6, 7, 10, 11)},
    )
    *c_state, xhat2, rstd2 = c_stats
    sums_shape = ((8, model), F32)
    low_side, low_wide = ((length, hidden), BF16), ((length, n_tensor * hidden), BF16)
    f_weights = [((model, hidden), BF16), ((hidden, model), BF16)]
    f_own, mine_f = lax.optimization_barrier((
        call(
            ffn_forward_own, sc, [ffn_in, norm_gain, norm_shift, xhat2, ffn_out, residual_scale],
            [low_side, low_side, (wide, F32)], [], 8, cuts={3: cut}, out_cuts={n: cut for n in range(3)},
        ),
        mine_f,
    ))
    act_own, slope_own, pre_own = f_own
    sib_f = lax.ppermute(mine_f, "dp", swap(1))

    def grads(width, parts=2):
        return [((parts * size, 4 * width // parts), BF16)] * 2

    def core_swap(send):
        return lax.ppermute(send, "dp", swap(1)) if dealt else send

    turned = ((model, length), BF16)
    chunk_rows = chunk if dealt else model // 4
    out_row, output, slope_rest, d_pre3, f1_keep, f1_send, sums3 = call(
        functools.partial(ffn_forward_rest, chunk=chunk_rows), sc,
        [mine_f, sib_f, norm_gain, norm_shift, xhat2, pre_own, cotangent, act_own],
        [(wide, BF16), ((n_tensor * length, model), BF16), low_side, (wide, F32), *grads(hidden), sums_shape],
        [low_side, *f_weights, turned, ((model, 2 * hidden), BF16)], 11,
        {6: (length, False)}, {1: (length, False)}, cuts={4: cut, 5: cut, 6: cut}, out_cuts={n: cut for n in range(4)},
        bare=(4, 5), dealt=dealt,
    )
    out_other = lax.ppermute(out_row, "tensor", swap_y)
    f1_other = core_swap(f1_send)
    back, f1_other = lax.optimization_barrier((
        call(
            functools.partial(ffn_backward, chunk=chunk_rows), sc,
            [ffn_out, ffn_in, *norms, d_pre3, slope_own, xhat2, slope_rest, mine_f, sib_f, rstd2],
            [(wide, F32), *grads(hidden), sums_shape],
            [low_wide, turned, *f_weights, block_wide, ((model, 2 * hidden), BF16)], 12,
            cuts={n: cut for n in (5, 6, 7, 8, 11)}, out_cuts={0: cut}, bare=(1, 2), dealt=dealt,
        ),
        f1_other,
    ))
    d_pre2, f2_keep, f2_send, sums2 = back
    f2_other = core_swap(f2_send)
    if dealt:
        f_there = jnp.concatenate([part_total(1, f1_keep, f1_other), part_total(1, f2_keep, f2_other)], axis=1)
        d_pre2 = after(d_pre2, f_there)
        f_x = lax.ppermute(f_there, "dp", swap(2))
    else:
        f_x = sums2
    logs = ((half // HEAD_DIM, length), F32)
    halves = [((n_tensor * length, half), F32), (side, BF16)]
    back, f_x, out_other = lax.optimization_barrier((
        call(
            functools.partial(cross_backward, chunk=chunk_rows), sc,
            [mine_c, sib_c, cross_out, *norms, d_pre2, xhat1, memory, c_state[3], c_state[8],
             *c_state[:3], *c_state[5:8], c_state[4], c_state[9], brow, *own_c[:3], rstd1],
            [(wide, F32), *halves, *grads(4 * half), sums_shape],
            [*square_weights, *[(side, BF16)] * 2, logs, logs, *[(side, BF16)] * 2, *[(side, F32)] * 4,
             *[(side, BF16)] * 4, ((4, heads * QB, GW), F32), turned, turned, turned, block_wide,
             ((model, 8 * half), BF16)],
            23, {8: (length, False)}, {1: (length, False)}, cuts={n: cut for n in range(6, 11)},
            out_cuts={n: cut for n in range(3)}, bare=(3, 4), dealt=dealt, full=True,
        ),
        f_x, out_other,
    ))
    d_pre1, memory_grad, mem_send, c_keep, c_send, sums1 = back
    mem_other = lax.ppermute(mem_send, "tensor", swap_y)
    c_other = core_swap(c_send)
    c_x, f_z = sums1, sums1
    if dealt:
        f_part = jnp.concatenate(
            [
                part_total(
                    0, keep[:, first : first + hidden], other[:, first : first + hidden],
                    f_x[:, base + first : base + first + hidden],
                )
                for first in (0, hidden)
                for keep, other, base in ((f1_keep, f1_other, 0), (f2_keep, f2_other, 2 * hidden))
            ],
            axis=1,
        )
        f_z = z_send(f_part)
        c_there = part_total(1, c_keep, c_other)
        c_x = lax.ppermute(c_there, "dp", swap(2))
        d_pre1 = after(d_pre1, c_there, f_part)
    back, c_x, mem_other = lax.optimization_barrier((
        call(
            functools.partial(self_backward, chunk=chunk_rows), sc,
            [mine_s, sib_s, self_out, d_pre1, inputs, s_own[3], s_rest[3], *s_own[:3],
             *s_rest[:3], s_own[4], s_rest[4], brow, sums1, sums2, sums3, out_other, output],
            [*[(side, BF16)] * 6, *grads(4 * half + QB, 4 if dealt else 2), (output.shape, BF16)],
            [*square_weights, *[(side, BF16)] * 2, logs, logs, *[(side, F32)] * 4,
             ((4, heads * QB, GW), F32), turned, turned, ((8, model), F32), ((QB, model), F32), ((model, QB), BF16),
             ((model, 2 * (4 * half + QB)), BF16)],
            16, {4: (length, False)}, {8: (length, True)}, {20: 8}, cuts={n: cut for n in range(3, 7)},
            bare=(6, 7, 8), dealt=dealt,
        ),
        c_x, mem_other,
    ))
    *d_self, s_keep, s_send, output = back
    s_other = core_swap(s_send)
    if dealt:
        across = [(i * 2 + j, (i ^ 2) * 2 + 1 - j) for i in range(n_dp) for j in range(2)]
        s_near = [part_total(n, s_keep, s_other) for n in range(1, 4)]
        f_last = total(*f_z).astype(BF16)
        c_part = part_total(0, c_keep, c_other, c_x)
        d_self[0] = after(d_self[0], *s_near, f_last, c_part)
        s_near = [
            lax.ppermute(s_near[0], "tensor", swap_y), lax.ppermute(s_near[1], "dp", swap(2)),
            lax.ppermute(s_near[2], ("dp", "tensor"), across),
        ]
    input_grad, in_send, memory_grad = call(
        input_backward, sc,
        [mine_s, sib_s, *own_s[:3], residual_scale, d_pre1, *d_self, mem_other, memory_grad],
        [*halves, (memory_grad.shape, F32)], square_weights, 5, None, {0: (length, False), 2: (length, True)},
        {14: 2}, cuts={n: cut for n in range(6, 13)}, out_cuts={0: cut, 1: cut},
    )
    thin, broad = ((chunk, half), F32), ((chunk, hidden), F32)
    three = ((3, chunk), F32)
    if dealt:
        in_send, c_part = lax.optimization_barrier((in_send, c_part))
        in_other = lax.ppermute(in_send, "tensor", swap_y)
        c_z = z_send(c_part)
        in_other, c_z = lax.optimization_barrier((in_other, c_z))
        s_far = z_send(part_total(0, s_keep, s_other, *s_near))
        c_last = total(*c_z).astype(BF16)
        late = lax.ppermute(
            jnp.concatenate([f_last[:, 2 * hidden :], c_last[:, 4 * half :]], axis=1), "tensor", swap_y
        )
        while len(s_far) < 4:
            s_far.append(jnp.zeros_like(s_far[0]))
        s_far = [*s_far[:3], s_far[3] if len(s_far) == 4 else total(*s_far[3:]).astype(BF16)]
        input_grad = fill(input_grad, in_other)
        sq, sk, sv, so, cq, ck, cv, co, ffn_in_grad, ffn_out_grad, gain_grad, shift_grad, scale_grad = call(
            finish, sc, [f_last, c_last, late, *s_far], [*[thin] * 8, broad, broad, three, three, three], [], 0.01
        )
    else:
        input_grad = fill(input_grad, lax.ppermute(in_send, "tensor", swap_y))
        f1_sum, f2_sum = reduce_any(f1_keep, f1_send), reduce_any(f2_keep, f2_send)
        c_sum, s_sum = reduce_any(c_keep, c_send), reduce_any(s_keep, s_send)
        ffn_in_grad, ffn_out_grad = f2_sum, f1_sum
        cq, ck, cv, co = [c_sum[:, n * half : (n + 1) * half] for n in range(4)]
        sq, sk, sv, so = [s_sum[:, n * half : (n + 1) * half] for n in range(4)]
        gain_grad, shift_grad, scale_grad = [s_sum[:, 4 * half + 3 * n : 4 * half + 3 * n + 3].T for n in range(3)]
    return (
        output, input_grad, memory_grad, sq, sk, sv, so.T, cq, ck, cv, co.T, ffn_in_grad, ffn_out_grad.T,
        gain_grad, shift_grad, scale_grad,
    )


def solution(mesh):
    rows, cols = P("dp", None), P(None, "tensor")
    both, turned = P("dp", "tensor"), P("tensor", "dp")
    return jax.shard_map(
        functools.partial(local, n_dp=mesh.shape["dp"], n_tensor=mesh.shape["tensor"]),
        mesh=mesh,
        in_specs=(
            rows, rows, rows, rows, cols, cols, cols, turned_rows(), cols, cols, cols, turned_rows(), cols,
            turned_rows(), P(), P(), P(), rows,
        ),
        out_specs=(
            rows, both, both, both, both, both, turned, both, both, both, turned, both, turned,
            P(None, "dp"), P(None, "dp"), P(None, "dp"),
        ),
        check_vma=False,
    )


def turned_rows():
    return P("tensor", None)
```
